32 devices in a mesh: tok: 4 (over z), row: 2 (over x), col: 4 (over y, core).
Axes of the slice: x: 2, y: 2, z: 4, core: 2. Of those that a mesh axis runs over, the one named last changes fastest.
Arguments:
- tokens: bfloat16 [512, 8192], P('tok', 'row'), may hold values from -6 to 6
- w1_blocks: bfloat16 [2, 4, 8, 128, 128], P('row', 'col'), may hold values from -0.5 to 0.5
- w1_rows: int32 [2, 4, 8], P('row', 'col'), may hold values from 0 to 31
- w1_cols: int32 [2, 4, 8], P('row', 'col'), may hold values from 0 to 63
- w2_blocks: bfloat16 [2, 4, 8, 128, 128], P('row', 'col'), may hold values from -0.5 to 0.5
- w2_hidden: int32 [2, 4, 8], P('row', 'col'), may hold values from 0 to 63
- w2_outs: int32 [2, 4, 8], P('row', 'col'), may hold values from 0 to 31
- grad_out: bfloat16 [512, 8192], P('tok', 'row'), may hold values from -6 to 6
Outputs:
- output: bfloat16 [512, 8192], P(('tok', 'col'), 'row')
- grad_in: bfloat16 [512, 8192], P(('tok', 'col'), 'row')
- grad_w1: float32 [2, 4, 8, 128, 128], P('row', 'col', None, 'tok')
- grad_w2: float32 [2, 4, 8, 128, 128], P('row', 'col', None, 'tok')
The draws below stay inside these ranges and needn't reach their ends.
All inputs are finite; a program needn't handle non-finite values.
Results may differ from the reference program's by a relative error of at most 0.0049.
Values may be sent and summed in bfloat16 or wider, within the bound.
No kernel may reach another device: no remote copies, remote signals or barrier semaphores. Data moves between devices by JAX's collectives and lax.ppermute only.
A program may use at most 64 MiB of HBM per device.

```python
import math
import jax
import jax.numpy as jnp
import numpy as np
from jax import lax

D = 8192
FF = 32768
BLK = 128
NB = 8
TOKENS = 512
RB = 32
CB = 64
FAN1 = 128
FAN2 = 128
N_ROW = 2
N_COL = 4


def touch_ends(result, own_key, smallest, high):
    dims = result.shape
    index_at = [jax.random.randint(jax.random.fold_in(own_key, axis), (), 0, dims[axis]) for axis in range(len(dims))]
    result = result.at[tuple(index_at)].set(smallest)
    longest = dims.index(max(dims))
    index_at[longest] = (index_at[longest] + 1) % dims[longest]
    return result.at[tuple(index_at)].set(high)


def block_scale(stream_key, extent, split, least, high):
    loudness, own = 1.0, jax.random.fold_in(stream_key, 6)
    for axis_at, parts in split:
        heights = jnp.exp(jax.random.uniform(jax.random.fold_in(own, axis_at), (parts,), jnp.float32, least / len(split), high / len(split)))
        loudness = loudness * jnp.repeat(heights, extent[axis_at] // parts).reshape([-1 if axis == axis_at else 1 for axis in range(len(extent))])
    return loudness


def cumulative_ranks(number_of, skew):
    loads = [(1 << 20) // math.isqrt(grade ** skew) + 1 for grade in range(1, number_of + 1)]
    deviation = 1 + sum(loads) // (1 << 30)
    return np.cumsum(np.array([max(1, weight // deviation) for weight in loads]))


def ranked(rng, shape, number_of, slope):
    grid = cumulative_ranks(number_of, slope)
    pick = jax.random.randint(jax.random.fold_in(rng, 1), shape, 0, int(grid[number_of - 1]))
    rank = jnp.searchsorted(jnp.asarray(grid, jnp.int32), pick, side="right")
    return jax.random.permutation(jax.random.fold_in(rng, 2), number_of)[rank].astype(jnp.int32)


def centred(own_key, extent, deviation, limit, split=(), kind=jnp.bfloat16):
    factor_of = block_scale(own_key, extent, split, -0.22, 0.18) if split else 1.0
    entries = jax.random.normal(own_key, extent, jnp.float32) * deviation * factor_of
    return jnp.minimum(jnp.maximum(entries, -limit), limit).astype(kind)


def setup_inputs(seed: int = 0) -> dict:
    key_list = jax.random.split(jax.random.key(seed), 9)
    tokens = centred(key_list[0], (TOKENS, D), 1.0, 6.0, ((0, 4), (1, 2)))
    w1_blocks = centred(key_list[1], (N_ROW, N_COL, NB, BLK, BLK), FAN1 ** -0.5, 0.5, ((0, 2), (1, 4)))
    w1_rows = touch_ends(jax.random.randint(key_list[2], (N_ROW, N_COL, NB), 0, RB), jax.random.fold_in(key_list[2], 1), 0, RB - 1).astype(jnp.int32)
    w1_cols = touch_ends(ranked(key_list[3], (N_ROW, N_COL, NB), CB, 1), jax.random.fold_in(key_list[3], 3), 0, CB - 1).astype(jnp.int32)
    w2_blocks = centred(key_list[4], (N_ROW, N_COL, NB, BLK, BLK), FAN2 ** -0.5, 0.5, ((0, 2), (1, 4)))
    w2_hidden = touch_ends(jax.random.randint(key_list[5], (N_ROW, N_COL, NB), 0, CB), jax.random.fold_in(key_list[5], 1), 0, CB - 1).astype(jnp.int32)
    w2_outs = touch_ends(ranked(key_list[6], (N_ROW, N_COL, NB), RB, 1), jax.random.fold_in(key_list[6], 3), 0, RB - 1).astype(jnp.int32)
    grad_out = centred(key_list[7], (TOKENS, D), 1.0, 6.0, ((0, 4), (1, 2)))
    return {"tokens": tokens, "w1_blocks": w1_blocks, "w1_rows": w1_rows, "w1_cols": w1_cols, "w2_blocks": w2_blocks, "w2_hidden": w2_hidden, "w2_outs": w2_outs, "grad_out": grad_out}


highest = lax.Precision.HIGHEST

def gelu_value(value):
    return value * (0.5 * (1.0 + jax.scipy.special.erf(value / jnp.sqrt(2.0))))

def gelu_slope(value):
    cdf_part = 0.5 * (1.0 + jax.scipy.special.erf(value / jnp.sqrt(2.0)))
    return cdf_part + value * jnp.exp(-0.5 * value * value) / jnp.sqrt(2.0 * jnp.pi)

def select_blocks(source, indices, count):
    onehot = (indices[:, None] == jnp.arange(count, dtype=jnp.int32)[None, :]).astype(jnp.float32)
    shaped = source.astype(jnp.float32).reshape(source.shape[0], count, BLK)
    return jnp.einsum('kr,trb->ktb', onehot, shaped, precision=highest)

def place_blocks(product, indices, count):
    onehot = (indices[:, None] == jnp.arange(count, dtype=jnp.int32)[None, :]).astype(jnp.float32)
    placed = jnp.einsum('kc,ktj->tcj', onehot, product, precision=highest)
    return placed.reshape(product.shape[1], count * BLK)

def sweep(source, weights, index_in, index_out, in_row, count_in, count_out, total_width, flip):
    rows = source.shape[0]
    form = 'ktb,kjb->ktj' if flip else 'ktb,kbj->ktj'

    def step(total, owner):
        row_id = owner // N_COL
        col_id = owner % N_COL
        in_start = (row_id if in_row else col_id) * (count_in * BLK)
        out_start = (col_id if in_row else row_id) * (count_out * BLK)
        piece = lax.dynamic_slice_in_dim(source, in_start, count_in * BLK, 1)
        taken = select_blocks(piece, index_in[owner], count_in)
        product = jnp.einsum(form, taken, weights[owner].astype(jnp.float32), precision=highest)
        placed = place_blocks(product, index_out[owner], count_out)
        current = lax.dynamic_slice_in_dim(total, out_start, count_out * BLK, 1)
        total = lax.dynamic_update_slice_in_dim(total, current + placed, out_start, 1)
        return (total, None)
    owners = jnp.arange(N_ROW * N_COL, dtype=jnp.int32)
    total, _ = lax.scan(step, jnp.zeros((rows, total_width), jnp.float32), owners)
    return total

def block_grads(left, right, weights_shape, index_left, index_right, left_row, count_left, count_right):

    def step(carry, owner):
        row_id = owner // N_COL
        col_id = owner % N_COL
        left_start = (row_id if left_row else col_id) * (count_left * BLK)
        right_start = (col_id if left_row else row_id) * (count_right * BLK)
        left_piece = lax.dynamic_slice_in_dim(left, left_start, count_left * BLK, 1)
        right_piece = lax.dynamic_slice_in_dim(right, right_start, count_right * BLK, 1)
        left_taken = select_blocks(left_piece, index_left[owner], count_left)
        right_taken = select_blocks(right_piece, index_right[owner], count_right)
        return (carry, jnp.einsum('ktb,ktj->kbj', left_taken, right_taken, precision=highest))
    owners = jnp.arange(N_ROW * N_COL, dtype=jnp.int32)
    _, stacked = lax.scan(step, jnp.zeros((), jnp.float32), owners)
    return stacked.reshape(weights_shape)

def reference(tokens, w1_blocks, w1_rows, w1_cols, w2_blocks, w2_hidden, w2_outs, grad_out):
    owners = N_ROW * N_COL
    first = w1_blocks.reshape(owners, NB, BLK, BLK)
    second = w2_blocks.reshape(owners, NB, BLK, BLK)
    first_rows = w1_rows.reshape(owners, NB)
    first_cols = w1_cols.reshape(owners, NB)
    second_hidden = w2_hidden.reshape(owners, NB)
    second_outs = w2_outs.reshape(owners, NB)
    hidden = sweep(tokens, first, first_rows, first_cols, True, RB, CB, FF, False)
    active = gelu_value(hidden).astype(jnp.bfloat16)
    output = sweep(active, second, second_hidden, second_outs, False, CB, RB, D, False).astype(jnp.bfloat16)
    back = sweep(grad_out, second, second_outs, second_hidden, True, RB, CB, FF, True)
    grad_hidden = (back * gelu_slope(hidden)).astype(jnp.bfloat16)
    grad_in = sweep(grad_hidden, first, first_cols, first_rows, False, CB, RB, D, True).astype(jnp.bfloat16)
    grad_w1 = block_grads(tokens, grad_hidden, w1_blocks.shape, first_rows, first_cols, True, RB, CB)
    grad_w2 = block_grads(active, grad_out, w2_blocks.shape, second_hidden, second_outs, False, CB, RB)
    return (output, grad_in, grad_w1, grad_w2)
```

```python
import functools
import math

import jax
import jax.numpy as jnp
from jax import lax
from jax.experimental import pallas as pl
from jax.experimental.pallas import tpu as pltpu
from jax.sharding import PartitionSpec as P

FF = 32768
f32 = jnp.float32
bf16 = jnp.bfloat16
VMEM = pl.BlockSpec(memory_space=pltpu.VMEM)
SMEM = pl.BlockSpec(memory_space=pltpu.SMEM)
ANY = pl.BlockSpec(memory_space=pl.ANY)
PARAMS = pltpu.CompilerParams(vmem_limit_bytes=32 * 1024 * 1024)

W1_ROW, W1_COL, W2_HID, W2_OUT = range(4)


def dot(a, b, contract):
    return lax.dot_general(a, b, ((contract[:1], contract[1:]), ((), ())), preferred_element_type=f32)


def shift(x, axis, by):
    n = lax.axis_size(axis)
    if by % n == 0:
        return x
    return lax.ppermute(x, axis, [(i, (i + by) % n) for i in range(n)])


def cdf(v):
    return 0.5 * (1.0 + lax.erf(v * math.sqrt(0.5)))


def first_kernel(slots, blk, tab, tokens, grad_out, w1, w2, p_own, p_send, b_own, b_send, taken, cot, w1_v, w2_v, sems):
    def block_of(source, index, target, sem):
        start = pl.multiple_of(index * blk, blk)
        return pltpu.make_async_copy(source.at[:, pl.ds(start, blk)], target, sem)

    w1_copy = pltpu.make_async_copy(w1, w1_v, sems.at[2 * slots])
    w2_copy = pltpu.make_async_copy(w2, w2_v, sems.at[2 * slots + 1])
    w1_copy.start()
    t_copies = [block_of(tokens, tab[W1_ROW, k], taken.at[k], sems.at[k]) for k in range(slots)]
    g_copies = [block_of(grad_out, tab[W2_OUT, k], cot.at[k], sems.at[slots + k]) for k in range(slots)]
    for c in t_copies:
        c.start()
    w2_copy.start()
    for c in g_copies:
        c.start()
    w1_copy.wait()
    for k in range(slots):
        t_copies[k].wait()
        value = dot(taken[k], w1_v[k], (1, 0))
        p_own[k] = value
        p_send[k] = value.astype(bf16)
    w2_copy.wait()
    for k in range(slots):
        g_copies[k].wait()
        value = dot(cot[k], w2_v[k], (1, 1))
        b_own[k] = value
        b_send[k] = value.astype(bf16)


def peer_tables(tabs, n_row, n_col):
    me_r, me_c = lax.axis_index("row"), lax.axis_index("col")

    def entry(d, which, k):
        r = lax.rem(me_r + (n_row - d), n_row)
        return tabs[r * n_col + me_c, which, k]

    return entry


def sum_at(acc, entry, targets, sources, own, peers, slots):
    for which in targets:
        for k in range(slots):
            acc[entry(0, which, k)] = jnp.zeros(acc.shape[1:], f32)
    for d, ref in enumerate([own] + list(peers)):
        for k in range(slots):
            at = entry(d, sources, k)
            acc[at] = acc[at] + ref[k].astype(f32)


def send_shares(value, refs, k, me, n):
    share = value.shape[0] // n
    for d in range(n):
        start = pl.multiple_of(lax.rem(me + d, n) * share, share)
        refs[d][k] = value[pl.ds(start, share), :].astype(refs[d].dtype)


def hidden_kernel(dims, tabs, p_own, *refs):
    slots, n_row, n_col, n_tok = dims
    p_peers, refs = refs[: n_row - 1], refs[n_row - 1 :]
    cot, w2, slope = refs[:3]
    outs, grads = refs[3 : 3 + n_col], refs[3 + n_col : 3 + n_col + n_tok]
    acc, value, grad = refs[3 + n_col + n_tok :]
    entry = peer_tables(tabs, n_row, n_col)
    me_c, me_t = lax.axis_index("col"), lax.axis_index("tok")
    sum_at(acc, entry, (W1_COL, W2_HID), W1_COL, p_own, p_peers, slots)
    for k in range(slots):
        h = acc[entry(0, W2_HID, k)]
        active = (h * cdf(h)).astype(bf16)
        value[...] = dot(active, w2[k], (1, 0))
        send_shares(value, outs, k, me_c, n_col)
        grad[...] = dot(active, cot[k], (0, 0))
        send_shares(grad, grads, k, me_t, n_tok)
    for k in range(slots):
        h = acc[entry(0, W1_COL, k)]
        slope[k] = cdf(h) + h * jnp.exp(-0.5 * h * h) * (1.0 / math.sqrt(2.0 * math.pi))


def back_kernel(dims, tabs, b_own, *refs):
    slots, n_row, n_col, n_tok = dims
    b_peers, refs = refs[: n_row - 1], refs[n_row - 1 :]
    slope, taken, w1 = refs[:3]
    outs, grads = refs[3 : 3 + n_col], refs[3 + n_col : 3 + n_col + n_tok]
    acc, value, grad = refs[3 + n_col + n_tok :]
    entry = peer_tables(tabs, n_row, n_col)
    me_c, me_t = lax.axis_index("col"), lax.axis_index("tok")
    sum_at(acc, entry, (W1_COL,), W2_HID, b_own, b_peers, slots)
    for k in range(slots):
        g = (acc[entry(0, W1_COL, k)] * slope[k]).astype(bf16)
        value[...] = dot(g, w1[k], (1, 1))
        send_shares(value, outs, k, me_c, n_col)
        grad[...] = dot(taken[k], g, (0, 0))
        send_shares(grad, grads, k, me_t, n_tok)


def last_kernel(dims, tabs, *refs):
    slots, n_row, n_col, n_tok = dims
    o_parts, refs = refs[:n_col], refs[n_col:]
    i_parts, refs = refs[:n_col], refs[n_col:]
    g2_parts, refs = refs[:n_tok], refs[n_tok:]
    g1_parts, refs = refs[:n_tok], refs[n_tok:]
    output, grad_in, gw1, gw2, acc = refs
    me_r, me_c = lax.axis_index("row"), lax.axis_index("col")
    blk = acc.shape[-1]
    for parts, which, result in ((o_parts, W2_OUT, output), (i_parts, W1_ROW, grad_in)):
        acc[...] = jnp.zeros(acc.shape, f32)
        for d, ref in enumerate(parts):
            src = me_r * n_col + lax.rem(me_c + (n_col - d), n_col)
            for k in range(slots):
                at = tabs[src, which, k]
                acc[at] = acc[at] + ref[k].astype(f32)
        for b in range(acc.shape[0]):
            result[:, b * blk : (b + 1) * blk] = acc[b].astype(bf16)
    for parts, result in ((g2_parts, gw2), (g1_parts, gw1)):
        for k in range(slots):
            total = parts[0][k].astype(f32)
            for ref in parts[1:]:
                total = total + ref[k].astype(f32)
            result[k] = total


def shards(tokens, w1_blocks, w1_rows, w1_cols, w2_blocks, w2_hidden, w2_outs, grad_out):
    slots, blk = w1_blocks.shape[2], w1_blocks.shape[-1]
    rows = tokens.shape[0]
    n_row, n_col, n_tok = (lax.axis_size(a) for a in ("row", "col", "tok"))
    dims = (slots, n_row, n_col, n_tok)
    row_blocks = tokens.shape[1] // blk
    col_blocks = FF // n_col // blk
    share, part = rows // n_col, blk // n_tok
    w1 = w1_blocks.reshape(slots, blk, blk)
    w2 = w2_blocks.reshape(slots, blk, blk)
    tab = jnp.concatenate([t.reshape(1, slots) for t in (w1_rows, w1_cols, w2_hidden, w2_outs)])
    tabs = lax.all_gather(tab, ("row", "col"))

    S = jax.ShapeDtypeStruct
    wide, narrow = S((slots, rows, blk), f32), S((slots, rows, blk), bf16)
    p_own, p_send, b_own, b_send, taken, cot = pl.pallas_call(
        functools.partial(first_kernel, slots, blk),
        out_shape=(wide, narrow, wide, narrow, narrow, narrow),
        in_specs=[SMEM, ANY, ANY, ANY, ANY],
        out_specs=(VMEM,) * 6,
        scratch_shapes=[
            pltpu.VMEM((slots, blk, blk), bf16),
            pltpu.VMEM((slots, blk, blk), bf16),
            pltpu.SemaphoreType.DMA((2 * slots + 2,)),
        ],
        compiler_params=PARAMS,
        name="take_and_multiply",
    )(tab, tokens, grad_out, w1, w2)

    p_peers = [shift(p_send, "row", d) for d in range(1, n_row)]
    b_peers = [shift(b_send, "row", d) for d in range(1, n_row)]

    shares = (S((slots, share, blk), bf16),) * n_col
    parts = (S((slots, part, blk), bf16),) * n_tok
    scratch = [
        pltpu.VMEM((col_blocks, rows, blk), f32),
        pltpu.VMEM((rows, blk), f32),
        pltpu.VMEM((blk, blk), f32),
    ]
    slope, *sent = pl.pallas_call(
        functools.partial(hidden_kernel, dims),
        out_shape=(wide,) + shares + parts,
        in_specs=[SMEM] + [VMEM] * (n_row + 2),
        out_specs=(VMEM,) * (1 + n_col + n_tok),
        scratch_shapes=scratch,
        compiler_params=PARAMS,
        name="hidden",
    )(tabs, p_own, *p_peers, cot, w2)
    o_parts = [shift(x, "col", d) for d, x in enumerate(sent[:n_col])]
    g2_parts = [shift(x, "tok", d) for d, x in enumerate(sent[n_col:])]

    sent = pl.pallas_call(
        functools.partial(back_kernel, dims),
        out_shape=shares + parts,
        in_specs=[SMEM] + [VMEM] * (n_row + 3),
        out_specs=(VMEM,) * (n_col + n_tok),
        scratch_shapes=scratch,
        compiler_params=PARAMS,
        name="back",
    )(tabs, b_own, *b_peers, slope, taken, w1)
    i_parts = [shift(x, "col", d) for d, x in enumerate(sent[:n_col])]
    g1_parts = [shift(x, "tok", d) for d, x in enumerate(sent[n_col:])]

    summed = S((slots, part, blk), f32)
    output, grad_in, gw1, gw2 = pl.pallas_call(
        functools.partial(last_kernel, dims),
        out_shape=(
            S((share, row_blocks * blk), bf16),
            S((share, row_blocks * blk), bf16),
            summed,
            summed,
        ),
        in_specs=[SMEM] + [VMEM] * (2 * n_col + 2 * n_tok),
        out_specs=(VMEM,) * 4,
        scratch_shapes=[pltpu.VMEM((row_blocks, share, blk), f32)],
        compiler_params=PARAMS,
        name="add_up",
    )(tabs, *o_parts, *i_parts, *g2_parts, *g1_parts)
    return (output, grad_in, gw1.reshape(1, 1, slots, part, blk), gw2.reshape(1, 1, slots, part, blk))


def solution(mesh):
    placed = (
        P("tok", "row"),
        P("row", "col", None, None, None),
        P("row", "col", None),
        P("row", "col", None),
        P("row", "col", None, None, None),
        P("row", "col", None),
        P("row", "col", None),
        P("tok", "row"),
    )
    return jax.shard_map(
        shards,
        mesh=mesh,
        in_specs=placed,
        out_specs=(
            P(("tok", "col"), "row"),
            P(("tok", "col"), "row"),
            P("row", "col", None, "tok", None),
            P("row", "col", None, "tok", None),
        ),
        check_vma=False,
    )
```

```python
import functools
import math

import jax
import jax.numpy as jnp
from jax import lax
from jax.experimental import pallas as pl
from jax.experimental.pallas import tpu as pltpu
from jax.sharding import PartitionSpec as P

FF = 32768
f32 = jnp.float32
bf16 = jnp.bfloat16
VMEM = pl.BlockSpec(memory_space=pltpu.VMEM)
SMEM = pl.BlockSpec(memory_space=pltpu.SMEM)
HBM = pl.BlockSpec(memory_space=pltpu.HBM)
LANES = 128
PARAMS = pltpu.CompilerParams(vmem_limit_bytes=32 * 1024 * 1024)

W1_ROW, W1_COL, W2_HID, W2_OUT = range(4)


def dot(a, b, contract):
    return lax.dot_general(a, b, ((contract[:1], contract[1:]), ((), ())), preferred_element_type=f32)


def shift(x, axis, by):
    n = lax.axis_size(axis)
    if by % n == 0:
        return x
    return lax.ppermute(x, axis, [(i, (i + by) % n) for i in range(n)])


def cdf(v):
    return 0.5 * (1.0 + lax.erf(v * math.sqrt(0.5)))


def table_row(tables, slots):
    lane = lax.broadcasted_iota(jnp.int32, (16, LANES), 1)
    row = jnp.zeros((16, LANES), f32)
    for which, table in enumerate(tables):
        for k in range(slots):
            row = jnp.where(lane == which * slots + k, table[k].astype(f32), row)
    return row.astype(bf16)


def decode_tables(refs, rows, ints, scalars, sem):
    for i, ref in enumerate(refs):
        ints[i * 8 : i * 8 + 8] = ref[rows : rows + 16, :].astype(f32)[:8].astype(jnp.int32)
    copy = pltpu.make_async_copy(ints, scalars, sem)
    copy.start()
    return copy


def take_kernel(slots, blk, flip, at, c0, c1, c2, c3, source, weights, own, send, taken, w_v, sems):
    tables = (c0, c1, c2, c3)
    w_copy = pltpu.make_async_copy(weights, w_v, sems.at[slots])
    copies = []
    for k in range(slots):
        begin = pl.multiple_of(tables[at][k] * blk, blk)
        copies.append(pltpu.make_async_copy(source.at[:, pl.ds(begin, blk)], taken.at[k], sems.at[k]))
    for c in copies[:1] + [w_copy] + copies[1:]:
        c.start()
    rows = taken.shape[1]
    send[slots * rows :, :] = table_row(tables, slots)
    w_copy.wait()
    for k in range(slots):
        copies[k].wait()
        value = dot(taken[k], w_v[k], (1, 1) if flip else (1, 0))
        own[k] = value
        send[k * rows : (k + 1) * rows, :] = value.astype(bf16)


def sum_at(acc, targets, tables, own_at, own, peers, peer_at, slots, scratch):
    ints, scalars, sem = scratch
    rows = acc.shape[1]
    copy = decode_tables(peers, slots * rows, ints, scalars, sem) if peers else None
    for which in targets:
        for k in range(slots):
            acc[tables[which][k]] = jnp.zeros(acc.shape[1:], f32)
    for k in range(slots):
        at = tables[own_at][k]
        acc[at] = acc[at] + own[k]
    if peers:
        copy.wait()
    for i, ref in enumerate(peers):
        for k in range(slots):
            at = scalars[i * 8, peer_at * slots + k]
            acc[at] = acc[at] + ref[k * rows : (k + 1) * rows, :].astype(f32)


def send_shares(value, ref, k):
    n = ref.shape[0]
    share = value.shape[0] // n
    for d in range(n):
        ref[d, k * share : (k + 1) * share, :] = value[d * share : (d + 1) * share].astype(ref.dtype)


def hidden_kernel(dims, c0, c1, c2, c3, p_own, *refs):
    slots, n_row, n_col, n_tok = dims
    p_peers, refs = refs[: n_row - 1], refs[n_row - 1 :]
    cot, w2, slope, outs, grads, acc, *scratch = refs
    tables = (c0, c1, c2, c3)
    row = table_row(tables, slots)
    for d in range(n_col):
        outs[d, outs.shape[1] - 16 :, :] = row
    sum_at(acc, (W1_COL, W2_HID), tables, W1_COL, p_own, p_peers, W1_COL, slots, scratch)
    for k in range(slots):
        h = acc[tables[W2_HID][k]]
        active = (h * cdf(h)).astype(bf16)
        send_shares(dot(active, w2[k], (1, 0)), outs, k)
        send_shares(dot(active, cot[k], (0, 0)), grads, k)
    for k in range(slots):
        h = acc[tables[W1_COL][k]]
        slope[k] = cdf(h) + h * jnp.exp(-0.5 * h * h) * (1.0 / math.sqrt(2.0 * math.pi))


def back_kernel(dims, c0, c1, c2, c3, b_own, *refs):
    slots, n_row, n_col, n_tok = dims
    b_peers, refs = refs[: n_row - 1], refs[n_row - 1 :]
    slope, taken, w1, outs, grads, acc, *scratch = refs
    tables = (c0, c1, c2, c3)
    sum_at(acc, (W1_COL,), tables, W2_HID, b_own, b_peers, W2_HID, slots, scratch)
    for k in range(slots):
        g = (acc[tables[W1_COL][k]] * slope[k]).astype(bf16)
        send_shares(dot(g, w1[k], (1, 1)), outs, k)
        send_shares(dot(taken[k], g, (0, 0)), grads, k)


def last_kernel(dims, o_parts, i_parts, g2_parts, g1_parts, output, grad_in, gw1, gw2, acc, ints, scalars, sem):
    slots, n_row, n_col, n_tok = dims
    blk, share = acc.shape[-1], acc.shape[1]
    copy = decode_tables([o_parts.at[c] for c in range(n_col)], slots * share, ints, scalars, sem)
    for parts, result in ((g2_parts, gw2), (g1_parts, gw1)):
        for k in range(slots):
            here = slice(k * result.shape[1], (k + 1) * result.shape[1])
            total = parts[0, here, :].astype(f32)
            for d in range(1, n_tok):
                total = total + parts[d, here, :].astype(f32)
            result[k] = total
    copy.wait()
    for parts, which, result in ((o_parts, W2_OUT, output), (i_parts, W1_ROW, grad_in)):
        acc[...] = jnp.zeros(acc.shape, f32)
        for c in range(n_col):
            for k in range(slots):
                at = scalars[c * 8, which * slots + k]
                acc[at] = acc[at] + parts[c, k * share : (k + 1) * share, :].astype(f32)
        for b in range(acc.shape[0]):
            result[:, b * blk : (b + 1) * blk] = acc[b].astype(bf16)


def shards(tokens, w1_blocks, w1_rows, w1_cols, w2_blocks, w2_hidden, w2_outs, grad_out):
    slots, blk = w1_blocks.shape[2], w1_blocks.shape[-1]
    rows = tokens.shape[0]
    n_row, n_col, n_tok = (lax.axis_size(a) for a in ("row", "col", "tok"))
    dims = (slots, n_row, n_col, n_tok)
    row_blocks = tokens.shape[1] // blk
    col_blocks = FF // n_col // blk
    share, part = rows // n_col, blk // n_tok
    w1 = w1_blocks.reshape(slots, blk, blk)
    w2 = w2_blocks.reshape(slots, blk, blk)
    tables = [t.reshape(slots) for t in (w1_rows, w1_cols, w2_hidden, w2_outs)]

    S = jax.ShapeDtypeStruct
    wide, narrow = S((slots, rows, blk), f32), S((slots, rows, blk), bf16)
    message = S((slots * rows + 16, blk), bf16)

    def take(source, weights, flip, at, name):
        return pl.pallas_call(
            functools.partial(take_kernel, slots, blk, flip, at),
            out_shape=(wide, message, narrow),
            in_specs=[SMEM] * 4 + [HBM, HBM],
            out_specs=(VMEM,) * 3,
            scratch_shapes=[
                pltpu.VMEM((slots, blk, blk), bf16),
                pltpu.SemaphoreType.DMA((slots + 1,)),
            ],
            compiler_params=PARAMS,
            name=name,
        )(*tables, source, weights)

    p_own, p_send, taken = take(tokens, w1, False, W1_ROW, "take_tokens")
    p_peers = [shift(p_send, "row", d) for d in range(1, n_row)]
    b_own, b_send, cot = take(grad_out, w2, True, W2_OUT, "take_cotangent")
    b_peers = [shift(b_send, "row", d) for d in range(1, n_row)]

    parts = S((n_tok, slots * part, blk), bf16)
    scratch = [
        pltpu.VMEM((col_blocks, rows, blk), f32),
        pltpu.VMEM((8 * max(1, n_row - 1), LANES), jnp.int32),
        pltpu.SMEM((8 * max(1, n_row - 1), LANES), jnp.int32),
        pltpu.SemaphoreType.DMA,
    ]
    slope, o_sent, g2_sent = pl.pallas_call(
        functools.partial(hidden_kernel, dims),
        out_shape=(wide, S((n_col, slots * share + 16, blk), bf16), parts),
        in_specs=[SMEM] * 4 + [VMEM] * (n_row + 2),
        out_specs=(VMEM,) * 3,
        scratch_shapes=scratch,
        compiler_params=PARAMS,
        name="hidden",
    )(*tables, p_own, *p_peers, cot, w2)
    o_parts = lax.all_to_all(o_sent, "col", 0, 0, tiled=True)
    g2_parts = lax.all_to_all(g2_sent, "tok", 0, 0, tiled=True)

    i_sent, g1_sent = pl.pallas_call(
        functools.partial(back_kernel, dims),
        out_shape=(S((n_col, slots * share, blk), bf16), parts),
        in_specs=[SMEM] * 4 + [VMEM] * (n_row + 3),
        out_specs=(VMEM,) * 2,
        scratch_shapes=scratch,
        compiler_params=PARAMS,
        name="back",
    )(*tables, b_own, *b_peers, slope, taken, w1)
    i_parts = lax.all_to_all(i_sent, "col", 0, 0, tiled=True)
    g1_parts = lax.all_to_all(g1_sent, "tok", 0, 0, tiled=True)

    summed = S((slots, part, blk), f32)
    output, grad_in, gw1, gw2 = pl.pallas_call(
        functools.partial(last_kernel, dims),
        out_shape=(
            S((share, row_blocks * blk), bf16),
            S((share, row_blocks * blk), bf16),
            summed,
            summed,
        ),
        in_specs=[VMEM] * 4,
        out_specs=(VMEM,) * 4,
        scratch_shapes=[
            pltpu.VMEM((row_blocks, share, blk), f32),
            pltpu.VMEM((8 * n_col, LANES), jnp.int32),
            pltpu.SMEM((8 * n_col, LANES), jnp.int32),
            pltpu.SemaphoreType.DMA,
        ],
        compiler_params=PARAMS,
        name="add_up",
    )(o_parts, i_parts, g2_parts, g1_parts)
    return (output, grad_in, gw1.reshape(1, 1, slots, part, blk), gw2.reshape(1, 1, slots, part, blk))


def solution(mesh):
    placed = (
        P("tok", "row"),
        P("row", "col", None, None, None),
        P("row", "col", None),
        P("row", "col", None),
        P("row", "col", None, None, None),
        P("row", "col", None),
        P("row", "col", None),
        P("tok", "row"),
    )
    return jax.shard_map(
        shards,
        mesh=mesh,
        in_specs=placed,
        out_specs=(
            P(("tok", "col"), "row"),
            P(("tok", "col"), "row"),
            P("row", "col", None, "tok", None),
            P("row", "col", None, "tok", None),
        ),
        check_vma=False,
    )
```

```python
import functools
import math

import jax
import jax.numpy as jnp
from jax import lax
from jax.experimental import pallas as pl
from jax.experimental.pallas import tpu as pltpu
from jax.sharding import PartitionSpec as P

FF = 32768
f32 = jnp.float32
bf16 = jnp.bfloat16
VMEM = pl.BlockSpec(memory_space=pltpu.VMEM)
SMEM = pl.BlockSpec(memory_space=pltpu.SMEM)
HBM = pl.BlockSpec(memory_space=pltpu.HBM)
LANES = 128
PARAMS = pltpu.CompilerParams(vmem_limit_bytes=32 * 1024 * 1024)

TAKE_LIMIT = 62 * 1024 * 1024

W1_ROW, W1_COL, W2_HID, W2_OUT = range(4)


def dot(a, b, contract):
    return lax.dot_general(a, b, ((contract[:1], contract[1:]), ((), ())), preferred_element_type=f32)


def partner(i, d, n):
    return i ^ d if n & (n - 1) == 0 else (i + d) % n


def send(x, axis, d):
    n = lax.axis_size(axis)
    return lax.ppermute(x, axis, [(i, partner(i, d, n)) for i in range(n)]) if d else x


def target(axis, d):
    n = lax.axis_size(axis)
    me = lax.axis_index(axis)
    return jnp.bitwise_xor(me, d) if n & (n - 1) == 0 else lax.rem(me + d, n)


def cdf(v):
    return 0.5 * (1.0 + lax.erf(v * math.sqrt(0.5)))


def table_row(tables, slots):
    lane = lax.broadcasted_iota(jnp.int32, (16, LANES), 1)
    row = jnp.zeros((16, LANES), f32)
    for which, table in enumerate(tables):
        for k in range(slots):
            row = jnp.where(lane == which * slots + k, table[k].astype(f32), row)
    return row.astype(bf16)


def decode_tables(refs, rows, ints, scalars, sem):
    for i, ref in enumerate(refs):
        ints[i * 8 : i * 8 + 8] = ref[rows : rows + 16, :].astype(f32)[:8].astype(jnp.int32)
    copy = pltpu.make_async_copy(ints, scalars, sem)
    copy.start()
    return copy


def take_kernel(slots, blk, flip, at, c0, c1, c2, c3, source, weights, own, message, taken, w_v, sems):
    tables = (c0, c1, c2, c3)
    w_copy = pltpu.make_async_copy(weights, w_v, sems.at[slots])
    copies = []
    for k in range(slots):
        begin = pl.multiple_of(tables[at][k] * blk, blk)
        copies.append(pltpu.make_async_copy(source.at[:, pl.ds(begin, blk)], taken.at[k], sems.at[k]))
    for c in copies[:1] + [w_copy] + copies[1:]:
        c.start()
    rows = taken.shape[1]
    message[slots * rows :, :] = table_row(tables, slots)
    w_copy.wait()
    for k in range(slots):
        copies[k].wait()
        value = dot(taken[k], w_v[k], (1, 1) if flip else (1, 0))
        own[k] = value
        message[k * rows : (k + 1) * rows, :] = value.astype(bf16)


def sum_at(acc, targets, tables, own_at, own, peers, peer_at, slots, scratch):
    ints, scalars, sem = scratch
    rows = acc.shape[1]
    copy = decode_tables(peers, slots * rows, ints, scalars, sem) if peers else None
    for which in targets:
        for k in range(slots):
            acc[tables[which][k]] = jnp.zeros(acc.shape[1:], f32)
    for k in range(slots):
        at = tables[own_at][k]
        acc[at] = acc[at] + own[k]
    if peers:
        copy.wait()
    for i, ref in enumerate(peers):
        for k in range(slots):
            at = scalars[i * 8, peer_at * slots + k]
            acc[at] = acc[at] + ref[k * rows : (k + 1) * rows, :].astype(f32)


def cut(value, refs, k, axis):
    share = value.shape[0] // len(refs)
    for d, ref in enumerate(refs):
        begin = pl.multiple_of(target(axis, d) * share, share)
        ref[k * share : (k + 1) * share, :] = value[pl.ds(begin, share), :].astype(ref.dtype)


def hidden_kernel(dims, c0, c1, c2, c3, p_own, *refs):
    slots, n_row, n_col, n_tok = dims
    p_peers, refs = refs[: n_row - 1], refs[n_row - 1 :]
    cot, w2, slope, out = refs[:4]
    grads, refs = refs[4 : 4 + n_tok], refs[4 + n_tok :]
    acc, value, grad, *scratch = refs
    tables = (c0, c1, c2, c3)
    sum_at(acc, (W1_COL, W2_HID), tables, W1_COL, p_own, p_peers, W1_COL, slots, scratch)
    for k in range(slots):
        h = acc[tables[W2_HID][k]]
        active = (h * cdf(h)).astype(bf16)
        grad[k] = dot(active, cot[k], (0, 0))
        cut(grad.at[k], grads, k, "tok")
        out[k] = dot(active, w2[k], (1, 0)).astype(bf16)
    for k in range(slots):
        h = acc[tables[W1_COL][k]]
        slope[k] = cdf(h) + h * jnp.exp(-0.5 * h * h) * (1.0 / math.sqrt(2.0 * math.pi))


def back_kernel(dims, c0, c1, c2, c3, b_own, *refs):
    slots, n_row, n_col, n_tok = dims
    b_peers, refs = refs[: n_row - 1], refs[n_row - 1 :]
    slope, taken, w1, out = refs[:4]
    refs = refs[4:]
    outs, refs = refs[:n_col], refs[n_col:]
    grads, refs = refs[:n_tok], refs[n_tok:]
    acc, value, grad, *scratch = refs
    tables = (c0, c1, c2, c3)
    row = table_row(tables, slots)
    for ref in outs:
        ref[ref.shape[0] - 16 :, :] = row
    sum_at(acc, (W1_COL,), tables, W2_HID, b_own, b_peers, W2_HID, slots, scratch)
    for k in range(slots):
        g = (acc[tables[W1_COL][k]] * slope[k]).astype(bf16)
        grad[k] = dot(taken[k], g, (0, 0))
        cut(grad.at[k], grads, k, "tok")
        value[...] = dot(g, w1[k], (1, 1))
        cut(out.at[k], outs, k, "col")
        cut(value, outs, slots + k, "col")


def last_kernel(dims, *refs):
    slots, n_row, n_col, n_tok = dims
    o_parts, refs = refs[:n_col], refs[n_col:]
    g2_parts, refs = refs[:n_tok], refs[n_tok:]
    g1_parts, refs = refs[:n_tok], refs[n_tok:]
    output, grad_in, gw1, gw2, acc, ints, scalars, sem = refs
    blk, share = acc.shape[-1], acc.shape[1]
    copy = decode_tables(o_parts, 2 * slots * share, ints, scalars, sem)
    for parts, result in ((g2_parts, gw2), (g1_parts, gw1)):
        for k in range(slots):
            here = slice(k * result.shape[1], (k + 1) * result.shape[1])
            total = parts[0][here, :].astype(f32)
            for ref in parts[1:]:
                total = total + ref[here, :].astype(f32)
            result[k] = total
    copy.wait()
    for first, which, result in ((0, W2_OUT, output), (slots, W1_ROW, grad_in)):
        acc[...] = jnp.zeros(acc.shape, f32)
        for c, ref in enumerate(o_parts):
            for k in range(slots):
                at = scalars[c * 8, which * slots + k]
                here = slice((first + k) * share, (first + k + 1) * share)
                acc[at] = acc[at] + ref[here, :].astype(f32)
        for b in range(acc.shape[0]):
            result[:, b * blk : (b + 1) * blk] = acc[b].astype(bf16)


def shards(tokens, w1_blocks, w1_rows, w1_cols, w2_blocks, w2_hidden, w2_outs, grad_out):
    slots, blk = w1_blocks.shape[2], w1_blocks.shape[-1]
    rows = tokens.shape[0]
    n_row, n_col, n_tok = (lax.axis_size(a) for a in ("row", "col", "tok"))
    dims = (slots, n_row, n_col, n_tok)
    row_blocks = tokens.shape[1] // blk
    col_blocks = FF // n_col // blk
    share, part = rows // n_col, blk // n_tok
    w1 = w1_blocks.reshape(slots, blk, blk)
    w2 = w2_blocks.reshape(slots, blk, blk)
    tables = [t.reshape(slots) for t in (w1_rows, w1_cols, w2_hidden, w2_outs)]

    S = jax.ShapeDtypeStruct
    wide, narrow = S((slots, rows, blk), f32), S((slots, rows, blk), bf16)
    message = S((slots * rows + 16, blk), bf16)

    def take(source, weights, flip, at, name):
        return pl.pallas_call(
            functools.partial(take_kernel, slots, blk, flip, at),
            out_shape=(wide, message, narrow),
            in_specs=[SMEM] * 4 + [HBM, HBM],
            out_specs=(VMEM,) * 3,
            scratch_shapes=[
                pltpu.VMEM((slots, blk, blk), bf16),
                pltpu.SemaphoreType.DMA((slots + 1,)),
            ],
            compiler_params=pltpu.CompilerParams(vmem_limit_bytes=TAKE_LIMIT),
            name=name,
        )(*tables, source, weights)

    p_own, p_send, taken = take(tokens, w1, False, W1_ROW, "take_tokens")
    p_peers = [send(p_send, "row", d) for d in range(1, n_row)]
    b_own, b_send, cot = take(grad_out, w2, True, W2_OUT, "take_cotangent")
    b_peers = [send(b_send, "row", d) for d in range(1, n_row)]

    parts = (S((slots * part, blk), bf16),) * n_tok
    outs = (S((2 * slots * share + 16, blk), bf16),) * n_col
    scratch = [
        pltpu.VMEM((col_blocks, rows, blk), f32),
        pltpu.VMEM((rows, blk), f32),
        pltpu.VMEM((slots, blk, blk), f32),
        pltpu.VMEM((8 * max(1, n_row - 1), LANES), jnp.int32),
        pltpu.SMEM((8 * max(1, n_row - 1), LANES), jnp.int32),
        pltpu.SemaphoreType.DMA,
    ]
    slope, out, *g2_sent = pl.pallas_call(
        functools.partial(hidden_kernel, dims),
        out_shape=(wide, narrow) + parts,
        in_specs=[SMEM] * 4 + [VMEM] * (n_row + 2),
        out_specs=(VMEM,) * (2 + n_tok),
        scratch_shapes=scratch,
        compiler_params=PARAMS,
        name="hidden",
    )(*tables, p_own, *p_peers, cot, w2)
    g2_parts = [send(x, "tok", d) for d, x in enumerate(g2_sent)]

    sent = pl.pallas_call(
        functools.partial(back_kernel, dims),
        out_shape=outs + parts,
        in_specs=[SMEM] * 4 + [VMEM] * (n_row + 4),
        out_specs=(VMEM,) * (n_col + n_tok),
        scratch_shapes=scratch,
        compiler_params=PARAMS,
        name="back",
    )(*tables, b_own, *b_peers, slope, taken, w1, out)
    g1_parts = [send(x, "tok", d) for d, x in enumerate(sent[n_col:])]
    o_parts = [send(x, "col", d) for d, x in enumerate(sent[:n_col])]

    summed = S((slots, part, blk), f32)
    output, grad_in, gw1, gw2 = pl.pallas_call(
        functools.partial(last_kernel, dims),
        out_shape=(
            S((share, row_blocks * blk), bf16),
            S((share, row_blocks * blk), bf16),
            summed,
            summed,
        ),
        in_specs=[VMEM] * (n_col + 2 * n_tok),
        out_specs=(VMEM,) * 4,
        scratch_shapes=[
            pltpu.VMEM((row_blocks, share, blk), f32),
            pltpu.VMEM((8 * n_col, LANES), jnp.int32),
            pltpu.SMEM((8 * n_col, LANES), jnp.int32),
            pltpu.SemaphoreType.DMA,
        ],
        compiler_params=PARAMS,
        name="add_up",
    )(*o_parts, *g2_parts, *g1_parts)
    return (output, grad_in, gw1.reshape(1, 1, slots, part, blk), gw2.reshape(1, 1, slots, part, blk))


def solution(mesh):
    placed = (
        P("tok", "row"),
        P("row", "col", None, None, None),
        P("row", "col", None),
        P("row", "col", None),
        P("row", "col", None, None, None),
        P("row", "col", None),
        P("row", "col", None),
        P("tok", "row"),
    )
    return jax.shard_map(
        shards,
        mesh=mesh,
        in_specs=placed,
        out_specs=(
            P(("tok", "col"), "row"),
            P(("tok", "col"), "row"),
            P("row", "col", None, "tok", None),
            P("row", "col", None, "tok", None),
        ),
        check_vma=False,
    )
```

```python
import functools
import math

import jax
import jax.numpy as jnp
from jax import lax
from jax.experimental import pallas as pl
from jax.experimental.pallas import tpu as pltpu
from jax.sharding import PartitionSpec as P

FF = 32768
f32 = jnp.float32
bf16 = jnp.bfloat16
VMEM = pl.BlockSpec(memory_space=pltpu.VMEM)
SMEM = pl.BlockSpec(memory_space=pltpu.SMEM)
HBM = pl.BlockSpec(memory_space=pltpu.HBM)
LANES = 128
PARAMS = pltpu.CompilerParams(vmem_limit_bytes=32 * 1024 * 1024)

TAKE_LIMIT = 62 * 1024 * 1024

W1_ROW, W1_COL, W2_HID, W2_OUT = range(4)


def dot(a, b, contract):
    return lax.dot_general(a, b, ((contract[:1], contract[1:]), ((), ())), preferred_element_type=f32)


def partner(i, d, n):
    return i ^ d if n & (n - 1) == 0 else (i + d) % n


def send(x, axis, d):
    n = lax.axis_size(axis)
    return lax.ppermute(x, axis, [(i, partner(i, d, n)) for i in range(n)]) if d else x


def target(axis, d):
    n = lax.axis_size(axis)
    me = lax.axis_index(axis)
    return jnp.bitwise_xor(me, d) if n & (n - 1) == 0 else lax.rem(me + d, n)


def cdf(v):
    return 0.5 * (1.0 + lax.erf(v * math.sqrt(0.5)))


def table_row(tables, slots):
    lane = lax.broadcasted_iota(jnp.int32, (16, LANES), 1)
    row = jnp.zeros((16, LANES), f32)
    for which, table in enumerate(tables):
        for k in range(slots):
            row = jnp.where(lane == which * slots + k, table[k].astype(f32), row)
    return row.astype(bf16)


def decode_tables(refs, rows, ints, scalars, sem):
    for i, ref in enumerate(refs):
        ints[i * 8 : i * 8 + 8] = ref[rows : rows + 16, :].astype(f32)[:8].astype(jnp.int32)
    copy = pltpu.make_async_copy(ints, scalars, sem)
    copy.start()
    return copy


def start_taking(source, table, taken, sems):
    slots, _, blk = taken.shape
    copies = []
    for k in range(slots):
        begin = pl.multiple_of(table[k] * blk, blk)
        copies.append(pltpu.make_async_copy(source.at[:, pl.ds(begin, blk)], taken.at[k], sems.at[k]))
        copies[-1].start()
    return copies


def token_kernel(t0, t1, t2, t3, tokens, w1, message, taken, w_v, c0, c1, c2, c3, sems):
    slots, rows, blk = taken.shape
    tables = (c0, c1, c2, c3)
    loads = [pltpu.make_async_copy(t, c, sems.at[slots + 1 + i]) for i, (t, c) in enumerate(zip((t0, t1, t2, t3), tables))]
    w_copy = pltpu.make_async_copy(w1, w_v, sems.at[slots])
    for c in loads:
        c.start()
    w_copy.start()
    loads[W1_ROW].wait()
    copies = start_taking(tokens, c0, taken, sems)
    for c in loads[1:]:
        c.wait()
    message[slots * rows :, :] = table_row(tables, slots)
    w_copy.wait()
    for k in range(slots):
        copies[k].wait()
        message[k * rows : (k + 1) * rows, :] = dot(taken[k], w_v[k], (1, 0)).astype(bf16)


def cotangent_kernel(c0, c1, c2, c3, grad_out, w1, w2, taken, message, cot, p_own, b_own, tab, sems):
    slots, rows, blk = cot.shape
    copies = start_taking(grad_out, c3, cot, sems)
    for which, table in enumerate((c0, c1, c2, c3)):
        for k in range(slots):
            tab[which * slots + k] = table[k]
    for k in range(slots):
        copies[k].wait()
        value = dot(cot[k], w2[k], (1, 1))
        b_own[k] = value
        message[k * rows : (k + 1) * rows, :] = value.astype(bf16)
    message[slots * rows :, :] = jnp.zeros((16, blk), bf16)
    for k in range(slots):
        p_own[k] = dot(taken[k], w1[k], (1, 0))


def sum_at(acc, targets, tab, own_at, own, peers, peer_at, slots, scratch):
    ints, scalars, sem = scratch
    rows = acc.shape[1]
    copy = decode_tables(peers, slots * rows, ints, scalars, sem) if peers else None
    for which in targets:
        for k in range(slots):
            acc[tab[which * slots + k]] = jnp.zeros(acc.shape[1:], f32)
    for k in range(slots):
        at = tab[own_at * slots + k]
        acc[at] = acc[at] + own[k]
    if peers:
        copy.wait()
    for i, ref in enumerate(peers):
        for k in range(slots):
            at = scalars[i * 8, peer_at * slots + k]
            acc[at] = acc[at] + ref[k * rows : (k + 1) * rows, :].astype(f32)


def cut(value, refs, k, axis):
    share = value.shape[0] // len(refs)
    for d, ref in enumerate(refs):
        begin = pl.multiple_of(target(axis, d) * share, share)
        ref[k * share : (k + 1) * share, :] = value[pl.ds(begin, share), :].astype(ref.dtype)


def hidden_kernel(dims, tab, p_own, *refs):
    slots, n_row, n_col, n_tok = dims
    p_peers, refs = refs[: n_row - 1], refs[n_row - 1 :]
    cot, active, hidden, peer_tabs = refs[:4]
    grads, refs = refs[4 : 4 + n_tok], refs[4 + n_tok :]
    acc, grad, *scratch = refs
    sum_at(acc, (W1_COL, W2_HID), tab, W1_COL, p_own, p_peers, W1_COL, slots, scratch)
    for k in range(slots):
        h = acc[tab[W2_HID * slots + k]]
        active[k] = (h * cdf(h)).astype(bf16)
        grad[k] = dot(active[k], cot[k], (0, 0))
        cut(grad.at[k], grads, k, "tok")
    for k in range(slots):
        hidden[k] = acc[tab[W1_COL * slots + k]]
    peer_tabs[...] = scratch[0][...]


def slope_kernel(dims, active, hidden, w2, out, slope):
    slots = dims[0]
    for k in range(slots):
        out[k] = dot(active[k], w2[k], (1, 0)).astype(bf16)
    for k in range(slots):
        h = hidden[k]
        slope[k] = cdf(h) + h * jnp.exp(-0.5 * h * h) * (1.0 / math.sqrt(2.0 * math.pi))


def back_kernel(dims, tab, peer_tabs, b_own, *refs):
    slots, n_row, n_col, n_tok = dims
    b_peers, refs = refs[: n_row - 1], refs[n_row - 1 :]
    slope, taken, w1, out = refs[:4]
    refs = refs[4:]
    outs, refs = refs[:n_col], refs[n_col:]
    grads, refs = refs[:n_tok], refs[n_tok:]
    acc, value, grad = refs
    rows = acc.shape[1]
    for k in range(slots):
        acc[tab[W1_COL * slots + k]] = jnp.zeros(acc.shape[1:], f32)
    for k in range(slots):
        at = tab[W2_HID * slots + k]
        acc[at] = acc[at] + b_own[k]
    for i, ref in enumerate(b_peers):
        for k in range(slots):
            at = peer_tabs[i * 8, W2_HID * slots + k]
            acc[at] = acc[at] + ref[k * rows : (k + 1) * rows, :].astype(f32)
    for k in range(slots):
        g = (acc[tab[W1_COL * slots + k]] * slope[k]).astype(bf16)
        grad[k] = dot(taken[k], g, (0, 0))
        cut(grad.at[k], grads, k, "tok")
        value[k] = dot(g, w1[k], (1, 1))
        cut(value.at[k], outs, slots + k, "col")
    for k in range(slots):
        cut(out.at[k], outs, k, "col")
    row = table_row([[tab[which * slots + k] for k in range(slots)] for which in range(4)], slots)
    for ref in outs:
        ref[ref.shape[0] - 16 :, :] = row


def add_shares(parts, result):
    for k in range(result.shape[0]):
        here = slice(k * result.shape[1], (k + 1) * result.shape[1])
        total = parts[0][here, :].astype(f32)
        for ref in parts[1:]:
            total = total + ref[here, :].astype(f32)
        result[k] = total


def output_kernel(dims, *refs):
    slots, n_row, n_col, n_tok = dims
    o_parts, refs = refs[:n_col], refs[n_col:]
    g2_parts, refs = refs[:n_tok], refs[n_tok:]
    output, grad_in, gw2, acc, ints, scalars, sem = refs
    blk, share = acc.shape[-1], acc.shape[1]
    copy = decode_tables(o_parts, 2 * slots * share, ints, scalars, sem)
    add_shares(g2_parts, gw2)
    copy.wait()
    for first, which, result in ((0, W2_OUT, output), (slots, W1_ROW, grad_in)):
        acc[...] = jnp.zeros(acc.shape, f32)
        for c, ref in enumerate(o_parts):
            for k in range(slots):
                at = scalars[c * 8, which * slots + k]
                here = slice((first + k) * share, (first + k + 1) * share)
                acc[at] = acc[at] + ref[here, :].astype(f32)
        for b in range(acc.shape[0]):
            result[:, b * blk : (b + 1) * blk] = acc[b].astype(bf16)


def grad_kernel(*refs):
    add_shares(refs[:-1], refs[-1])


def shards(tokens, w1_blocks, w1_rows, w1_cols, w2_blocks, w2_hidden, w2_outs, grad_out):
    slots, blk = w1_blocks.shape[2], w1_blocks.shape[-1]
    rows = tokens.shape[0]
    n_row, n_col, n_tok = (lax.axis_size(a) for a in ("row", "col", "tok"))
    dims = (slots, n_row, n_col, n_tok)
    row_blocks = tokens.shape[1] // blk
    col_blocks = FF // n_col // blk
    share, part = rows // n_col, blk // n_tok
    w1 = w1_blocks.reshape(slots, blk, blk)
    w2 = w2_blocks.reshape(slots, blk, blk)
    tables = [t.reshape(slots) for t in (w1_rows, w1_cols, w2_hidden, w2_outs)]

    S = jax.ShapeDtypeStruct
    message = S((slots * rows + 16, blk), bf16)
    wide, narrow = S((slots, rows, blk), f32), S((slots, rows, blk), bf16)
    p_send, taken = pl.pallas_call(
        token_kernel,
        out_shape=(message, narrow),
        in_specs=[HBM] * 6,
        out_specs=(VMEM,) * 2,
        scratch_shapes=[pltpu.VMEM((slots, blk, blk), bf16)]
        + [pltpu.SMEM((slots,), jnp.int32)] * 4
        + [pltpu.SemaphoreType.DMA((slots + 5,))],
        compiler_params=pltpu.CompilerParams(vmem_limit_bytes=TAKE_LIMIT),
        name="take_tokens",
    )(*tables, tokens, w1)
    p_peers = [send(p_send, "row", d) for d in range(1, n_row)]
    b_send, cot, p_own, b_own, tab = pl.pallas_call(
        cotangent_kernel,
        out_shape=(message, narrow, wide, wide, S((4 * slots,), jnp.int32)),
        in_specs=[SMEM] * 4 + [HBM] + [VMEM] * 3,
        out_specs=(VMEM,) * 4 + (SMEM,),
        scratch_shapes=[pltpu.SemaphoreType.DMA((slots,))],
        compiler_params=PARAMS,
        name="take_cotangent",
    )(*tables, grad_out, w1, w2, taken)
    b_peers = [send(b_send, "row", d) for d in range(1, n_row)]

    parts = (S((slots * part, blk), bf16),) * n_tok
    outs = (S((2 * slots * share + 16, blk), bf16),) * n_col
    peer_rows = 8 * max(1, n_row - 1)
    active, hidden, peer_tabs, *g2_sent = pl.pallas_call(
        functools.partial(hidden_kernel, dims),
        out_shape=(narrow, wide, S((peer_rows, LANES), jnp.int32)) + parts,
        in_specs=[SMEM] + [VMEM] * (n_row + 1),
        out_specs=(VMEM,) * (3 + n_tok),
        scratch_shapes=[
            pltpu.VMEM((col_blocks, rows, blk), f32),
            pltpu.VMEM((slots, blk, blk), f32),
            pltpu.VMEM((peer_rows, LANES), jnp.int32),
            pltpu.SMEM((peer_rows, LANES), jnp.int32),
            pltpu.SemaphoreType.DMA,
        ],
        compiler_params=PARAMS,
        name="hidden",
    )(tab, p_own, *p_peers, cot)
    g2_parts = [send(x, "tok", d) for d, x in enumerate(g2_sent)]
    out, slope = pl.pallas_call(
        functools.partial(slope_kernel, dims),
        out_shape=(narrow, wide),
        in_specs=[VMEM] * 3,
        out_specs=(VMEM,) * 2,
        compiler_params=PARAMS,
        name="slope",
    )(active, hidden, w2)

    sent = pl.pallas_call(
        functools.partial(back_kernel, dims),
        out_shape=outs + parts,
        in_specs=[SMEM] * 2 + [VMEM] * (n_row + 4),
        out_specs=(VMEM,) * (n_col + n_tok),
        scratch_shapes=[
            pltpu.VMEM((col_blocks, rows, blk), f32),
            pltpu.VMEM((slots, rows, blk), f32),
            pltpu.VMEM((slots, blk, blk), f32),
        ],
        compiler_params=PARAMS,
        name="back",
    )(tab, peer_tabs, b_own, *b_peers, slope, taken, w1, out)
    g1_parts = [send(x, "tok", d) for d, x in enumerate(sent[n_col:])]
    o_parts = [send(x, "col", d) for d, x in enumerate(sent[:n_col])]

    summed = S((slots, part, blk), f32)
    result = S((share, row_blocks * blk), bf16)
    output, grad_in, gw2 = pl.pallas_call(
        functools.partial(output_kernel, dims),
        out_shape=(result, result, summed),
        in_specs=[VMEM] * (n_col + n_tok),
        out_specs=(VMEM,) * 3,
        scratch_shapes=[
            pltpu.VMEM((row_blocks, share, blk), f32),
            pltpu.VMEM((8 * n_col, LANES), jnp.int32),
            pltpu.SMEM((8 * n_col, LANES), jnp.int32),
            pltpu.SemaphoreType.DMA,
        ],
        compiler_params=PARAMS,
        name="add_outputs",
    )(*o_parts, *g2_parts)
    gw1 = pl.pallas_call(
        grad_kernel,
        out_shape=summed,
        in_specs=[VMEM] * n_tok,
        out_specs=VMEM,
        compiler_params=PARAMS,
        name="add_grads",
    )(*g1_parts)
    return (output, grad_in, gw1.reshape(1, 1, slots, part, blk), gw2.reshape(1, 1, slots, part, blk))


def solution(mesh):
    placed = (
        P("tok", "row"),
        P("row", "col", None, None, None),
        P("row", "col", None),
        P("row", "col", None),
        P("row", "col", None, None, None),
        P("row", "col", None),
        P("row", "col", None),
        P("tok", "row"),
    )
    return jax.shard_map(
        shards,
        mesh=mesh,
        in_specs=placed,
        out_specs=(
            P(("tok", "col"), "row"),
            P(("tok", "col"), "row"),
            P("row", "col", None, "tok", None),
            P("row", "col", None, "tok", None),
        ),
        check_vma=False,
    )
```

```python
import functools
import math

import jax
import jax.numpy as jnp
from jax import lax
from jax.experimental import pallas as pl
from jax.experimental.pallas import tpu as pltpu
from jax.sharding import PartitionSpec as P

FF = 32768
f32 = jnp.float32
bf16 = jnp.bfloat16
VMEM = pl.BlockSpec(memory_space=pltpu.VMEM)
SMEM = pl.BlockSpec(memory_space=pltpu.SMEM)
ANY = pl.BlockSpec(memory_space=pl.ANY)
HBM = pl.BlockSpec(memory_space=pltpu.HBM)
LANES = 128
PARAMS = pltpu.CompilerParams(vmem_limit_bytes=32 * 1024 * 1024)

TAKE_LIMIT = 62 * 1024 * 1024

W1_ROW, W1_COL, W2_HID, W2_OUT = range(4)


def dot(a, b, contract):
    return lax.dot_general(a, b, ((contract[:1], contract[1:]), ((), ())), preferred_element_type=f32)


def partner(i, d, n):
    return i ^ d if n & (n - 1) == 0 else (i + d) % n


def send(x, axis, d):
    n = lax.axis_size(axis)
    return lax.ppermute(x, axis, [(i, partner(i, d, n)) for i in range(n)]) if d else x


def exchange(shares, axis):
    return [send(x, axis, d) for d, x in reversed(list(enumerate(shares)))][::-1]


def target(axis, d):
    n = lax.axis_size(axis)
    me = lax.axis_index(axis)
    return jnp.bitwise_xor(me, d) if n & (n - 1) == 0 else lax.rem(me + d, n)


def cdf(v):
    return 0.5 * (1.0 + lax.erf(v * math.sqrt(0.5)))


def table_row(tables, slots):
    lane = lax.broadcasted_iota(jnp.int32, (16, LANES), 1)
    row = jnp.zeros((16, LANES), f32)
    for which, table in enumerate(tables):
        for k in range(slots):
            row = jnp.where(lane == which * slots + k, table[k].astype(f32), row)
    return row.astype(bf16)


def decode_tables(refs, rows, ints, scalars, sem):
    for i, ref in enumerate(refs):
        ints[i * 8 : i * 8 + 8] = ref[rows : rows + 16, :].astype(f32)[:8].astype(jnp.int32)
    copy = pltpu.make_async_copy(ints, scalars, sem)
    copy.start()
    return copy


def start_taking(source, table, taken, sems):
    slots, _, blk = taken.shape
    copies = []
    for k in range(slots):
        begin = pl.multiple_of(table[k] * blk, blk)
        copies.append(pltpu.make_async_copy(source.at[:, pl.ds(begin, blk)], taken.at[k], sems.at[k]))
        copies[-1].start()
    return copies


def token_kernel(t0, t1, t2, t3, tokens, w1, message, taken, w_v, c0, c1, c2, c3, sems):
    slots, rows, blk = taken.shape
    tables = (c0, c1, c2, c3)
    loads = [pltpu.make_async_copy(t, c, sems.at[slots + 1 + i]) for i, (t, c) in enumerate(zip((t0, t1, t2, t3), tables))]
    w_copy = pltpu.make_async_copy(w1, w_v, sems.at[slots])
    for c in loads:
        c.start()
    w_copy.start()
    loads[W1_ROW].wait()
    copies = start_taking(tokens, c0, taken, sems)
    for c in loads[1:]:
        c.wait()
    message[slots * rows :, :] = table_row(tables, slots)
    w_copy.wait()
    for k in range(slots):
        copies[k].wait()
        message[k * rows : (k + 1) * rows, :] = dot(taken[k], w_v[k], (1, 0)).astype(bf16)


def cotangent_kernel(c0, c1, c2, c3, grad_out, w1, w2, taken, message, cot, p_own, b_own, tab, sems):
    slots, rows, blk = cot.shape
    copies = start_taking(grad_out, c3, cot, sems)
    for which, table in enumerate((c0, c1, c2, c3)):
        for k in range(slots):
            tab[which * slots + k] = table[k]
    for k in range(slots):
        copies[k].wait()
        value = dot(cot[k], w2[k], (1, 1))
        b_own[k] = value
        message[k * rows : (k + 1) * rows, :] = value.astype(bf16)
    message[slots * rows :, :] = jnp.zeros((16, blk), bf16)
    for k in range(slots):
        p_own[k] = dot(taken[k], w1[k], (1, 0))


def sum_at(acc, targets, tab, own_at, own, peers, peer_at, slots, scratch):
    ints, scalars, sem = scratch
    rows = acc.shape[1]
    copy = decode_tables(peers, slots * rows, ints, scalars, sem) if peers else None
    for which in targets:
        for k in range(slots):
            acc[tab[which * slots + k]] = jnp.zeros(acc.shape[1:], f32)
    for k in range(slots):
        at = tab[own_at * slots + k]
        acc[at] = acc[at] + own[k]
    if peers:
        copy.wait()
    for i, ref in enumerate(peers):
        for k in range(slots):
            at = scalars[i * 8, peer_at * slots + k]
            acc[at] = acc[at] + ref[k * rows : (k + 1) * rows, :].astype(f32)


def cut(value, refs, k, axis):
    share = value.shape[0] // len(refs)
    for d, ref in enumerate(refs):
        begin = pl.multiple_of(target(axis, d) * share, share)
        ref[k * share : (k + 1) * share, :] = value[pl.ds(begin, share), :].astype(ref.dtype)


def hidden_kernel(dims, tab, p_own, *refs):
    slots, n_row, n_col, n_tok = dims
    p_peers, refs = refs[: n_row - 1], refs[n_row - 1 :]
    cot, active, hidden, peer_tabs = refs[:4]
    grads, refs = refs[4 : 4 + n_tok], refs[4 + n_tok :]
    acc, grad, *scratch = refs
    sum_at(acc, (W1_COL, W2_HID), tab, W1_COL, p_own, p_peers, W1_COL, slots, scratch)
    for k in range(slots):
        h = acc[tab[W2_HID * slots + k]]
        active[k] = (h * cdf(h)).astype(bf16)
        grad[k] = dot(active[k], cot[k], (0, 0))
        cut(grad.at[k], grads, k, "tok")
    for k in range(slots):
        hidden[k] = acc[tab[W1_COL * slots + k]]
    peer_tabs[...] = scratch[0][...]


def slope_kernel(dims, active, hidden, w2, out, slope):
    slots = dims[0]
    for k in range(slots):
        out[k] = dot(active[k], w2[k], (1, 0)).astype(bf16)
    for k in range(slots):
        h = hidden[k]
        slope[k] = cdf(h) + h * jnp.exp(-0.5 * h * h) * (1.0 / math.sqrt(2.0 * math.pi))


def back_kernel(dims, tab, peer_tabs, b_own, *refs):
    slots, n_row, n_col, n_tok = dims
    b_peers, refs = refs[: n_row - 1], refs[n_row - 1 :]
    slope, w1, out, grad_hidden = refs[:4]
    outs, (acc, value) = refs[4 : 4 + n_col], refs[4 + n_col :]
    rows = acc.shape[1]
    for k in range(slots):
        acc[tab[W1_COL * slots + k]] = jnp.zeros(acc.shape[1:], f32)
    for k in range(slots):
        at = tab[W2_HID * slots + k]
        acc[at] = acc[at] + b_own[k]
    for i, ref in enumerate(b_peers):
        for k in range(slots):
            at = peer_tabs[i * 8, W2_HID * slots + k]
            acc[at] = acc[at] + ref[k * rows : (k + 1) * rows, :].astype(f32)
    for k in range(slots):
        g = (acc[tab[W1_COL * slots + k]] * slope[k]).astype(bf16)
        grad_hidden[k] = g
        value[k] = dot(g, w1[k], (1, 1))
        cut(value.at[k], outs, slots + k, "col")
    for k in range(slots):
        cut(out.at[k], outs, k, "col")
    row = table_row([[tab[which * slots + k] for k in range(slots)] for which in range(4)], slots)
    for ref in outs:
        ref[ref.shape[0] - 16 :, :] = row


def add_shares(parts, result):
    for k in range(result.shape[0]):
        here = slice(k * result.shape[1], (k + 1) * result.shape[1])
        total = parts[0][here, :].astype(f32)
        for ref in parts[1:]:
            total = total + ref[here, :].astype(f32)
        result[k] = total


def grads_kernel(dims, taken, grad_hidden, *refs):
    slots, n_row, n_col, n_tok = dims
    g2_parts, gw2 = refs[:n_tok], refs[n_tok]
    grads, grad = refs[n_tok + 1 : -1], refs[-1]
    for k in range(slots):
        grad[k] = dot(taken[k], grad_hidden[k], (0, 0))
        cut(grad.at[k], grads, k, "tok")
    add_shares(g2_parts, gw2)


def output_kernel(dims, *refs):
    slots, n_row, n_col, n_tok = dims
    o_parts, refs = refs[:n_col], refs[n_col:]
    output, grad_in, tabs, acc, ints, scalars, sem = refs
    blk, share = acc.shape[-1], acc.shape[1]
    copy = decode_tables(o_parts, 2 * slots * share, ints, scalars, sem)
    copy.wait()
    tabs[...] = ints[...]
    for first, which, result in ((0, W2_OUT, output), (slots, W1_ROW, grad_in)):
        acc[...] = jnp.zeros(acc.shape, f32)
        for c, ref in enumerate(o_parts):
            for k in range(slots):
                at = scalars[c * 8, which * slots + k]
                here = slice((first + k) * share, (first + k + 1) * share)
                acc[at] = acc[at] + ref[here, :].astype(f32)
        for b in range(acc.shape[0]):
            result[:, b * blk : (b + 1) * blk] = acc[b].astype(bf16)


def grad_kernel(after, *refs):
    del after
    add_shares(refs[:-1], refs[-1])


def shards(tokens, w1_blocks, w1_rows, w1_cols, w2_blocks, w2_hidden, w2_outs, grad_out):
    slots, blk = w1_blocks.shape[2], w1_blocks.shape[-1]
    rows = tokens.shape[0]
    n_row, n_col, n_tok = (lax.axis_size(a) for a in ("row", "col", "tok"))
    dims = (slots, n_row, n_col, n_tok)
    row_blocks = tokens.shape[1] // blk
    col_blocks = FF // n_col // blk
    share, part = rows // n_col, blk // n_tok
    w1 = w1_blocks.reshape(slots, blk, blk)
    w2 = w2_blocks.reshape(slots, blk, blk)
    tables = [t.reshape(slots) for t in (w1_rows, w1_cols, w2_hidden, w2_outs)]

    S = jax.ShapeDtypeStruct
    message = S((slots * rows + 16, blk), bf16)
    wide, narrow = S((slots, rows, blk), f32), S((slots, rows, blk), bf16)
    p_send, taken = pl.pallas_call(
        token_kernel,
        out_shape=(message, narrow),
        in_specs=[HBM] * 6,
        out_specs=(VMEM,) * 2,
        scratch_shapes=[pltpu.VMEM((slots, blk, blk), bf16)]
        + [pltpu.SMEM((slots,), jnp.int32)] * 4
        + [pltpu.SemaphoreType.DMA((slots + 5,))],
        compiler_params=pltpu.CompilerParams(vmem_limit_bytes=TAKE_LIMIT),
        name="take_tokens",
    )(*tables, tokens, w1)
    p_peers = [send(p_send, "row", d) for d in range(1, n_row)]
    b_send, cot, p_own, b_own, tab = pl.pallas_call(
        cotangent_kernel,
        out_shape=(message, narrow, wide, wide, S((4 * slots,), jnp.int32)),
        in_specs=[SMEM] * 4 + [HBM] + [VMEM] * 3,
        out_specs=(VMEM,) * 4 + (SMEM,),
        scratch_shapes=[pltpu.SemaphoreType.DMA((slots,))],
        compiler_params=PARAMS,
        name="take_cotangent",
    )(*tables, grad_out, w1, w2, taken)
    b_peers = [send(b_send, "row", d) for d in range(1, n_row)]

    parts = (S((slots * part, blk), bf16),) * n_tok
    outs = (S((2 * slots * share + 16, blk), bf16),) * n_col
    peer_rows = 8 * max(1, n_row - 1)
    active, hidden, peer_tabs, *g2_sent = pl.pallas_call(
        functools.partial(hidden_kernel, dims),
        out_shape=(narrow, wide, S((peer_rows, LANES), jnp.int32)) + parts,
        in_specs=[SMEM] + [VMEM] * (n_row + 1),
        out_specs=(VMEM,) * (3 + n_tok),
        scratch_shapes=[
            pltpu.VMEM((col_blocks, rows, blk), f32),
            pltpu.VMEM((slots, blk, blk), f32),
            pltpu.VMEM((peer_rows, LANES), jnp.int32),
            pltpu.SMEM((peer_rows, LANES), jnp.int32),
            pltpu.SemaphoreType.DMA,
        ],
        compiler_params=PARAMS,
        name="hidden",
    )(tab, p_own, *p_peers, cot)
    g2_parts = exchange(g2_sent, "tok")
    out, slope = pl.pallas_call(
        functools.partial(slope_kernel, dims),
        out_shape=(narrow, wide),
        in_specs=[VMEM] * 3,
        out_specs=(VMEM,) * 2,
        compiler_params=PARAMS,
        name="slope",
    )(active, hidden, w2)

    grad_hidden, *o_sent = pl.pallas_call(
        functools.partial(back_kernel, dims),
        out_shape=(narrow,) + outs,
        in_specs=[SMEM] * 2 + [VMEM] * (n_row + 3),
        out_specs=(VMEM,) * (1 + n_col),
        scratch_shapes=[
            pltpu.VMEM((col_blocks, rows, blk), f32),
            pltpu.VMEM((slots, rows, blk), f32),
        ],
        compiler_params=PARAMS,
        name="back",
    )(tab, peer_tabs, b_own, *b_peers, slope, w1, out)
    o_parts = exchange(o_sent, "col")

    summed = S((slots, part, blk), f32)
    gw2, *g1_sent = pl.pallas_call(
        functools.partial(grads_kernel, dims),
        out_shape=(summed,) + parts,
        in_specs=[VMEM] * (2 + n_tok),
        out_specs=(VMEM,) * (1 + n_tok),
        scratch_shapes=[pltpu.VMEM((slots, blk, blk), f32)],
        compiler_params=PARAMS,
        name="grads",
    )(taken, grad_hidden, *g2_parts)
    g1_parts = exchange(g1_sent, "tok")

    result = S((share, row_blocks * blk), bf16)
    output, grad_in, tabs = pl.pallas_call(
        functools.partial(output_kernel, dims),
        out_shape=(result, result, S((8 * n_col, LANES), jnp.int32)),
        in_specs=[VMEM] * n_col,
        out_specs=(VMEM,) * 3,
        scratch_shapes=[
            pltpu.VMEM((row_blocks, share, blk), f32),
            pltpu.VMEM((8 * n_col, LANES), jnp.int32),
            pltpu.SMEM((8 * n_col, LANES), jnp.int32),
            pltpu.SemaphoreType.DMA,
        ],
        compiler_params=PARAMS,
        name="add_outputs",
    )(*o_parts)
    gw1 = pl.pallas_call(
        grad_kernel,
        out_shape=summed,
        in_specs=[ANY] + [VMEM] * n_tok,
        out_specs=VMEM,
        compiler_params=PARAMS,
        name="add_grads",
    )(tabs, *g1_parts)
    return (output, grad_in, gw1.reshape(1, 1, slots, part, blk), gw2.reshape(1, 1, slots, part, blk))


def solution(mesh):
    placed = (
        P("tok", "row"),
        P("row", "col", None, None, None),
        P("row", "col", None),
        P("row", "col", None),
        P("row", "col", None, None, None),
        P("row", "col", None),
        P("row", "col", None),
        P("tok", "row"),
    )
    return jax.shard_map(
        shards,
        mesh=mesh,
        in_specs=placed,
        out_specs=(
            P(("tok", "col"), "row"),
            P(("tok", "col"), "row"),
            P("row", "col", None, "tok", None),
            P("row", "col", None, "tok", None),
        ),
        check_vma=False,
    )
```

```python
import functools
import math

import jax
import jax.numpy as jnp
from jax import lax
from jax.experimental import pallas as pl
from jax.experimental.pallas import tpu as pltpu
from jax.sharding import PartitionSpec as P

FF = 32768
f32 = jnp.float32
bf16 = jnp.bfloat16
VMEM = pl.BlockSpec(memory_space=pltpu.VMEM)
SMEM = pl.BlockSpec(memory_space=pltpu.SMEM)
ANY = pl.BlockSpec(memory_space=pl.ANY)
HBM = pl.BlockSpec(memory_space=pltpu.HBM)
LANES = 128
PARAMS = pltpu.CompilerParams(vmem_limit_bytes=32 * 1024 * 1024)

TAKE_LIMIT = 62 * 1024 * 1024

W1_ROW, W1_COL, W2_HID, W2_OUT = range(4)


def dot(a, b, contract):
    return lax.dot_general(a, b, ((contract[:1], contract[1:]), ((), ())), preferred_element_type=f32)


def partner(i, d, n):
    return i ^ d if n & (n - 1) == 0 else (i + d) % n


def send(x, axis, d):
    n = lax.axis_size(axis)
    return lax.ppermute(x, axis, [(i, partner(i, d, n)) for i in range(n)]) if d else x


def exchange(shares, axis):
    return [send(x, axis, d) for d, x in reversed(list(enumerate(shares)))][::-1]


def target(axis, d):
    n = lax.axis_size(axis)
    me = lax.axis_index(axis)
    return jnp.bitwise_xor(me, d) if n & (n - 1) == 0 else lax.rem(me + d, n)


def cdf(v):
    return 0.5 * (1.0 + lax.erf(v * math.sqrt(0.5)))


def table_row(tables, slots):
    lane = lax.broadcasted_iota(jnp.int32, (16, LANES), 1)
    row = jnp.zeros((16, LANES), f32)
    for which, table in enumerate(tables):
        for k in range(slots):
            row = jnp.where(lane == which * slots + k, table[k].astype(f32), row)
    return row.astype(bf16)


def decode_tables(refs, rows, ints, scalars, sem):
    for i, ref in enumerate(refs):
        ints[i * 8 : i * 8 + 8] = ref[rows : rows + 16, :].astype(f32)[:8].astype(jnp.int32)
    copy = pltpu.make_async_copy(ints, scalars, sem)
    copy.start()
    return copy


def start_taking(source, table, taken, sems):
    slots, _, blk = taken.shape
    copies = []
    for k in range(slots):
        begin = pl.multiple_of(table[k] * blk, blk)
        copies.append(pltpu.make_async_copy(source.at[:, pl.ds(begin, blk)], taken.at[k], sems.at[k]))
        copies[-1].start()
    return copies


def token_kernel(t0, t1, t2, t3, tokens, w1, message, taken, w_v, c0, c1, c2, c3, sems):
    slots, rows, blk = taken.shape
    tables = (c0, c1, c2, c3)
    loads = [pltpu.make_async_copy(t, c, sems.at[slots + 1 + i]) for i, (t, c) in enumerate(zip((t0, t1, t2, t3), tables))]
    w_copy = pltpu.make_async_copy(w1, w_v, sems.at[slots])
    for c in loads:
        c.start()
    w_copy.start()
    loads[W1_ROW].wait()
    copies = start_taking(tokens, c0, taken, sems)
    for c in loads[1:]:
        c.wait()
    message[slots * rows :, :] = table_row(tables, slots)
    w_copy.wait()
    for k in range(slots):
        copies[k].wait()
        message[k * rows : (k + 1) * rows, :] = dot(taken[k], w_v[k], (1, 0)).astype(bf16)


def cotangent_kernel(c0, c1, c2, c3, grad_out, w1, w2, taken, message, cot, p_own, b_own, tab, sems):
    slots, rows, blk = cot.shape
    copies = start_taking(grad_out, c3, cot, sems)
    for which, table in enumerate((c0, c1, c2, c3)):
        for k in range(slots):
            tab[which * slots + k] = table[k]
    for k in range(slots):
        copies[k].wait()
        value = dot(cot[k], w2[k], (1, 1))
        b_own[k] = value
        message[k * rows : (k + 1) * rows, :] = value.astype(bf16)
    message[slots * rows :, :] = jnp.zeros((16, blk), bf16)
    for k in range(slots):
        p_own[k] = dot(taken[k], w1[k], (1, 0))


def sum_at(acc, targets, tab, own_at, own, peers, peer_at, slots, scratch):
    ints, scalars, sem = scratch
    rows = acc.shape[1]
    copy = decode_tables(peers, slots * rows, ints, scalars, sem) if peers else None
    for which in targets:
        for k in range(slots):
            acc[tab[which * slots + k]] = jnp.zeros(acc.shape[1:], f32)
    for k in range(slots):
        at = tab[own_at * slots + k]
        acc[at] = acc[at] + own[k]
    if peers:
        copy.wait()
    for i, ref in enumerate(peers):
        for k in range(slots):
            at = scalars[i * 8, peer_at * slots + k]
            acc[at] = acc[at] + ref[k * rows : (k + 1) * rows, :].astype(f32)


def cut(value, refs, k, axis):
    share = value.shape[0] // len(refs)
    for d, ref in enumerate(refs):
        begin = pl.multiple_of(target(axis, d) * share, share)
        ref[k * share : (k + 1) * share, :] = value[pl.ds(begin, share), :].astype(ref.dtype)


def hidden_kernel(dims, tab, p_own, *refs):
    slots, n_row, n_col, n_tok = dims
    p_peers, refs = refs[: n_row - 1], refs[n_row - 1 :]
    cot, active, hidden, peer_tabs, grad, half, acc, *scratch = refs
    part = grad.shape[1] // n_tok
    other = 1 - lax.rem(lax.axis_index("tok"), 2)
    sum_at(acc, (W1_COL, W2_HID), tab, W1_COL, p_own, p_peers, W1_COL, slots, scratch)
    for k in range(slots):
        h = acc[tab[W2_HID * slots + k]]
        active[k] = (h * cdf(h)).astype(bf16)
        grad[k] = dot(active[k], cot[k], (0, 0))
        for j in range(n_tok // 2):
            begin = pl.multiple_of((2 * j + other) * part, part)
            here = (j * slots + k) * part
            half[here : here + part, :] = grad[k, pl.ds(begin, part), :].astype(bf16)
    for k in range(slots):
        hidden[k] = acc[tab[W1_COL * slots + k]]
    peer_tabs[...] = scratch[0][...]


def slope_kernel(dims, active, hidden, w2, out, slope):
    slots = dims[0]
    for k in range(slots):
        out[k] = dot(active[k], w2[k], (1, 0)).astype(bf16)
    for k in range(slots):
        h = hidden[k]
        slope[k] = cdf(h) + h * jnp.exp(-0.5 * h * h) * (1.0 / math.sqrt(2.0 * math.pi))


def back_kernel(dims, tab, peer_tabs, b_own, *refs):
    slots, n_row, n_col, n_tok = dims
    b_peers, refs = refs[: n_row - 1], refs[n_row - 1 :]
    slope, w1, out, taken, grad2, half = refs[:6]
    refs = refs[6:]
    outs, refs = refs[:n_col], refs[n_col:]
    grads, (acc, value, grad) = refs[:n_tok], refs[n_tok:]
    part = grad.shape[1] // n_tok
    rows = acc.shape[1]
    for k in range(slots):
        acc[tab[W1_COL * slots + k]] = jnp.zeros(acc.shape[1:], f32)
    for k in range(slots):
        at = tab[W2_HID * slots + k]
        acc[at] = acc[at] + b_own[k]
    for i, ref in enumerate(b_peers):
        for k in range(slots):
            at = peer_tabs[i * 8, W2_HID * slots + k]
            acc[at] = acc[at] + ref[k * rows : (k + 1) * rows, :].astype(f32)
    for k in range(slots):
        g = (acc[tab[W1_COL * slots + k]] * slope[k]).astype(bf16)
        grad[k] = dot(taken[k], g, (0, 0))
        cut(grad.at[k], grads, k, "tok")
        value[k] = dot(g, w1[k], (1, 1))
        cut(value.at[k], outs, slots + k, "col")
    for k in range(slots):
        cut(out.at[k], outs, k, "col")
    for d in range(0, n_tok, 2 if n_tok % 2 == 0 else 1):
        to = target("tok", d)
        begin = pl.multiple_of(to * part, part)
        for k in range(slots):
            total = grad2[k, pl.ds(begin, part), :]
            if n_tok % 2 == 0:
                there = pl.multiple_of((lax.div(to, 2) * slots + k) * part, part)
                total = total + half[pl.ds(there, part), :].astype(f32)
            grads[d][(slots + k) * part : (slots + k + 1) * part, :] = total.astype(bf16)
    row = table_row([[tab[which * slots + k] for k in range(slots)] for which in range(4)], slots)
    for ref in outs:
        ref[ref.shape[0] - 16 :, :] = row


def add_shares(parts, result, first):
    for k in range(result.shape[0]):
        here = slice((first + k) * result.shape[1], (first + k + 1) * result.shape[1])
        total = parts[0][here, :].astype(f32)
        for ref in parts[1:]:
            total = total + ref[here, :].astype(f32)
        result[k] = total


def output_kernel(dims, *refs):
    slots, n_row, n_col, n_tok = dims
    o_parts, refs = refs[:n_col], refs[n_col:]
    output, grad_in, tabs, acc, ints, scalars, sem = refs
    blk, share = acc.shape[-1], acc.shape[1]
    copy = decode_tables(o_parts, 2 * slots * share, ints, scalars, sem)
    copy.wait()
    tabs[...] = ints[...]
    for first, which, result in ((0, W2_OUT, output), (slots, W1_ROW, grad_in)):
        acc[...] = jnp.zeros(acc.shape, f32)
        for c, ref in enumerate(o_parts):
            for k in range(slots):
                at = scalars[c * 8, which * slots + k]
                here = slice((first + k) * share, (first + k + 1) * share)
                acc[at] = acc[at] + ref[here, :].astype(f32)
        for b in range(acc.shape[0]):
            result[:, b * blk : (b + 1) * blk] = acc[b].astype(bf16)


def grad_kernel(after, *refs):
    del after
    parts, gw1, gw2 = refs[:-2], refs[-2], refs[-1]
    slots = gw1.shape[0]
    add_shares(parts, gw1, 0)
    add_shares([ref for ref in parts if ref.shape[0] > slots * gw1.shape[1]], gw2, slots)


def shards(tokens, w1_blocks, w1_rows, w1_cols, w2_blocks, w2_hidden, w2_outs, grad_out):
    slots, blk = w1_blocks.shape[2], w1_blocks.shape[-1]
    rows = tokens.shape[0]
    n_row, n_col, n_tok = (lax.axis_size(a) for a in ("row", "col", "tok"))
    dims = (slots, n_row, n_col, n_tok)
    row_blocks = tokens.shape[1] // blk
    col_blocks = FF // n_col // blk
    share, part = rows // n_col, blk // n_tok
    w1 = w1_blocks.reshape(slots, blk, blk)
    w2 = w2_blocks.reshape(slots, blk, blk)
    tables = [t.reshape(slots) for t in (w1_rows, w1_cols, w2_hidden, w2_outs)]

    S = jax.ShapeDtypeStruct
    message = S((slots * rows + 16, blk), bf16)
    wide, narrow = S((slots, rows, blk), f32), S((slots, rows, blk), bf16)
    p_send, taken = pl.pallas_call(
        token_kernel,
        out_shape=(message, narrow),
        in_specs=[HBM] * 6,
        out_specs=(VMEM,) * 2,
        scratch_shapes=[pltpu.VMEM((slots, blk, blk), bf16)]
        + [pltpu.SMEM((slots,), jnp.int32)] * 4
        + [pltpu.SemaphoreType.DMA((slots + 5,))],
        compiler_params=pltpu.CompilerParams(vmem_limit_bytes=TAKE_LIMIT),
        name="take_tokens",
    )(*tables, tokens, w1)
    p_peers = [send(p_send, "row", d) for d in range(1, n_row)]
    b_send, cot, p_own, b_own, tab = pl.pallas_call(
        cotangent_kernel,
        out_shape=(message, narrow, wide, wide, S((4 * slots,), jnp.int32)),
        in_specs=[SMEM] * 4 + [HBM] + [VMEM] * 3,
        out_specs=(VMEM,) * 4 + (SMEM,),
        scratch_shapes=[pltpu.SemaphoreType.DMA((slots,))],
        compiler_params=PARAMS,
        name="take_cotangent",
    )(*tables, grad_out, w1, w2, taken)
    b_peers = [send(b_send, "row", d) for d in range(1, n_row)]

    both = [n_tok % 2 == 1 or d % 2 == 0 for d in range(n_tok)]
    grads = tuple(S(((2 if b else 1) * slots * part, blk), bf16) for b in both)
    half = S((max(1, n_tok // 2) * slots * part, blk), bf16)
    outs = (S((2 * slots * share + 16, blk), bf16),) * n_col
    peer_rows = 8 * max(1, n_row - 1)
    active, hidden, peer_tabs, grad2, half = pl.pallas_call(
        functools.partial(hidden_kernel, dims),
        out_shape=(narrow, wide, S((peer_rows, LANES), jnp.int32), S((slots, blk, blk), f32), half),
        in_specs=[SMEM] + [VMEM] * (n_row + 1),
        out_specs=(VMEM,) * 5,
        scratch_shapes=[
            pltpu.VMEM((col_blocks, rows, blk), f32),
            pltpu.VMEM((peer_rows, LANES), jnp.int32),
            pltpu.SMEM((peer_rows, LANES), jnp.int32),
            pltpu.SemaphoreType.DMA,
        ],
        compiler_params=PARAMS,
        name="hidden",
    )(tab, p_own, *p_peers, cot)
    if n_tok % 2 == 0:
        half = lax.ppermute(half, "tok", [(i, i ^ 1) for i in range(n_tok)])
    out, slope = pl.pallas_call(
        functools.partial(slope_kernel, dims),
        out_shape=(narrow, wide),
        in_specs=[VMEM] * 3,
        out_specs=(VMEM,) * 2,
        compiler_params=PARAMS,
        name="slope",
    )(active, hidden, w2)

    sent = pl.pallas_call(
        functools.partial(back_kernel, dims),
        out_shape=outs + grads,
        in_specs=[SMEM] * 2 + [VMEM] * (n_row + 6),
        out_specs=(VMEM,) * (n_col + n_tok),
        scratch_shapes=[
            pltpu.VMEM((col_blocks, rows, blk), f32),
            pltpu.VMEM((slots, rows, blk), f32),
            pltpu.VMEM((slots, blk, blk), f32),
        ],
        compiler_params=PARAMS,
        name="back",
    )(tab, peer_tabs, b_own, *b_peers, slope, w1, out, taken, grad2, half)
    g_parts = exchange(sent[n_col:], "tok")
    o_parts = exchange(sent[:n_col], "col")

    result = S((share, row_blocks * blk), bf16)
    output, grad_in, tabs = pl.pallas_call(
        functools.partial(output_kernel, dims),
        out_shape=(result, result, S((8 * n_col, LANES), jnp.int32)),
        in_specs=[VMEM] * n_col,
        out_specs=(VMEM,) * 3,
        scratch_shapes=[
            pltpu.VMEM((row_blocks, share, blk), f32),
            pltpu.VMEM((8 * n_col, LANES), jnp.int32),
            pltpu.SMEM((8 * n_col, LANES), jnp.int32),
            pltpu.SemaphoreType.DMA,
        ],
        compiler_params=PARAMS,
        name="add_outputs",
    )(*o_parts)
    summed = S((slots, part, blk), f32)
    gw1, gw2 = pl.pallas_call(
        grad_kernel,
        out_shape=(summed, summed),
        in_specs=[ANY] + [VMEM] * n_tok,
        out_specs=(VMEM,) * 2,
        compiler_params=PARAMS,
        name="add_grads",
    )(tabs, *g_parts)
    return (output, grad_in, gw1.reshape(1, 1, slots, part, blk), gw2.reshape(1, 1, slots, part, blk))


def solution(mesh):
    placed = (
        P("tok", "row"),
        P("row", "col", None, None, None),
        P("row", "col", None),
        P("row", "col", None),
        P("row", "col", None, None, None),
        P("row", "col", None),
        P("row", "col", None),
        P("tok", "row"),
    )
    return jax.shard_map(
        shards,
        mesh=mesh,
        in_specs=placed,
        out_specs=(
            P(("tok", "col"), "row"),
            P(("tok", "col"), "row"),
            P("row", "col", None, "tok", None),
            P("row", "col", None, "tok", None),
        ),
        check_vma=False,
    )
```

```python
import functools
import math

import jax
import jax.numpy as jnp
from jax import lax
from jax.experimental import pallas as pl
from jax.experimental.pallas import tpu as pltpu
from jax.sharding import PartitionSpec as P

FF = 32768
f32 = jnp.float32
bf16 = jnp.bfloat16
VMEM = pl.BlockSpec(memory_space=pltpu.VMEM)
SMEM = pl.BlockSpec(memory_space=pltpu.SMEM)
ANY = pl.BlockSpec(memory_space=pl.ANY)
HBM = pl.BlockSpec(memory_space=pltpu.HBM)
LANES = 128
PARAMS = pltpu.CompilerParams(vmem_limit_bytes=32 * 1024 * 1024)

TAKE_LIMIT = 62 * 1024 * 1024

W1_ROW, W1_COL, W2_HID, W2_OUT = range(4)


def dot(a, b, contract):
    return lax.dot_general(a, b, ((contract[:1], contract[1:]), ((), ())), preferred_element_type=f32)


def partner(i, d, n):
    return i ^ d if n & (n - 1) == 0 else (i + d) % n


def send(x, axis, d):
    n = lax.axis_size(axis)
    return lax.ppermute(x, axis, [(i, partner(i, d, n)) for i in range(n)]) if d else x


def exchange(shares, axis):
    return [send(x, axis, d) for d, x in reversed(list(enumerate(shares)))][::-1]


def target(axis, d):
    n = lax.axis_size(axis)
    me = lax.axis_index(axis)
    return jnp.bitwise_xor(me, d) if n & (n - 1) == 0 else lax.rem(me + d, n)


def cdf(v):
    return 0.5 * (1.0 + lax.erf(v * math.sqrt(0.5)))


def table_row(tables, slots):
    lane = lax.broadcasted_iota(jnp.int32, (16, LANES), 1)
    row = jnp.zeros((16, LANES), f32)
    for which, table in enumerate(tables):
        for k in range(slots):
            row = jnp.where(lane == which * slots + k, table[k].astype(f32), row)
    return row.astype(bf16)


def decode_tables(refs, rows, ints, scalars, sem):
    for i, ref in enumerate(refs):
        ints[i * 8 : i * 8 + 8] = ref[rows : rows + 16, :].astype(f32)[:8].astype(jnp.int32)
    copy = pltpu.make_async_copy(ints, scalars, sem)
    copy.start()
    return copy


def start_taking(source, table, taken, sems):
    slots, _, blk = taken.shape
    copies = []
    for k in range(slots):
        begin = pl.multiple_of(table[k] * blk, blk)
        copies.append(pltpu.make_async_copy(source.at[:, pl.ds(begin, blk)], taken.at[k], sems.at[k]))
        copies[-1].start()
    return copies


def token_kernel(t0, t1, t2, t3, tokens, w1, message, tokens_v, w_v, sent, c0, c1, c2, c3, sems):
    slots, blk, _ = w_v.shape
    rows = tokens_v.shape[0]
    tables = (c0, c1, c2, c3)
    loads = [pltpu.make_async_copy(t, c, sems.at[i]) for i, (t, c) in enumerate(zip((t0, t1, t2, t3), tables))]
    loads.append(pltpu.make_async_copy(tokens, tokens_v, sems.at[4]))
    loads.append(pltpu.make_async_copy(w1, w_v, sems.at[5]))
    stores = []

    def store(begin, size):
        here = pl.ds(begin, size)
        stores.append(pltpu.make_async_copy(sent.at[here], message.at[here], sems.at[6 + len(stores)]))
        stores[-1].start()

    for c in loads:
        c.start()
    for c in loads[:4]:
        c.wait()
    sent[slots * rows :, :] = table_row(tables, slots)
    store(slots * rows, 16)
    for c in loads[4:]:
        c.wait()
    for k in range(slots):
        here = pl.ds(pl.multiple_of(c0[k] * blk, blk), blk)
        sent[k * rows : (k + 1) * rows, :] = dot(tokens_v[:, here], w_v[k], (1, 0)).astype(bf16)
        store(k * rows, rows)
    for c in stores:
        c.wait()


def cotangent_kernel(c0, c1, c2, c3, tokens, grad_out, w1, w2, message, taken, cot, p_own, b_own, tab, sems):
    slots, rows, blk = cot.shape
    copies = start_taking(grad_out, c3, cot, sems.at[0])
    copies_t = start_taking(tokens, c0, taken, sems.at[1])
    for which, table in enumerate((c0, c1, c2, c3)):
        for k in range(slots):
            tab[which * slots + k] = table[k]
    for k in range(slots):
        copies[k].wait()
        value = dot(cot[k], w2[k], (1, 1))
        b_own[k] = value
        message[k * rows : (k + 1) * rows, :] = value.astype(bf16)
    message[slots * rows :, :] = jnp.zeros((16, blk), bf16)
    for k in range(slots):
        copies_t[k].wait()
        p_own[k] = dot(taken[k], w1[k], (1, 0))


def sum_at(acc, targets, tab, own_at, own, peers, peer_at, slots, scratch):
    ints, scalars, sem = scratch
    rows = acc.shape[1]
    copy = decode_tables(peers, slots * rows, ints, scalars, sem) if peers else None
    for which in targets:
        for k in range(slots):
            acc[tab[which * slots + k]] = jnp.zeros(acc.shape[1:], f32)
    for k in range(slots):
        at = tab[own_at * slots + k]
        acc[at] = acc[at] + own[k]
    if peers:
        copy.wait()
    for i, ref in enumerate(peers):
        for k in range(slots):
            at = scalars[i * 8, peer_at * slots + k]
            acc[at] = acc[at] + ref[k * rows : (k + 1) * rows, :].astype(f32)


def cut(value, refs, k, axis):
    share = value.shape[0] // len(refs)
    for d, ref in enumerate(refs):
        begin = pl.multiple_of(target(axis, d) * share, share)
        ref[k * share : (k + 1) * share, :] = value[pl.ds(begin, share), :].astype(ref.dtype)


def hidden_kernel(dims, tab, p_own, *refs):
    slots, n_row, n_col, n_tok = dims
    p_peers, refs = refs[: n_row - 1], refs[n_row - 1 :]
    cot, active, hidden, peer_tabs, grad, half, acc, *scratch = refs
    part = grad.shape[1] // n_tok
    other = 1 - lax.rem(lax.axis_index("tok"), 2)
    sum_at(acc, (W1_COL, W2_HID), tab, W1_COL, p_own, p_peers, W1_COL, slots, scratch)
    for k in range(slots):
        h = acc[tab[W2_HID * slots + k]]
        active[k] = (h * cdf(h)).astype(bf16)
        grad[k] = dot(active[k], cot[k], (0, 0))
        for j in range(n_tok // 2):
            begin = pl.multiple_of((2 * j + other) * part, part)
            here = (j * slots + k) * part
            half[here : here + part, :] = grad[k, pl.ds(begin, part), :].astype(bf16)
    for k in range(slots):
        hidden[k] = acc[tab[W1_COL * slots + k]]
    peer_tabs[...] = scratch[0][...]


def slope_kernel(dims, active, hidden, w2, out, slope):
    slots = dims[0]
    for k in range(slots):
        out[k] = dot(active[k], w2[k], (1, 0)).astype(bf16)
    for k in range(slots):
        h = hidden[k]
        slope[k] = cdf(h) + h * jnp.exp(-0.5 * h * h) * (1.0 / math.sqrt(2.0 * math.pi))


def back_kernel(dims, tab, peer_tabs, b_own, *refs):
    slots, n_row, n_col, n_tok = dims
    b_peers, refs = refs[: n_row - 1], refs[n_row - 1 :]
    slope, w1, out, taken, grad2, half = refs[:6]
    refs = refs[6:]
    outs, refs = refs[:n_col], refs[n_col:]
    grads, (acc, value, grad) = refs[:n_tok], refs[n_tok:]
    part = grad.shape[1] // n_tok
    rows = acc.shape[1]
    for k in range(slots):
        acc[tab[W1_COL * slots + k]] = jnp.zeros(acc.shape[1:], f32)
    for k in range(slots):
        at = tab[W2_HID * slots + k]
        acc[at] = acc[at] + b_own[k]
    for i, ref in enumerate(b_peers):
        for k in range(slots):
            at = peer_tabs[i * 8, W2_HID * slots + k]
            acc[at] = acc[at] + ref[k * rows : (k + 1) * rows, :].astype(f32)
    for k in range(slots):
        g = (acc[tab[W1_COL * slots + k]] * slope[k]).astype(bf16)
        grad[k] = dot(taken[k], g, (0, 0))
        cut(grad.at[k], grads, k, "tok")
        value[k] = dot(g, w1[k], (1, 1))
        cut(value.at[k], outs, slots + k, "col")
    for k in range(slots):
        cut(out.at[k], outs, k, "col")
    for d in range(0, n_tok, 2 if n_tok % 2 == 0 else 1):
        to = target("tok", d)
        begin = pl.multiple_of(to * part, part)
        for k in range(slots):
            total = grad2[k, pl.ds(begin, part), :]
            if n_tok % 2 == 0:
                there = pl.multiple_of((lax.div(to, 2) * slots + k) * part, part)
                total = total + half[pl.ds(there, part), :].astype(f32)
            grads[d][(slots + k) * part : (slots + k + 1) * part, :] = total.astype(bf16)
    row = table_row([[tab[which * slots + k] for k in range(slots)] for which in range(4)], slots)
    for ref in outs:
        ref[ref.shape[0] - 16 :, :] = row


def add_shares(parts, result, first):
    for k in range(result.shape[0]):
        here = slice((first + k) * result.shape[1], (first + k + 1) * result.shape[1])
        total = parts[0][here, :].astype(f32)
        for ref in parts[1:]:
            total = total + ref[here, :].astype(f32)
        result[k] = total


def output_kernel(dims, *refs):
    slots, n_row, n_col, n_tok = dims
    first = min(2, n_col)
    o_parts, refs = refs[:first] + refs[first + 1 : n_col + 1], refs[n_col + 1 :]
    output, grad_in, tabs, acc_out, acc_in, scalars, sem = refs
    blk, share = acc_out.shape[-1], acc_out.shape[1]
    copy = decode_tables(o_parts, 2 * slots * share, tabs, scalars, sem)
    acc_out[...] = jnp.zeros(acc_out.shape, f32)
    acc_in[...] = jnp.zeros(acc_in.shape, f32)
    copy.wait()
    for first, which, acc, result in ((0, W2_OUT, acc_out, output), (slots, W1_ROW, acc_in, grad_in)):
        for c, ref in enumerate(o_parts):
            for k in range(slots):
                at = scalars[c * 8, which * slots + k]
                here = slice((first + k) * share, (first + k + 1) * share)
                acc[at] = acc[at] + ref[here, :].astype(f32)
        for b in range(acc.shape[0]):
            result[:, b * blk : (b + 1) * blk] = acc[b].astype(bf16)


def grad_kernel(after, *refs):
    del after
    parts, gw1, gw2 = refs[:-2], refs[-2], refs[-1]
    slots = gw1.shape[0]
    add_shares(parts, gw1, 0)
    add_shares([ref for ref in parts if ref.shape[0] > slots * gw1.shape[1]], gw2, slots)


def shards(tokens, w1_blocks, w1_rows, w1_cols, w2_blocks, w2_hidden, w2_outs, grad_out):
    slots, blk = w1_blocks.shape[2], w1_blocks.shape[-1]
    rows = tokens.shape[0]
    n_row, n_col, n_tok = (lax.axis_size(a) for a in ("row", "col", "tok"))
    dims = (slots, n_row, n_col, n_tok)
    row_blocks = tokens.shape[1] // blk
    col_blocks = FF // n_col // blk
    share, part = rows // n_col, blk // n_tok
    w1 = w1_blocks.reshape(slots, blk, blk)
    w2 = w2_blocks.reshape(slots, blk, blk)
    tables = [t.reshape(slots) for t in (w1_rows, w1_cols, w2_hidden, w2_outs)]

    S = jax.ShapeDtypeStruct
    message = S((slots * rows + 16, blk), bf16)
    wide, narrow = S((slots, rows, blk), f32), S((slots, rows, blk), bf16)
    p_send = pl.pallas_call(
        token_kernel,
        out_shape=message,
        in_specs=[HBM] * 6,
        out_specs=HBM,
        scratch_shapes=[
            pltpu.VMEM(tokens.shape, bf16),
            pltpu.VMEM((slots, blk, blk), bf16),
            pltpu.VMEM((slots * rows + 16, blk), bf16),
        ]
        + [pltpu.SMEM((slots,), jnp.int32)] * 4
        + [pltpu.SemaphoreType.DMA((7 + slots,))],
        compiler_params=pltpu.CompilerParams(vmem_limit_bytes=TAKE_LIMIT),
        name="take_tokens",
    )(*tables, tokens, w1)
    p_peers = [send(p_send, "row", d) for d in range(1, n_row)]
    b_send, taken, cot, p_own, b_own, tab = pl.pallas_call(
        cotangent_kernel,
        out_shape=(message, narrow, narrow, wide, wide, S((4 * slots,), jnp.int32)),
        in_specs=[SMEM] * 4 + [HBM, HBM] + [VMEM] * 2,
        out_specs=(VMEM,) * 5 + (SMEM,),
        scratch_shapes=[pltpu.SemaphoreType.DMA((2, slots))],
        compiler_params=PARAMS,
        name="take_cotangent",
    )(*tables, tokens, grad_out, w1, w2)
    b_peers = [send(b_send, "row", d) for d in range(1, n_row)]

    both = [n_tok % 2 == 1 or d % 2 == 0 for d in range(n_tok)]
    grads = tuple(S(((2 if b else 1) * slots * part, blk), bf16) for b in both)
    half = S((max(1, n_tok // 2) * slots * part, blk), bf16)
    outs = (S((2 * slots * share + 16, blk), bf16),) * n_col
    peer_rows = 8 * max(1, n_row - 1)
    active, hidden, peer_tabs, grad2, half = pl.pallas_call(
        functools.partial(hidden_kernel, dims),
        out_shape=(narrow, wide, S((peer_rows, LANES), jnp.int32), S((slots, blk, blk), f32), half),
        in_specs=[SMEM] + [VMEM] * (n_row + 1),
        out_specs=(VMEM,) * 5,
        scratch_shapes=[
            pltpu.VMEM((col_blocks, rows, blk), f32),
            pltpu.VMEM((peer_rows, LANES), jnp.int32),
            pltpu.SMEM((peer_rows, LANES), jnp.int32),
            pltpu.SemaphoreType.DMA,
        ],
        compiler_params=PARAMS,
        name="hidden",
    )(tab, p_own, *p_peers, cot)
    if n_tok % 2 == 0:
        half = lax.ppermute(half, "tok", [(i, i ^ 1) for i in range(n_tok)])
    out, slope = pl.pallas_call(
        functools.partial(slope_kernel, dims),
        out_shape=(narrow, wide),
        in_specs=[VMEM] * 3,
        out_specs=(VMEM,) * 2,
        compiler_params=PARAMS,
        name="slope",
    )(active, hidden, w2)

    sent = pl.pallas_call(
        functools.partial(back_kernel, dims),
        out_shape=outs + grads,
        in_specs=[SMEM] * 2 + [VMEM] * (n_row + 6),
        out_specs=(VMEM,) * (n_col + n_tok),
        scratch_shapes=[
            pltpu.VMEM((col_blocks, rows, blk), f32),
            pltpu.VMEM((slots, rows, blk), f32),
            pltpu.VMEM((slots, blk, blk), f32),
        ],
        compiler_params=PARAMS,
        name="back",
    )(tab, peer_tabs, b_own, *b_peers, slope, w1, out, taken, grad2, half)
    g_parts = exchange(sent[n_col:], "tok")
    o_parts = exchange(sent[:n_col], "col")

    first = min(2, n_col)
    result = S((share, row_blocks * blk), bf16)
    output, grad_in, tabs = pl.pallas_call(
        functools.partial(output_kernel, dims),
        out_shape=(result, result, S((8 * n_col, LANES), jnp.int32)),
        in_specs=[VMEM] * first + [ANY] + [VMEM] * (n_col - first),
        out_specs=(VMEM,) * 3,
        scratch_shapes=[
            pltpu.VMEM((row_blocks, share, blk), f32),
            pltpu.VMEM((row_blocks, share, blk), f32),
            pltpu.SMEM((8 * n_col, LANES), jnp.int32),
            pltpu.SemaphoreType.DMA,
        ],
        compiler_params=PARAMS,
        name="add_outputs",
    )(*o_parts[:first], g_parts[n_tok // 2], *o_parts[first:])
    summed = S((slots, part, blk), f32)
    gw1, gw2 = pl.pallas_call(
        grad_kernel,
        out_shape=(summed, summed),
        in_specs=[ANY] + [VMEM] * n_tok,
        out_specs=(VMEM,) * 2,
        compiler_params=PARAMS,
        name="add_grads",
    )(tabs, *g_parts[::-1])
    return (output, grad_in, gw1.reshape(1, 1, slots, part, blk), gw2.reshape(1, 1, slots, part, blk))


def solution(mesh):
    placed = (
        P("tok", "row"),
        P("row", "col", None, None, None),
        P("row", "col", None),
        P("row", "col", None),
        P("row", "col", None, None, None),
        P("row", "col", None),
        P("row", "col", None),
        P("tok", "row"),
    )
    return jax.shard_map(
        shards,
        mesh=mesh,
        in_specs=placed,
        out_specs=(
            P(("tok", "col"), "row"),
            P(("tok", "col"), "row"),
            P("row", "col", None, "tok", None),
            P("row", "col", None, "tok", None),
        ),
        check_vma=False,
    )
```

```python
import functools
import math

import jax
import jax.numpy as jnp
from jax import lax
from jax.experimental import pallas as pl
from jax.experimental.pallas import tpu as pltpu
from jax.sharding import PartitionSpec as P

FF = 32768
LANES = 128
f32 = jnp.float32
bf16 = jnp.bfloat16
VMEM = pl.BlockSpec(memory_space=pltpu.VMEM)
SMEM = pl.BlockSpec(memory_space=pltpu.SMEM)
ANY = pl.BlockSpec(memory_space=pl.ANY)
HBM = pl.BlockSpec(memory_space=pltpu.HBM)
TAKE_LIMIT = 62 * 1024 * 1024
LIMIT = 32 * 1024 * 1024

W1_ROW, W1_COL, W2_HID, W2_OUT = range(4)


def call(kernel, name, limit=LIMIT, **kwargs):
    return pl.pallas_call(
        kernel,
        name=name,
        compiler_params=pltpu.CompilerParams(vmem_limit_bytes=limit),
        cost_estimate=pl.CostEstimate(flops=1 << 25, bytes_accessed=1 << 19, transcendentals=0),
        **kwargs,
    )


def dot(a, b, contract):
    return lax.dot_general(a, b, ((contract[:1], contract[1:]), ((), ())), preferred_element_type=f32)


def cdf(v):
    return 0.5 * (1.0 + lax.erf(v * math.sqrt(0.5)))


def partner(i, d, n):
    return i ^ d if n & (n - 1) == 0 else (i + d) % n


def target(axis, d):
    n = lax.axis_size(axis)
    me = lax.axis_index(axis)
    return jnp.bitwise_xor(me, d) if n & (n - 1) == 0 else lax.rem(me + d, n)


def send(x, axis, d):
    n = lax.axis_size(axis)
    return lax.ppermute(x, axis, [(i, partner(i, d, n)) for i in range(n)]) if d else x


def cut(value, refs, k, axis):
    share = value.shape[0] // len(refs)
    for d, ref in enumerate(refs):
        begin = pl.multiple_of(target(axis, d) * share, share)
        ref[k * share : (k + 1) * share, :] = value[pl.ds(begin, share), :].astype(ref.dtype)


def table_row(tables, slots):
    lane = lax.broadcasted_iota(jnp.int32, (16, LANES), 1)
    row = jnp.zeros((16, LANES), f32)
    for which, table in enumerate(tables):
        for k in range(slots):
            row = jnp.where(lane == which * slots + k, table[k].astype(f32), row)
    return row.astype(bf16)


def decode_tables(refs, rows, ints, scalars, sem):
    for i, ref in enumerate(refs):
        ints[i * 8 : i * 8 + 8] = ref[rows : rows + 16, :].astype(f32)[:8].astype(jnp.int32)
    copy = pltpu.make_async_copy(ints, scalars, sem)
    copy.start()
    return copy


def token_kernel(t0, t1, t2, t3, tokens, w1, message, tokens_v, w_v, sent, c0, c1, c2, c3, sems):
    slots, blk, _ = w_v.shape
    rows = tokens_v.shape[0]
    tables = (c0, c1, c2, c3)
    loads = [pltpu.make_async_copy(t, c, sems.at[i]) for i, (t, c) in enumerate(zip((t0, t1, t2, t3), tables))]
    loads.append(pltpu.make_async_copy(tokens, tokens_v, sems.at[4]))
    loads.append(pltpu.make_async_copy(w1, w_v, sems.at[5]))
    stores = []

    def store(begin, size):
        here = pl.ds(begin, size)
        stores.append(pltpu.make_async_copy(sent.at[here], message.at[here], sems.at[6 + len(stores)]))
        stores[-1].start()

    for c in loads:
        c.start()
    for c in loads[:4]:
        c.wait()
    sent[slots * rows :, :] = table_row(tables, slots)
    store(slots * rows, 16)
    for c in loads[4:]:
        c.wait()
    for k in range(slots):
        here = pl.ds(pl.multiple_of(c0[k] * blk, blk), blk)
        sent[k * rows : (k + 1) * rows, :] = dot(tokens_v[:, here], w_v[k], (1, 0)).astype(bf16)
        store(k * rows, rows)
    for c in stores:
        c.wait()


def first_place(tab, slots, k):
    return tab[4 * slots + k]


def place_of(tab, slots, block):
    return tab[6 * slots + block]


def start_taking(source, table, taken, sems):
    slots, _, blk = taken.shape
    copies = []
    for k in range(slots):
        begin = pl.multiple_of(table[k] * blk, blk)
        copies.append(pltpu.make_async_copy(source.at[:, pl.ds(begin, blk)], taken.at[k], sems.at[k]))
        copies[-1].start()
    return copies


def cotangent_kernel(c0, c1, c2, c3, tokens, grad_out, w1, w2, message, taken, cot, hid, back, tab, sems):
    slots, rows, blk = cot.shape
    copies = start_taking(grad_out, c3, cot, sems.at[0])
    copies_t = start_taking(tokens, c0, taken, sems.at[1])
    for which, table in enumerate((c0, c1, c2, c3)):
        for k in range(slots):
            tab[which * slots + k] = table[k]

    @pl.loop(0, tab.shape[0] - 6 * slots)
    def _(block):
        tab[6 * slots + block] = 2 * slots

    for j in range(2 * slots):
        block = c1[j] if j < slots else c2[j - slots]
        place = jnp.minimum(place_of(tab, slots, block), j)
        tab[6 * slots + block] = place
        tab[4 * slots + j] = place
    hid[...] = jnp.zeros(hid.shape, f32)
    back[...] = jnp.zeros(back.shape, f32)
    message[slots * rows :, :] = jnp.zeros((16, blk), bf16)
    for k in range(slots):
        copies[k].wait()
        value = dot(cot[k], w2[k], (1, 1))
        message[k * rows : (k + 1) * rows, :] = value.astype(bf16)
        at = jnp.minimum(place_of(tab, slots, c2[k]), slots)
        back[at] = back[at] + value
    for k in range(slots):
        copies_t[k].wait()
        at = place_of(tab, slots, c1[k])
        hid[at] = hid[at] + dot(taken[k], w1[k], (1, 0))


def add_peers(acc, own, tab, tables, which, peers, slots):
    places, rows, _ = acc.shape
    for j in range(places):
        acc[j] = own[j]
    for i, ref in enumerate(peers):
        for k in range(slots):
            at = place_of(tab, slots, tables[i * 8, which * slots + k])

            @pl.when(at < places)
            def _():
                acc[at] = acc[at] + ref[k * rows : (k + 1) * rows, :].astype(f32)


def hidden_kernel(dims, tab, own, *refs):
    slots, n_row, n_col, n_tok = dims
    peers, refs = refs[: n_row - 1], refs[n_row - 1 :]
    cot, active, hid, tabs, grad, half, scalars, sem = refs
    part = grad.shape[1] // n_tok
    other = 1 - lax.rem(lax.axis_index("tok"), 2)
    if peers:
        decode_tables(peers, slots * cot.shape[1], tabs, scalars, sem).wait()
    else:
        tabs[...] = jnp.zeros(tabs.shape, jnp.int32)
    add_peers(hid, own, tab, scalars, W1_COL, peers, slots)
    for k in range(slots):
        h = hid[first_place(tab, slots, slots + k)]
        active[k] = (h * cdf(h)).astype(bf16)
        grad[k] = dot(active[k], cot[k], (0, 0))
        for j in range(n_tok // 2):
            begin = pl.multiple_of((2 * j + other) * part, part)
            here = (j * slots + k) * part
            half[here : here + part, :] = grad[k, pl.ds(begin, part), :].astype(bf16)


def slope_kernel(dims, tab, active, hid, w2, out, slope):
    slots = dims[0]
    for k in range(slots):
        out[k] = dot(active[k], w2[k], (1, 0)).astype(bf16)
    for k in range(slots):
        h = hid[first_place(tab, slots, k)]
        slope[k] = cdf(h) + h * jnp.exp(-0.5 * h * h) * (1.0 / math.sqrt(2.0 * math.pi))


def back_kernel(dims, tab, tabs, own, *refs):
    slots, n_row, n_col, n_tok = dims
    peers, refs = refs[: n_row - 1], refs[n_row - 1 :]
    slope, w1, out, taken, grad2, half = refs[:6]
    refs = refs[6:]
    outs, refs = refs[:n_col], refs[n_col:]
    grads, (acc, value, grad) = refs[:n_tok], refs[n_tok:]
    part = grad.shape[1] // n_tok
    paired = n_tok % 2 == 0
    add_peers(acc, own, tab, tabs, W2_HID, peers, slots)
    for k in range(slots):
        g = (acc[first_place(tab, slots, k)] * slope[k]).astype(bf16)
        grad[k] = dot(taken[k], g, (0, 0))
        cut(grad.at[k], grads, k, "tok")
        value[k] = dot(g, w1[k], (1, 1))
        cut(value.at[k], outs, slots + k, "col")
    for k in range(slots):
        cut(out.at[k], outs, k, "col")
    for d in range(0, n_tok, 2 if paired else 1):
        to = target("tok", d)
        begin = pl.multiple_of(to * part, part)
        for k in range(slots):
            total = grad2[k, pl.ds(begin, part), :]
            if paired:
                there = pl.multiple_of((lax.div(to, 2) * slots + k) * part, part)
                total = total + half[pl.ds(there, part), :].astype(f32)
            grads[d][(slots + k) * part : (slots + k + 1) * part, :] = total.astype(bf16)
        spare = grads[d].shape[0] - 2 * slots * part
        grads[d][2 * slots * part :, :] = jnp.zeros((spare, LANES), bf16)
    row = table_row([[tab[which * slots + k] for k in range(slots)] for which in range(4)], slots)
    for ref in outs:
        ref[ref.shape[0] - 16 :, :] = row


def add_shares(parts, result, first):
    part = result.shape[1]
    for k in range(result.shape[0]):
        here = slice((first + k) * part, (first + k + 1) * part)
        result[k] = sum(ref[here, :].astype(f32) for ref in parts)


def output_kernel(dims, *refs):
    slots, n_row, n_col, n_tok = dims
    parts, refs = refs[1 : 1 + n_col], refs[1 + n_col :]
    outputs, tabs, results, (acc_out, acc_in, scalars, sems) = refs[:2], refs[2], refs[3:5], refs[5:]
    blk, share = acc_out.shape[-1], acc_out.shape[1]
    copy = decode_tables(parts, 2 * slots * share, tabs, scalars, sems.at[2])
    acc_out[...] = jnp.zeros(acc_out.shape, f32)
    acc_in[...] = jnp.zeros(acc_in.shape, f32)
    copy.wait()
    for c, ref in enumerate(parts):
        for k in range(slots):
            for first, which, acc in ((0, W2_OUT, acc_out), (slots, W1_ROW, acc_in)):
                at = scalars[c * 8, which * slots + k]
                here = slice((first + k) * share, (first + k + 1) * share)
                acc[at] = acc[at] + ref[here, :].astype(f32)
    stores = []
    for i, acc in enumerate((acc_out, acc_in)):
        for b in range(acc.shape[0]):
            results[i][:, b * blk : (b + 1) * blk] = acc[b].astype(bf16)
        stores.append(pltpu.make_async_copy(results[i], outputs[i], sems.at[i]))
        stores[-1].start()
    for c in stores:
        c.wait()


def grad_kernel(after, *refs):
    del after
    parts, gw1, gw2 = refs[:-2], refs[-2], refs[-1]
    slots, part, _ = gw1.shape
    add_shares(parts, gw1, 0)
    add_shares([ref for ref in parts if ref.shape[0] > slots * part], gw2, slots)


def shards(tokens, w1_blocks, w1_rows, w1_cols, w2_blocks, w2_hidden, w2_outs, grad_out):
    slots, blk = w1_blocks.shape[2], w1_blocks.shape[-1]
    rows = tokens.shape[0]
    n_row, n_col, n_tok = (lax.axis_size(a) for a in ("row", "col", "tok"))
    dims = (slots, n_row, n_col, n_tok)
    row_blocks = tokens.shape[1] // blk
    col_blocks = FF // n_col // blk
    share, part = rows // n_col, blk // n_tok
    w1 = w1_blocks.reshape(slots, blk, blk)
    w2 = w2_blocks.reshape(slots, blk, blk)
    tables = [t.reshape(slots) for t in (w1_rows, w1_cols, w2_hidden, w2_outs)]

    S = jax.ShapeDtypeStruct
    message = S((slots * rows + 16, blk), bf16)
    wide, narrow = S((slots, rows, blk), f32), S((slots, rows, blk), bf16)

    p_send = call(
        token_kernel,
        "take_tokens",
        TAKE_LIMIT,
        out_shape=message,
        in_specs=[HBM] * 6,
        out_specs=HBM,
        scratch_shapes=[
            pltpu.VMEM(tokens.shape, bf16),
            pltpu.VMEM((slots, blk, blk), bf16),
            pltpu.VMEM((slots * rows + 16, blk), bf16),
        ]
        + [pltpu.SMEM((slots,), jnp.int32)] * 4
        + [pltpu.SemaphoreType.DMA((7 + slots,))],
    )(*tables, tokens, w1)
    p_peers = [send(p_send, "row", d) for d in range(1, n_row)]

    b_send, taken, cot, hid, back, tab = call(
        cotangent_kernel,
        "take_cotangent",
        out_shape=(
            message,
            narrow,
            narrow,
            S((2 * slots + 1, rows, blk), f32),
            S((slots + 1, rows, blk), f32),
            S((6 * slots + col_blocks,), jnp.int32),
        ),
        in_specs=[SMEM] * 4 + [HBM, HBM] + [VMEM] * 2,
        out_specs=(VMEM,) * 5 + (SMEM,),
        scratch_shapes=[pltpu.SemaphoreType.DMA((2, slots))],
    )(*tables, tokens, grad_out, w1, w2)
    b_peers = [send(b_send, "row", d) for d in range(1, n_row)]

    outs = (S((2 * slots * share + 16, blk), bf16),) * n_col
    single = S((slots * part, blk), bf16)
    double = S((2 * slots * part + 32, blk), bf16)
    grads = tuple(double if n_tok % 2 == 1 or d % 2 == 0 else single for d in range(n_tok))
    half = S((max(1, n_tok // 2) * slots * part, blk), bf16)
    peer_rows = 8 * max(1, n_row - 1)
    active, hid, peer_tabs, grad2, half = call(
        functools.partial(hidden_kernel, dims),
        "hidden",
        out_shape=(
            narrow,
            S((2 * slots, rows, blk), f32),
            S((peer_rows, LANES), jnp.int32),
            S((slots, blk, blk), f32),
            half,
        ),
        in_specs=[SMEM] + [VMEM] * (n_row + 1),
        out_specs=(VMEM,) * 5,
        scratch_shapes=[pltpu.SMEM((peer_rows, LANES), jnp.int32), pltpu.SemaphoreType.DMA],
    )(tab, hid, *p_peers, cot)
    if n_tok % 2 == 0:
        half = lax.ppermute(half, "tok", [(i, i ^ 1) for i in range(n_tok)])
    out, slope = call(
        functools.partial(slope_kernel, dims),
        "slope",
        out_shape=(narrow, wide),
        in_specs=[SMEM] + [VMEM] * 3,
        out_specs=(VMEM,) * 2,
    )(tab, active, hid, w2)

    sent = call(
        functools.partial(back_kernel, dims),
        "back",
        out_shape=outs + grads,
        in_specs=[SMEM] * 2 + [VMEM] * (n_row + 6),
        out_specs=(VMEM,) * (n_col + n_tok),
        scratch_shapes=[
            pltpu.VMEM((slots, rows, blk), f32),
            pltpu.VMEM((slots, rows, blk), f32),
            pltpu.VMEM((slots, blk, blk), f32),
        ],
    )(tab, peer_tabs, back, *b_peers, slope, w1, out, taken, grad2, half)

    col_parts = [send(sent[d], "col", d) for d in range(n_col)]
    tok_parts = [send(sent[n_col + d], "tok", d) for d in range(n_tok)]

    result = S((share, row_blocks * blk), bf16)
    summed = S((slots, part, blk), f32)
    acc = pltpu.VMEM((row_blocks, share, blk), f32)
    output, grad_in, tabs = call(
        functools.partial(output_kernel, dims),
        "add_outputs",
        out_shape=(result, result, S((8 * n_col, LANES), jnp.int32)),
        in_specs=[ANY] + [VMEM] * n_col,
        out_specs=(HBM, HBM, VMEM),
        scratch_shapes=[pltpu.VMEM(result.shape, bf16)] * 2
        + [acc, acc, pltpu.SMEM((8 * n_col, LANES), jnp.int32), pltpu.SemaphoreType.DMA((3,))],
    )(tok_parts[n_tok // 2], *col_parts)
    gw1, gw2 = call(
        grad_kernel,
        "add_grads",
        out_shape=(summed, summed),
        in_specs=[ANY] + [VMEM] * n_tok,
        out_specs=(VMEM,) * 2,
    )(tabs, *tok_parts[::-1])
    return (output, grad_in, gw1.reshape(1, 1, slots, part, blk), gw2.reshape(1, 1, slots, part, blk))


def solution(mesh):
    placed = (
        P("tok", "row"),
        P("row", "col", None, None, None),
        P("row", "col", None),
        P("row", "col", None),
        P("row", "col", None, None, None),
        P("row", "col", None),
        P("row", "col", None),
        P("tok", "row"),
    )
    return jax.shard_map(
        shards,
        mesh=mesh,
        in_specs=placed,
        out_specs=(
            P(("tok", "col"), "row"),
            P(("tok", "col"), "row"),
            P("row", "col", None, "tok", None),
            P("row", "col", None, "tok", None),
        ),
        check_vma=False,
    )
```

```python
import functools
import math

import jax
import jax.numpy as jnp
from jax import lax
from jax.experimental import pallas as pl
from jax.experimental.pallas import tpu as pltpu
from jax.sharding import PartitionSpec as P

FF = 32768
LANES = 128
f32 = jnp.float32
bf16 = jnp.bfloat16
VMEM = pl.BlockSpec(memory_space=pltpu.VMEM)
SMEM = pl.BlockSpec(memory_space=pltpu.SMEM)
ANY = pl.BlockSpec(memory_space=pl.ANY)
HBM = pl.BlockSpec(memory_space=pltpu.HBM)
TAKE_LIMIT = 62 * 1024 * 1024
LIMIT = 32 * 1024 * 1024

W1_ROW, W1_COL, W2_HID, W2_OUT = range(4)


def call(kernel, name, limit=LIMIT, **kwargs):
    return pl.pallas_call(
        kernel,
        name=name,
        compiler_params=pltpu.CompilerParams(vmem_limit_bytes=limit),
        cost_estimate=pl.CostEstimate(flops=1 << 25, bytes_accessed=1 << 19, transcendentals=0),
        **kwargs,
    )


def dot(a, b, contract):
    return lax.dot_general(a, b, ((contract[:1], contract[1:]), ((), ())), preferred_element_type=f32)


def cdf(v):
    return 0.5 * (1.0 + lax.erf(v * math.sqrt(0.5)))


def partner(i, d, n):
    return i ^ d if n & (n - 1) == 0 else (i + d) % n


def target(axis, d):
    n = lax.axis_size(axis)
    me = lax.axis_index(axis)
    return jnp.bitwise_xor(me, d) if n & (n - 1) == 0 else lax.rem(me + d, n)


def send(x, axis, d):
    n = lax.axis_size(axis)
    return lax.ppermute(x, axis, [(i, partner(i, d, n)) for i in range(n)]) if d else x


def cut(value, refs, k, axis):
    share = value.shape[0] // len(refs)
    for d, ref in enumerate(refs):
        begin = pl.multiple_of(target(axis, d) * share, share)
        ref[k * share : (k + 1) * share, :] = value[pl.ds(begin, share), :].astype(ref.dtype)


def table_row(tables, slots):
    lane = lax.broadcasted_iota(jnp.int32, (16, LANES), 1)
    row = jnp.zeros((16, LANES), f32)
    for which, table in enumerate(tables):
        for k in range(slots):
            row = jnp.where(lane == which * slots + k, table[k].astype(f32), row)
    return row.astype(bf16)


def numbers(ref, rows):
    return ref[rows : rows + 16, :].astype(f32)[:8].astype(jnp.int32)


def token_kernel(t0, t1, t2, t3, tokens, w1, message, tokens_v, w_v, sent, c0, c1, c2, c3, sems):
    slots, blk, _ = w_v.shape
    rows = tokens_v.shape[0]
    tables = (c0, c1, c2, c3)
    loads = [pltpu.make_async_copy(t, c, sems.at[i]) for i, (t, c) in enumerate(zip((t0, t1, t2, t3), tables))]
    loads.append(pltpu.make_async_copy(tokens, tokens_v, sems.at[4]))
    loads.append(pltpu.make_async_copy(w1, w_v, sems.at[5]))
    stores = []

    def store(begin, size):
        here = pl.ds(begin, size)
        stores.append(pltpu.make_async_copy(sent.at[here], message.at[here], sems.at[6 + len(stores)]))
        stores[-1].start()

    for c in loads:
        c.start()
    for c in loads[:4]:
        c.wait()
    sent[slots * rows :, :] = table_row(tables, slots)
    store(slots * rows, 16)
    for c in loads[4:]:
        c.wait()
    for k in range(slots):
        here = pl.ds(pl.multiple_of(c0[k] * blk, blk), blk)
        sent[k * rows : (k + 1) * rows, :] = dot(tokens_v[:, here], w_v[k], (1, 0)).astype(bf16)
        store(k * rows, rows)
    for c in stores:
        c.wait()


def first_places(tab):
    return tab[:8]


def places_of(tab, blocks, slots):
    place = lax.broadcasted_iota(jnp.int32, (2 * slots, LANES), 0)
    same = tab[8 : 8 + 2 * slots] == blocks[:1]
    return jnp.min(jnp.where(same, place, 2 * slots), axis=0, keepdims=True)


def start_taking(source, table, taken, sems):
    slots, _, blk = taken.shape
    copies = []
    for k in range(slots):
        begin = pl.multiple_of(table[k] * blk, blk)
        copies.append(pltpu.make_async_copy(source.at[:, pl.ds(begin, blk)], taken.at[k], sems.at[k]))
        copies[-1].start()
    return copies


def cotangent_kernel(
    c0, c1, c2, c3, tokens, grad_out, w1, w2, message, taken, cot, hid, back, tab, row, place_of, sems
):
    slots, rows, blk = cot.shape
    copies = start_taking(grad_out, c3, cot, sems.at[0])
    copies_t = start_taking(tokens, c0, taken, sems.at[1])

    @pl.loop(0, place_of.shape[0])
    def _(block):
        place_of[block] = 2 * slots

    lane = lax.broadcasted_iota(jnp.int32, (8, LANES), 1)
    firsts = jnp.zeros((8, LANES), jnp.int32)
    for j in range(2 * slots):
        block = c1[j] if j < slots else c2[j - slots]
        place = jnp.minimum(place_of[block], j)
        place_of[block] = place
        firsts = jnp.where(lane == j, place, firsts)
        tab[8 + j : 9 + j, :] = jnp.full((1, LANES), block, jnp.int32)
    tab[:8] = firsts
    row[...] = table_row((c0, c1, c2, c3), slots)
    hid[...] = jnp.zeros(hid.shape, f32)
    back[...] = jnp.zeros(back.shape, f32)
    message[slots * rows :, :] = jnp.zeros((16, blk), bf16)
    for k in range(slots):
        copies[k].wait()
        value = dot(cot[k], w2[k], (1, 1))
        message[k * rows : (k + 1) * rows, :] = value.astype(bf16)
        at = jnp.minimum(place_of[c2[k]], slots)
        back[at] = back[at] + value
    for k in range(slots):
        copies_t[k].wait()
        at = place_of[c1[k]]
        hid[at] = hid[at] + dot(taken[k], w1[k], (1, 0))


def add_peers(acc, own, places, which, peers, slots):
    count, rows, _ = acc.shape
    for j in range(count):
        acc[j] = own[j]
    for place, ref in zip(places, peers):
        for k in range(slots):
            at = place[0, which * slots + k]

            @pl.when(at < count)
            def _():
                acc[at] = acc[at] + ref[k * rows : (k + 1) * rows, :].astype(f32)


def hidden_kernel(dims, tab, own, *refs):
    slots, n_row, n_col, n_tok = dims
    peers, refs = refs[: n_row - 1], refs[n_row - 1 :]
    cot, active, hid, places, grad, half = refs
    part = grad.shape[1] // n_tok
    other = 1 - lax.rem(lax.axis_index("tok"), 2)
    found = [places_of(tab, numbers(ref, slots * cot.shape[1]), slots) for ref in peers]
    places[...] = jnp.zeros(places.shape, jnp.int32)
    for i, place in enumerate(found):
        places[8 * i : 8 * i + 8] = jnp.broadcast_to(place, (8, LANES))
    add_peers(hid, own, found, W1_COL, peers, slots)
    firsts = first_places(tab)
    for k in range(slots):
        h = hid[firsts[0, slots + k]]
        active[k] = (h * cdf(h)).astype(bf16)
        grad[k] = dot(active[k], cot[k], (0, 0))
        for j in range(n_tok // 2):
            begin = pl.multiple_of((2 * j + other) * part, part)
            here = (j * slots + k) * part
            half[here : here + part, :] = grad[k, pl.ds(begin, part), :].astype(bf16)


def slope_kernel(dims, tab, active, hid, w2, out, slope):
    slots = dims[0]
    firsts = first_places(tab)
    for k in range(slots):
        out[k] = dot(active[k], w2[k], (1, 0)).astype(bf16)
    for k in range(slots):
        h = hid[firsts[0, k]]
        slope[k] = cdf(h) + h * jnp.exp(-0.5 * h * h) * (1.0 / math.sqrt(2.0 * math.pi))


def back_kernel(dims, tab, row, places, own, *refs):
    slots, n_row, n_col, n_tok = dims
    peers, refs = refs[: n_row - 1], refs[n_row - 1 :]
    slope, w1, out, taken, grad2, half = refs[:6]
    refs = refs[6:]
    outs, refs = refs[:n_col], refs[n_col:]
    grads, (acc, value, grad) = refs[:n_tok], refs[n_tok:]
    part = grad.shape[1] // n_tok
    paired = n_tok % 2 == 0
    found = [places[8 * i : 8 * i + 8] for i in range(len(peers))]
    add_peers(acc, own, found, W2_HID, peers, slots)
    firsts = first_places(tab)
    for k in range(slots):
        g = (acc[firsts[0, k]] * slope[k]).astype(bf16)
        grad[k] = dot(taken[k], g, (0, 0))
        cut(grad.at[k], grads, k, "tok")
        value[k] = dot(g, w1[k], (1, 1))
        cut(value.at[k], outs, slots + k, "col")
    for k in range(slots):
        cut(out.at[k], outs, k, "col")
    for d in range(0, n_tok, 2 if paired else 1):
        to = target("tok", d)
        begin = pl.multiple_of(to * part, part)
        for k in range(slots):
            total = grad2[k, pl.ds(begin, part), :]
            if paired:
                there = pl.multiple_of((lax.div(to, 2) * slots + k) * part, part)
                total = total + half[pl.ds(there, part), :].astype(f32)
            grads[d][(slots + k) * part : (slots + k + 1) * part, :] = total.astype(bf16)
        spare = grads[d].shape[0] - 2 * slots * part
        grads[d][2 * slots * part :, :] = jnp.zeros((spare, LANES), bf16)
    for ref in outs:
        ref[ref.shape[0] - 16 :, :] = row[...]


def add_shares(parts, result, first):
    part = result.shape[1]
    for k in range(result.shape[0]):
        here = slice((first + k) * part, (first + k + 1) * part)
        result[k] = sum(ref[here, :].astype(f32) for ref in parts)


def output_kernel(dims, *refs):
    slots, n_row, n_col, n_tok = dims
    parts, refs = refs[1 : 1 + n_col], refs[1 + n_col :]
    outputs, last, results, (acc_out, acc_in, sems) = refs[:2], refs[2], refs[3:5], refs[5:]
    blk, share = acc_out.shape[-1], acc_out.shape[1]
    acc_out[...] = jnp.zeros(acc_out.shape, f32)
    acc_in[...] = jnp.zeros(acc_in.shape, f32)
    for ref in parts:
        blocks = numbers(ref, 2 * slots * share)
        last[...] = blocks
        for k in range(slots):
            for first, which, acc in ((0, W2_OUT, acc_out), (slots, W1_ROW, acc_in)):
                at = blocks[0, which * slots + k]
                here = slice((first + k) * share, (first + k + 1) * share)
                acc[at] = acc[at] + ref[here, :].astype(f32)
    stores = []
    for i, acc in enumerate((acc_out, acc_in)):
        for b in range(acc.shape[0]):
            results[i][:, b * blk : (b + 1) * blk] = acc[b].astype(bf16)
        stores.append(pltpu.make_async_copy(results[i], outputs[i], sems.at[i]))
        stores[-1].start()
    for c in stores:
        c.wait()


def grad_kernel(after, *refs):
    del after
    parts, gw1, gw2 = refs[:-2], refs[-2], refs[-1]
    slots, part, _ = gw1.shape
    add_shares(parts, gw1, 0)
    add_shares([ref for ref in parts if ref.shape[0] > slots * part], gw2, slots)


def shards(tokens, w1_blocks, w1_rows, w1_cols, w2_blocks, w2_hidden, w2_outs, grad_out):
    slots, blk = w1_blocks.shape[2], w1_blocks.shape[-1]
    rows = tokens.shape[0]
    n_row, n_col, n_tok = (lax.axis_size(a) for a in ("row", "col", "tok"))
    dims = (slots, n_row, n_col, n_tok)
    row_blocks = tokens.shape[1] // blk
    col_blocks = FF // n_col // blk
    share, part = rows // n_col, blk // n_tok
    w1 = w1_blocks.reshape(slots, blk, blk)
    w2 = w2_blocks.reshape(slots, blk, blk)
    tables = [t.reshape(slots) for t in (w1_rows, w1_cols, w2_hidden, w2_outs)]

    S = jax.ShapeDtypeStruct
    message = S((slots * rows + 16, blk), bf16)
    wide, narrow = S((slots, rows, blk), f32), S((slots, rows, blk), bf16)

    p_send = call(
        token_kernel,
        "take_tokens",
        TAKE_LIMIT,
        out_shape=message,
        in_specs=[HBM] * 6,
        out_specs=HBM,
        scratch_shapes=[
            pltpu.VMEM(tokens.shape, bf16),
            pltpu.VMEM((slots, blk, blk), bf16),
            pltpu.VMEM((slots * rows + 16, blk), bf16),
        ]
        + [pltpu.SMEM((slots,), jnp.int32)] * 4
        + [pltpu.SemaphoreType.DMA((7 + slots,))],
    )(*tables, tokens, w1)
    p_peers = [send(p_send, "row", d) for d in range(1, n_row)]

    b_send, taken, cot, hid, back, tab, row = call(
        cotangent_kernel,
        "take_cotangent",
        out_shape=(
            message,
            narrow,
            narrow,
            S((2 * slots, rows, blk), f32),
            S((slots + 1, rows, blk), f32),
            S((8 + 2 * slots, LANES), jnp.int32),
            S((16, LANES), bf16),
        ),
        in_specs=[SMEM] * 4 + [HBM, HBM] + [VMEM] * 2,
        out_specs=(VMEM,) * 7,
        scratch_shapes=[pltpu.SMEM((col_blocks,), jnp.int32), pltpu.SemaphoreType.DMA((2, slots))],
    )(*tables, tokens, grad_out, w1, w2)
    b_peers = [send(b_send, "row", d) for d in range(1, n_row)]

    outs = (S((2 * slots * share + 16, blk), bf16),) * n_col
    single = S((slots * part, blk), bf16)
    double = S((2 * slots * part + 32, blk), bf16)
    grads = tuple(double if n_tok % 2 == 1 or d % 2 == 0 else single for d in range(n_tok))
    half = S((max(1, n_tok // 2) * slots * part, blk), bf16)
    peer_rows = 8 * max(1, n_row - 1)
    active, hid, places, grad2, half = call(
        functools.partial(hidden_kernel, dims),
        "hidden",
        out_shape=(
            narrow,
            S((2 * slots, rows, blk), f32),
            S((peer_rows, LANES), jnp.int32),
            S((slots, blk, blk), f32),
            half,
        ),
        in_specs=[VMEM] * (n_row + 2),
        out_specs=(VMEM,) * 5,
    )(tab, hid, *p_peers, cot)
    if n_tok % 2 == 0:
        half = lax.ppermute(half, "tok", [(i, i ^ 1) for i in range(n_tok)])
    out, slope = call(
        functools.partial(slope_kernel, dims),
        "slope",
        out_shape=(narrow, wide),
        in_specs=[VMEM] * 4,
        out_specs=(VMEM,) * 2,
    )(tab, active, hid, w2)

    sent = call(
        functools.partial(back_kernel, dims),
        "back",
        out_shape=outs + grads,
        in_specs=[VMEM] * (n_row + 9),
        out_specs=(VMEM,) * (n_col + n_tok),
        scratch_shapes=[
            pltpu.VMEM((slots, rows, blk), f32),
            pltpu.VMEM((slots, rows, blk), f32),
            pltpu.VMEM((slots, blk, blk), f32),
        ],
    )(tab, row, places, back, *b_peers, slope, w1, out, taken, grad2, half)

    col_parts = [send(sent[d], "col", d) for d in range(n_col)]
    tok_parts = [send(sent[n_col + d], "tok", d) for d in range(n_tok)]

    result = S((share, row_blocks * blk), bf16)
    summed = S((slots, part, blk), f32)
    acc = pltpu.VMEM((row_blocks, share, blk), f32)
    output, grad_in, last = call(
        functools.partial(output_kernel, dims),
        "add_outputs",
        out_shape=(result, result, S((8, LANES), jnp.int32)),
        in_specs=[ANY] + [VMEM] * n_col,
        out_specs=(HBM, HBM, VMEM),
        scratch_shapes=[pltpu.VMEM(result.shape, bf16)] * 2
        + [acc, acc, pltpu.SemaphoreType.DMA((2,))],
    )(tok_parts[n_tok // 2], *col_parts)
    gw1, gw2 = call(
        grad_kernel,
        "add_grads",
        out_shape=(summed, summed),
        in_specs=[ANY] + [VMEM] * n_tok,
        out_specs=(VMEM,) * 2,
    )(last, *tok_parts[::-1])
    return (output, grad_in, gw1.reshape(1, 1, slots, part, blk), gw2.reshape(1, 1, slots, part, blk))


def solution(mesh):
    placed = (
        P("tok", "row"),
        P("row", "col", None, None, None),
        P("row", "col", None),
        P("row", "col", None),
        P("row", "col", None, None, None),
        P("row", "col", None),
        P("row", "col", None),
        P("tok", "row"),
    )
    return jax.shard_map(
        shards,
        mesh=mesh,
        in_specs=placed,
        out_specs=(
            P(("tok", "col"), "row"),
            P(("tok", "col"), "row"),
            P("row", "col", None, "tok", None),
            P("row", "col", None, "tok", None),
        ),
        check_vma=False,
    )
```

```python
import functools
import math

import jax
import jax.numpy as jnp
from jax import lax
from jax.experimental import pallas as pl
from jax.experimental.pallas import tpu as pltpu
from jax.sharding import PartitionSpec as P

FF = 32768
LANES = 128
f32 = jnp.float32
bf16 = jnp.bfloat16
VMEM = pl.BlockSpec(memory_space=pltpu.VMEM)
SMEM = pl.BlockSpec(memory_space=pltpu.SMEM)
ANY = pl.BlockSpec(memory_space=pl.ANY)
HBM = pl.BlockSpec(memory_space=pltpu.HBM)
TAKE_LIMIT = 62 * 1024 * 1024
LIMIT = 32 * 1024 * 1024

W1_ROW, W1_COL, W2_HID, W2_OUT = range(4)


def call(kernel, name, limit=LIMIT, **kwargs):
    return pl.pallas_call(
        kernel,
        name=name,
        compiler_params=pltpu.CompilerParams(vmem_limit_bytes=limit),
        cost_estimate=pl.CostEstimate(flops=1 << 25, bytes_accessed=1 << 19, transcendentals=0),
        **kwargs,
    )


def dot(a, b, contract):
    return lax.dot_general(a, b, ((contract[:1], contract[1:]), ((), ())), preferred_element_type=f32)


def cdf(v):
    return 0.5 * (1.0 + lax.erf(v * math.sqrt(0.5)))


def partner(i, d, n):
    return i ^ d if n & (n - 1) == 0 else (i + d) % n


def target(axis, d):
    n = lax.axis_size(axis)
    me = lax.axis_index(axis)
    return jnp.bitwise_xor(me, d) if n & (n - 1) == 0 else lax.rem(me + d, n)


def send(x, axis, d):
    n = lax.axis_size(axis)
    return lax.ppermute(x, axis, [(i, partner(i, d, n)) for i in range(n)]) if d else x


def cut(value, refs, k, axis):
    share = value.shape[0] // len(refs)
    for d, ref in enumerate(refs):
        begin = pl.multiple_of(target(axis, d) * share, share)
        ref[k * share : (k + 1) * share, :] = value[pl.ds(begin, share), :].astype(ref.dtype)


def table_row(tables, slots):
    lane = lax.broadcasted_iota(jnp.int32, (16, LANES), 1)
    row = jnp.zeros((16, LANES), f32)
    for which, table in enumerate(tables):
        for k in range(slots):
            row = jnp.where(lane == which * slots + k, table[k].astype(f32), row)
    return row.astype(bf16)


def numbers(ref, rows):
    return ref[rows : rows + 16, :].astype(f32)[:8].astype(jnp.int32)


def token_kernel(t0, t1, t2, t3, tokens, w1, message, tokens_v, w_v, sent, c0, c1, c2, c3, sems):
    slots, blk, _ = w_v.shape
    rows = tokens_v.shape[0]
    tables = (c0, c1, c2, c3)
    loads = [pltpu.make_async_copy(t, c, sems.at[i]) for i, (t, c) in enumerate(zip((t0, t1, t2, t3), tables))]
    loads.append(pltpu.make_async_copy(tokens, tokens_v, sems.at[4]))
    loads.append(pltpu.make_async_copy(w1, w_v, sems.at[5]))
    stores = []

    def store(begin, size):
        here = pl.ds(begin, size)
        stores.append(pltpu.make_async_copy(sent.at[here], message.at[here], sems.at[6 + len(stores)]))
        stores[-1].start()

    for c in loads:
        c.start()
    for c in loads[:4]:
        c.wait()
    sent[slots * rows :, :] = table_row(tables, slots)
    store(slots * rows, 16)
    for c in loads[4:]:
        c.wait()
    for k in range(slots):
        here = pl.ds(pl.multiple_of(c0[k] * blk, blk), blk)
        sent[k * rows : (k + 1) * rows, :] = dot(tokens_v[:, here], w_v[k], (1, 0)).astype(bf16)
        store(k * rows, rows)
    for c in stores:
        c.wait()


def first_places(tab):
    return tab[:8]


def places_of(tab, blocks, slots):
    place = lax.broadcasted_iota(jnp.int32, (2 * slots, LANES), 0)
    same = tab[8 : 8 + 2 * slots] == blocks[:1]
    return jnp.min(jnp.where(same, place, 2 * slots), axis=0, keepdims=True)


def start_taking(source, table, taken, sems):
    slots, _, blk = taken.shape
    copies = []
    for k in range(slots):
        begin = pl.multiple_of(table[k] * blk, blk)
        copies.append(pltpu.make_async_copy(source.at[:, pl.ds(begin, blk)], taken.at[k], sems.at[k]))
        copies[-1].start()
    return copies


def cotangent_kernel(
    c0, c1, c2, c3, tokens, grad_out, w1, w2, message, taken_t, cot, hid, back, tab, row, place_of, taken, sems
):
    slots, rows, blk = cot.shape
    copies = start_taking(grad_out, c3, cot, sems.at[0])
    copies_t = start_taking(tokens, c0, taken, sems.at[1])

    @pl.loop(0, place_of.shape[0])
    def _(block):
        place_of[block] = 2 * slots

    lane = lax.broadcasted_iota(jnp.int32, (8, LANES), 1)
    firsts = jnp.zeros((8, LANES), jnp.int32)
    for j in range(2 * slots):
        block = c1[j] if j < slots else c2[j - slots]
        place = jnp.minimum(place_of[block], j)
        place_of[block] = place
        firsts = jnp.where(lane == j, place, firsts)
        tab[8 + j : 9 + j, :] = jnp.full((1, LANES), block, jnp.int32)
    tab[:8] = firsts
    row[...] = table_row((c0, c1, c2, c3), slots)
    hid[...] = jnp.zeros(hid.shape, f32)
    back[...] = jnp.zeros(back.shape, f32)
    message[slots * rows :, :] = jnp.zeros((16, blk), bf16)
    for k in range(slots):
        copies[k].wait()
        value = dot(cot[k], w2[k], (1, 1))
        message[k * rows : (k + 1) * rows, :] = value.astype(bf16)
        at = jnp.minimum(place_of[c2[k]], slots)
        back[at] = back[at] + value
    for k in range(slots):
        copies_t[k].wait()
        at = place_of[c1[k]]
        hid[at] = hid[at] + dot(taken[k], w1[k], (1, 0))
        taken_t[k] = taken[k].T


def add_peers(acc, own, numbers_at, peers, slots):
    count, rows, _ = acc.shape
    for j in range(count):
        acc[j] = own[j]
    for numbers_of, ref in zip(numbers_at, peers):
        for k, at in enumerate(numbers_of):

            @pl.when(at < count)
            def _():
                acc[at] = acc[at] + ref[k * rows : (k + 1) * rows, :].astype(f32)


def hidden_kernel(dims, tab, own, *refs):
    slots, n_row, n_col, n_tok = dims
    peers, refs = refs[: n_row - 1], refs[n_row - 1 :]
    cot, active, hid, places, grad, half = refs
    part = grad.shape[1] // n_tok
    other = 1 - lax.rem(lax.axis_index("tok"), 2)
    found = [places_of(tab, numbers(ref, slots * cot.shape[1]), slots) for ref in peers]
    places[...] = jnp.zeros(places.shape, jnp.int32)
    for i, place in enumerate(found):
        places[8 * i : 8 * i + 8] = jnp.broadcast_to(place, (8, LANES))
    at = [[place[0, W1_COL * slots + k] for k in range(slots)] for place in found]
    firsts = first_places(tab)
    firsts = [firsts[0, slots + k] for k in range(slots)]
    add_peers(hid, own, at, peers, slots)
    for k in range(slots):
        h = hid[firsts[k]]
        active[k] = (h * cdf(h)).astype(bf16)
        grad[k] = dot(active[k], cot[k], (0, 0))
        for j in range(n_tok // 2):
            begin = pl.multiple_of((2 * j + other) * part, part)
            here = (j * slots + k) * part
            half[here : here + part, :] = grad[k, pl.ds(begin, part), :].astype(bf16)


def slope_kernel(dims, tab, active, hid, w2, out, slope):
    slots = dims[0]
    firsts = first_places(tab)
    for k in range(slots):
        out[k] = dot(active[k], w2[k], (1, 0)).astype(bf16)
    for k in range(slots):
        h = hid[firsts[0, k]]
        slope[k] = cdf(h) + h * jnp.exp(-0.5 * h * h) * (1.0 / math.sqrt(2.0 * math.pi))


def back_kernel(dims, tab, row, places, own, *refs):
    slots, n_row, n_col, n_tok = dims
    peers, refs = refs[: n_row - 1], refs[n_row - 1 :]
    slope, w1, out, taken_t, grad2, half = refs[:6]
    refs = refs[6:]
    outs, refs = refs[:n_col], refs[n_col:]
    grads, (acc, value, grad) = refs[:n_tok], refs[n_tok:]
    part = grad.shape[1] // n_tok
    paired = n_tok % 2 == 0
    found = [places[8 * i : 8 * i + 8] for i in range(len(peers))]
    at = [[place[0, W2_HID * slots + k] for k in range(slots)] for place in found]
    firsts = first_places(tab)
    firsts = [firsts[0, k] for k in range(slots)]
    add_peers(acc, own, at, peers, slots)
    for k in range(slots):
        g = (acc[firsts[k]] * slope[k]).astype(bf16)
        grad[k] = dot(taken_t[k], g, (1, 0))
        cut(grad.at[k], grads, k, "tok")
        value[k] = dot(g, w1[k], (1, 1))
        cut(value.at[k], outs, slots + k, "col")
    for k in range(slots):
        cut(out.at[k], outs, k, "col")
    for d in range(0, n_tok, 2 if paired else 1):
        to = target("tok", d)
        begin = pl.multiple_of(to * part, part)
        for k in range(slots):
            total = grad2[k, pl.ds(begin, part), :]
            if paired:
                there = pl.multiple_of((lax.div(to, 2) * slots + k) * part, part)
                total = total + half[pl.ds(there, part), :].astype(f32)
            grads[d][(slots + k) * part : (slots + k + 1) * part, :] = total.astype(bf16)
        spare = grads[d].shape[0] - 2 * slots * part
        grads[d][2 * slots * part :, :] = jnp.zeros((spare, LANES), bf16)
    for ref in outs:
        ref[ref.shape[0] - 16 :, :] = row[...]


def add_shares(parts, result, first):
    part = result.shape[1]
    for k in range(result.shape[0]):
        here = slice((first + k) * part, (first + k + 1) * part)
        result[k] = sum(ref[here, :].astype(f32) for ref in parts)


def output_kernel(dims, *refs):
    slots, n_row, n_col, n_tok = dims
    parts, refs = refs[1 : 1 + n_col], refs[1 + n_col :]
    outputs, last, results, (acc_out, acc_in, sems) = refs[:2], refs[2], refs[3:5], refs[5:]
    blk, share = acc_out.shape[-1], acc_out.shape[1]
    acc_out[...] = jnp.zeros(acc_out.shape, f32)
    acc_in[...] = jnp.zeros(acc_in.shape, f32)
    for ref in parts:
        blocks = numbers(ref, 2 * slots * share)
        last[...] = blocks
        for k in range(slots):
            for first, which, acc in ((0, W2_OUT, acc_out), (slots, W1_ROW, acc_in)):
                at = blocks[0, which * slots + k]
                here = slice((first + k) * share, (first + k + 1) * share)
                acc[at] = acc[at] + ref[here, :].astype(f32)
    stores = []
    for i, acc in enumerate((acc_out, acc_in)):
        for b in range(acc.shape[0]):
            results[i][:, b * blk : (b + 1) * blk] = acc[b].astype(bf16)
        stores.append(pltpu.make_async_copy(results[i], outputs[i], sems.at[i]))
        stores[-1].start()
    for c in stores:
        c.wait()


def grad_kernel(after, *refs):
    del after
    parts, gw1, gw2 = refs[:-2], refs[-2], refs[-1]
    slots, part, _ = gw1.shape
    add_shares(parts, gw1, 0)
    add_shares([ref for ref in parts if ref.shape[0] > slots * part], gw2, slots)


def shards(tokens, w1_blocks, w1_rows, w1_cols, w2_blocks, w2_hidden, w2_outs, grad_out):
    slots, blk = w1_blocks.shape[2], w1_blocks.shape[-1]
    rows = tokens.shape[0]
    n_row, n_col, n_tok = (lax.axis_size(a) for a in ("row", "col", "tok"))
    dims = (slots, n_row, n_col, n_tok)
    row_blocks = tokens.shape[1] // blk
    col_blocks = FF // n_col // blk
    share, part = rows // n_col, blk // n_tok
    w1 = w1_blocks.reshape(slots, blk, blk)
    w2 = w2_blocks.reshape(slots, blk, blk)
    tables = [t.reshape(slots) for t in (w1_rows, w1_cols, w2_hidden, w2_outs)]

    S = jax.ShapeDtypeStruct
    message = S((slots * rows + 16, blk), bf16)
    wide, narrow = S((slots, rows, blk), f32), S((slots, rows, blk), bf16)

    p_send = call(
        token_kernel,
        "take_tokens",
        TAKE_LIMIT,
        out_shape=message,
        in_specs=[HBM] * 6,
        out_specs=HBM,
        scratch_shapes=[
            pltpu.VMEM(tokens.shape, bf16),
            pltpu.VMEM((slots, blk, blk), bf16),
            pltpu.VMEM((slots * rows + 16, blk), bf16),
        ]
        + [pltpu.SMEM((slots,), jnp.int32)] * 4
        + [pltpu.SemaphoreType.DMA((7 + slots,))],
    )(*tables, tokens, w1)
    p_peers = [send(p_send, "row", d) for d in range(1, n_row)]

    b_send, taken_t, cot, hid, back, tab, row = call(
        cotangent_kernel,
        "take_cotangent",
        out_shape=(
            message,
            S((slots, blk, rows), bf16),
            narrow,
            S((2 * slots, rows, blk), f32),
            S((slots + 1, rows, blk), f32),
            S((8 + 2 * slots, LANES), jnp.int32),
            S((16, LANES), bf16),
        ),
        in_specs=[SMEM] * 4 + [HBM, HBM] + [VMEM] * 2,
        out_specs=(VMEM,) * 7,
        scratch_shapes=[
            pltpu.SMEM((col_blocks,), jnp.int32),
            pltpu.VMEM((slots, rows, blk), bf16),
            pltpu.SemaphoreType.DMA((2, slots)),
        ],
    )(*tables, tokens, grad_out, w1, w2)
    b_peers = [send(b_send, "row", d) for d in range(1, n_row)]

    outs = (S((2 * slots * share + 16, blk), bf16),) * n_col
    single = S((slots * part, blk), bf16)
    double = S((2 * slots * part + 32, blk), bf16)
    grads = tuple(double if n_tok % 2 == 1 or d % 2 == 0 else single for d in range(n_tok))
    half = S((max(1, n_tok // 2) * slots * part, blk), bf16)
    peer_rows = 8 * max(1, n_row - 1)
    active, hid, places, grad2, half = call(
        functools.partial(hidden_kernel, dims),
        "hidden",
        out_shape=(
            narrow,
            S((2 * slots, rows, blk), f32),
            S((peer_rows, LANES), jnp.int32),
            S((slots, blk, blk), f32),
            half,
        ),
        in_specs=[VMEM] * (n_row + 2),
        out_specs=(VMEM,) * 5,
    )(tab, hid, *p_peers, cot)
    if n_tok % 2 == 0:
        half = lax.ppermute(half, "tok", [(i, i ^ 1) for i in range(n_tok)])
    out, slope = call(
        functools.partial(slope_kernel, dims),
        "slope",
        out_shape=(narrow, wide),
        in_specs=[VMEM] * 4,
        out_specs=(VMEM,) * 2,
    )(tab, active, hid, w2)

    sent = call(
        functools.partial(back_kernel, dims),
        "back",
        out_shape=outs + grads,
        in_specs=[VMEM] * (n_row + 9),
        out_specs=(VMEM,) * (n_col + n_tok),
        scratch_shapes=[
            pltpu.VMEM((slots, rows, blk), f32),
            pltpu.VMEM((slots, rows, blk), f32),
            pltpu.VMEM((slots, blk, blk), f32),
        ],
    )(tab, row, places, back, *b_peers, slope, w1, out, taken_t, grad2, half)

    col_parts = [send(sent[d], "col", d) for d in [0] + list(range(2, n_col)) + [1][: n_col - 1]]
    tok_parts = [send(sent[n_col + d], "tok", d) for d in range(n_tok)]

    result = S((share, row_blocks * blk), bf16)
    summed = S((slots, part, blk), f32)
    acc = pltpu.VMEM((row_blocks, share, blk), f32)
    output, grad_in, last = call(
        functools.partial(output_kernel, dims),
        "add_outputs",
        out_shape=(result, result, S((8, LANES), jnp.int32)),
        in_specs=[ANY] + [VMEM] * n_col,
        out_specs=(HBM, HBM, VMEM),
        scratch_shapes=[pltpu.VMEM(result.shape, bf16)] * 2
        + [acc, acc, pltpu.SemaphoreType.DMA((2,))],
    )(tok_parts[n_tok // 2], *col_parts)
    gw1, gw2 = call(
        grad_kernel,
        "add_grads",
        out_shape=(summed, summed),
        in_specs=[ANY] + [VMEM] * n_tok,
        out_specs=(VMEM,) * 2,
    )(last, *tok_parts[::-1])
    return (output, grad_in, gw1.reshape(1, 1, slots, part, blk), gw2.reshape(1, 1, slots, part, blk))


def solution(mesh):
    placed = (
        P("tok", "row"),
        P("row", "col", None, None, None),
        P("row", "col", None),
        P("row", "col", None),
        P("row", "col", None, None, None),
        P("row", "col", None),
        P("row", "col", None),
        P("tok", "row"),
    )
    return jax.shard_map(
        shards,
        mesh=mesh,
        in_specs=placed,
        out_specs=(
            P(("tok", "col"), "row"),
            P(("tok", "col"), "row"),
            P("row", "col", None, "tok", None),
            P("row", "col", None, "tok", None),
        ),
        check_vma=False,
    )
```

```python
import functools
import math

import jax
import jax.numpy as jnp
from jax import lax
from jax.experimental import pallas as pl
from jax.experimental.pallas import tpu as pltpu
from jax.sharding import PartitionSpec as P

FF = 32768
LANES = 128
f32 = jnp.float32
bf16 = jnp.bfloat16
VMEM = pl.BlockSpec(memory_space=pltpu.VMEM)
SMEM = pl.BlockSpec(memory_space=pltpu.SMEM)
ANY = pl.BlockSpec(memory_space=pl.ANY)
HBM = pl.BlockSpec(memory_space=pltpu.HBM)
TAKE_LIMIT = 62 * 1024 * 1024
LIMIT = 32 * 1024 * 1024

W1_ROW, W1_COL, W2_HID, W2_OUT = range(4)


def call(kernel, name, limit=LIMIT, **kwargs):
    return pl.pallas_call(
        kernel,
        name=name,
        compiler_params=pltpu.CompilerParams(vmem_limit_bytes=limit),
        cost_estimate=pl.CostEstimate(flops=1 << 25, bytes_accessed=1 << 19, transcendentals=0),
        **kwargs,
    )


def dot(a, b, contract):
    return lax.dot_general(a, b, ((contract[:1], contract[1:]), ((), ())), preferred_element_type=f32)


def cdf(v):
    return 0.5 * (1.0 + lax.erf(v * math.sqrt(0.5)))


def partner(i, d, n):
    return i ^ d if n & (n - 1) == 0 else (i + d) % n


def target(axis, d):
    n = lax.axis_size(axis)
    me = lax.axis_index(axis)
    return jnp.bitwise_xor(me, d) if n & (n - 1) == 0 else lax.rem(me + d, n)


def send(x, axis, d):
    n = lax.axis_size(axis)
    return lax.ppermute(x, axis, [(i, partner(i, d, n)) for i in range(n)]) if d else x


def cut(value, refs, k, axis):
    share = value.shape[0] // len(refs)
    for d, ref in enumerate(refs):
        begin = pl.multiple_of(target(axis, d) * share, share)
        ref[k * share : (k + 1) * share, :] = value[pl.ds(begin, share), :].astype(ref.dtype)


def table_row(tables, slots):
    lane = lax.broadcasted_iota(jnp.int32, (16, LANES), 1)
    row = jnp.zeros((16, LANES), f32)
    for which, table in enumerate(tables):
        for k in range(slots):
            row = jnp.where(lane == which * slots + k, table[k].astype(f32), row)
    return row.astype(bf16)


def numbers(ref, rows):
    return ref[rows : rows + 16, :].astype(f32)[:8].astype(jnp.int32)


def token_kernel(t0, t1, t2, t3, tokens, w1, message, tokens_v, w_v, sent, c0, c1, c2, c3, sems):
    slots, blk, _ = w_v.shape
    rows = tokens_v.shape[0]
    tables = (c0, c1, c2, c3)
    loads = [pltpu.make_async_copy(t, c, sems.at[i]) for i, (t, c) in enumerate(zip((t0, t1, t2, t3), tables))]
    loads.append(pltpu.make_async_copy(tokens, tokens_v, sems.at[4]))
    loads.append(pltpu.make_async_copy(w1, w_v, sems.at[5]))
    stores = []

    def store(begin, size):
        here = pl.ds(begin, size)
        stores.append(pltpu.make_async_copy(sent.at[here], message.at[here], sems.at[6 + len(stores)]))
        stores[-1].start()

    for c in loads:
        c.start()
    for c in loads[:4]:
        c.wait()
    sent[slots * rows :, :] = table_row(tables, slots)
    store(slots * rows, 16)
    for c in loads[4:]:
        c.wait()
    for k in range(slots):
        here = pl.ds(pl.multiple_of(c0[k] * blk, blk), blk)
        sent[k * rows : (k + 1) * rows, :] = dot(tokens_v[:, here], w_v[k], (1, 0)).astype(bf16)
        store(k * rows, rows)
    for c in stores:
        c.wait()


def first_places(tab):
    return tab[:8]


def places_of(tab, blocks, slots):
    place = lax.broadcasted_iota(jnp.int32, (2 * slots, LANES), 0)
    same = tab[8 : 8 + 2 * slots] == blocks[:1]
    return jnp.min(jnp.where(same, place, 2 * slots), axis=0, keepdims=True)


def start_taking(source, table, taken, sems):
    slots, _, blk = taken.shape
    copies = []
    for k in range(slots):
        begin = pl.multiple_of(table[k] * blk, blk)
        copies.append(pltpu.make_async_copy(source.at[:, pl.ds(begin, blk)], taken.at[k], sems.at[k]))
        copies[-1].start()
    return copies


def cotangent_kernel(
    c0, c1, c2, c3, tokens, grad_out, w1, w2, message, taken_t, cot, hid, back, tab, row, place_of, taken, sems
):
    slots, rows, blk = cot.shape
    copies = start_taking(grad_out, c3, cot, sems.at[0])
    copies_t = start_taking(tokens, c0, taken, sems.at[1])

    @pl.loop(0, place_of.shape[0])
    def _(block):
        place_of[block] = 2 * slots

    lane = lax.broadcasted_iota(jnp.int32, (8, LANES), 1)
    firsts = jnp.zeros((8, LANES), jnp.int32)
    for j in range(2 * slots):
        block = c1[j] if j < slots else c2[j - slots]
        place = jnp.minimum(place_of[block], j)
        place_of[block] = place
        firsts = jnp.where(lane == j, place, firsts)
        tab[8 + j : 9 + j, :] = jnp.full((1, LANES), block, jnp.int32)
    tab[:8] = firsts
    row[...] = table_row((c0, c1, c2, c3), slots)
    hid[...] = jnp.zeros(hid.shape, f32)
    back[...] = jnp.zeros(back.shape, f32)
    message[slots * rows :, :] = jnp.zeros((16, blk), bf16)
    for k in range(slots):
        copies[k].wait()
        value = dot(cot[k], w2[k], (1, 1))
        message[k * rows : (k + 1) * rows, :] = value.astype(bf16)
        at = jnp.minimum(place_of[c2[k]], slots)
        back[at] = back[at] + value
    for k in range(slots):
        copies_t[k].wait()
        at = place_of[c1[k]]
        hid[at] = hid[at] + dot(taken[k], w1[k], (1, 0))
        taken_t[k] = taken[k].T


def add_peers(acc, own, numbers_at, peers, slots):
    count, rows, _ = acc.shape
    for j in range(count):
        acc[j] = own[j]
    for numbers_of, ref in zip(numbers_at, peers):
        for k, at in enumerate(numbers_of):

            @pl.when(at < count)
            def _():
                acc[at] = acc[at] + ref[k * rows : (k + 1) * rows, :].astype(f32)


def hidden_kernel(dims, tab, own, *refs):
    slots, n_row, n_col, n_tok = dims
    peers, refs = refs[: n_row - 1], refs[n_row - 1 :]
    cot, active, hid, places, grad, half = refs
    part = grad.shape[1] // n_tok
    other = 1 - lax.rem(lax.axis_index("tok"), 2)
    found = [places_of(tab, numbers(ref, slots * cot.shape[1]), slots) for ref in peers]
    places[...] = jnp.zeros(places.shape, jnp.int32)
    for i, place in enumerate(found):
        places[8 * i : 8 * i + 8] = jnp.broadcast_to(place, (8, LANES))
    at = [[place[0, W1_COL * slots + k] for k in range(slots)] for place in found]
    firsts = first_places(tab)
    firsts = [firsts[0, slots + k] for k in range(slots)]
    add_peers(hid, own, at, peers, slots)
    for k in range(slots):
        h = hid[firsts[k]]
        active[k] = (h * cdf(h)).astype(bf16)
        grad[k] = dot(active[k], cot[k], (0, 0))
        for j in range(n_tok // 2):
            begin = pl.multiple_of((2 * j + other) * part, part)
            here = (j * slots + k) * part
            half[here : here + part, :] = grad[k, pl.ds(begin, part), :].astype(bf16)


def slope_kernel(dims, tab, row, active, hid, w2, slope, *refs):
    slots, n_row, n_col, n_tok = dims
    outs, value = refs[:n_col], refs[n_col]
    for k in range(slots):
        value[k] = dot(active[k], w2[k], (1, 0))
        cut(value.at[k], outs, k, "col")
    for ref in outs:
        ref[ref.shape[0] - 16 :, :] = row[...]
    firsts = first_places(tab)
    for k in range(slots):
        h = hid[firsts[0, k]]
        slope[k] = cdf(h) + h * jnp.exp(-0.5 * h * h) * (1.0 / math.sqrt(2.0 * math.pi))


def back_kernel(dims, tab, places, own, *refs):
    slots, n_row, n_col, n_tok = dims
    peers, refs = refs[: n_row - 1], refs[n_row - 1 :]
    slope, w1, near, taken_t, grad2, half = refs[:6]
    refs = refs[6:]
    outs, refs = refs[:n_col], refs[n_col:]
    grads, (acc, value, grad) = refs[:n_tok], refs[n_tok:]
    part = grad.shape[1] // n_tok
    paired = n_tok % 2 == 0
    found = [places[8 * i : 8 * i + 8] for i in range(len(peers))]
    at = [[place[0, W2_HID * slots + k] for k in range(slots)] for place in found]
    firsts = first_places(tab)
    firsts = [firsts[0, k] for k in range(slots)]
    add_peers(acc, own, at, peers, slots)
    for k in range(slots):
        g = (acc[firsts[k]] * slope[k]).astype(bf16)
        grad[k] = dot(taken_t[k], g, (1, 0))
        cut(grad.at[k], grads, k, "tok")
        value[k] = dot(g, w1[k], (1, 1))
        cut(value.at[k], outs, k, "col")
    if n_col > 1:
        outs[1][outs[0].shape[0] :, :] = near[...]
    for d in range(0, n_tok, 2 if paired else 1):
        to = target("tok", d)
        begin = pl.multiple_of(to * part, part)
        for k in range(slots):
            total = grad2[k, pl.ds(begin, part), :]
            if paired:
                there = pl.multiple_of((lax.div(to, 2) * slots + k) * part, part)
                total = total + half[pl.ds(there, part), :].astype(f32)
            grads[d][(slots + k) * part : (slots + k + 1) * part, :] = total.astype(bf16)
        spare = grads[d].shape[0] - 2 * slots * part
        grads[d][2 * slots * part :, :] = jnp.zeros((spare, LANES), bf16)


def pass_kernel(share, *refs):
    refs[-1][...] = share[...]


def add_shares(parts, result, first):
    part = result.shape[1]
    for k in range(result.shape[0]):
        here = slice((first + k) * part, (first + k + 1) * part)
        result[k] = sum(ref[here, :].astype(f32) for ref in parts)


def halves(refs, count):
    refs = list(refs)
    second, first = refs[:count], refs[count:]
    if len(refs) % 2 == 1:
        joined = refs[-1]
        rows = refs[count].shape[0]
        first = refs[count:-1] + [joined.at[:rows]]
        second = second + [joined.at[rows:]]
    return second, first


def output_kernel(dims, *refs):
    slots, n_row, n_col, n_tok = dims
    alone = max(1, n_col - 1)
    count = 2 * alone + (n_col > 1)
    outs, backs = halves(refs[:count], alone)
    refs = refs[count:]
    outputs, last, results, (acc_out, acc_in, sems) = refs[:2], refs[2], refs[3:5], refs[5:]
    blk, share = acc_out.shape[-1], acc_out.shape[1]
    acc_out[...] = jnp.zeros(acc_out.shape, f32)
    acc_in[...] = jnp.zeros(acc_in.shape, f32)
    for out, back in zip(outs, backs):
        blocks = numbers(out, slots * share)
        last[...] = blocks
        for k in range(slots):
            here = slice(k * share, (k + 1) * share)
            for ref, which, acc in ((out, W2_OUT, acc_out), (back, W1_ROW, acc_in)):
                at = blocks[0, which * slots + k]
                acc[at] = acc[at] + ref[here, :].astype(f32)
    stores = []
    for i, acc in enumerate((acc_out, acc_in)):
        for b in range(acc.shape[0]):
            results[i][:, b * blk : (b + 1) * blk] = acc[b].astype(bf16)
        stores.append(pltpu.make_async_copy(results[i], outputs[i], sems.at[i]))
        stores[-1].start()
    for c in stores:
        c.wait()


def grad_kernel(after, *refs):
    del after
    parts, gw1, gw2 = refs[:-2], refs[-2], refs[-1]
    slots, part, _ = gw1.shape
    add_shares(parts, gw1, 0)
    add_shares([ref for ref in parts if ref.shape[0] > slots * part], gw2, slots)


def alone(n):
    return [0] + list(range(2, n))


def shards(tokens, w1_blocks, w1_rows, w1_cols, w2_blocks, w2_hidden, w2_outs, grad_out):
    slots, blk = w1_blocks.shape[2], w1_blocks.shape[-1]
    rows = tokens.shape[0]
    n_row, n_col, n_tok = (lax.axis_size(a) for a in ("row", "col", "tok"))
    dims = (slots, n_row, n_col, n_tok)
    row_blocks = tokens.shape[1] // blk
    col_blocks = FF // n_col // blk
    share, part = rows // n_col, blk // n_tok
    w1 = w1_blocks.reshape(slots, blk, blk)
    w2 = w2_blocks.reshape(slots, blk, blk)
    tables = [t.reshape(slots) for t in (w1_rows, w1_cols, w2_hidden, w2_outs)]

    S = jax.ShapeDtypeStruct
    message = S((slots * rows + 16, blk), bf16)
    wide, narrow = S((slots, rows, blk), f32), S((slots, rows, blk), bf16)

    p_send = call(
        token_kernel,
        "take_tokens",
        TAKE_LIMIT,
        out_shape=message,
        in_specs=[HBM] * 6,
        out_specs=HBM,
        scratch_shapes=[
            pltpu.VMEM(tokens.shape, bf16),
            pltpu.VMEM((slots, blk, blk), bf16),
            pltpu.VMEM((slots * rows + 16, blk), bf16),
        ]
        + [pltpu.SMEM((slots,), jnp.int32)] * 4
        + [pltpu.SemaphoreType.DMA((7 + slots,))],
    )(*tables, tokens, w1)
    p_peers = [send(p_send, "row", d) for d in range(1, n_row)]

    b_send, taken_t, cot, hid, back, tab, row = call(
        cotangent_kernel,
        "take_cotangent",
        out_shape=(
            message,
            S((slots, blk, rows), bf16),
            narrow,
            S((2 * slots, rows, blk), f32),
            S((slots + 1, rows, blk), f32),
            S((8 + 2 * slots, LANES), jnp.int32),
            S((16, LANES), bf16),
        ),
        in_specs=[SMEM] * 4 + [HBM, HBM] + [VMEM] * 2,
        out_specs=(VMEM,) * 7,
        scratch_shapes=[
            pltpu.SMEM((col_blocks,), jnp.int32),
            pltpu.VMEM((slots, rows, blk), bf16),
            pltpu.SemaphoreType.DMA((2, slots)),
        ],
    )(*tables, tokens, grad_out, w1, w2)
    b_peers = [send(b_send, "row", d) for d in range(1, n_row)]

    single = S((slots * part, blk), bf16)
    double = S((2 * slots * part + 32, blk), bf16)
    grads = tuple(double if n_tok % 2 == 1 or d % 2 == 0 else single for d in range(n_tok))
    half = S((max(1, n_tok // 2) * slots * part, blk), bf16)
    peer_rows = 8 * max(1, n_row - 1)
    active, hid, places, grad2, half = call(
        functools.partial(hidden_kernel, dims),
        "hidden",
        out_shape=(
            narrow,
            S((2 * slots, rows, blk), f32),
            S((peer_rows, LANES), jnp.int32),
            S((slots, blk, blk), f32),
            half,
        ),
        in_specs=[VMEM] * (n_row + 2),
        out_specs=(VMEM,) * 5,
    )(tab, hid, *p_peers, cot)
    if n_tok % 2 == 0:
        half = lax.ppermute(half, "tok", [(i, i ^ 1) for i in range(n_tok)])
    out_share, back_share = S((slots * share + 16, blk), bf16), S((slots * share, blk), bf16)
    slope, *o_sent = call(
        functools.partial(slope_kernel, dims),
        "slope",
        out_shape=(wide,) + (out_share,) * n_col,
        in_specs=[VMEM] * 5,
        out_specs=(VMEM,) * (1 + n_col),
        scratch_shapes=[pltpu.VMEM((slots, rows, blk), f32)],
    )(tab, row, active, hid, w2)
    o_parts = [send(o_sent[d], "col", d) for d in alone(n_col)]

    outs = [back_share] * n_col
    if n_col > 1:
        outs[1] = S((2 * slots * share + 16, blk), bf16)
    sent = call(
        functools.partial(back_kernel, dims),
        "back",
        out_shape=(*outs, *grads),
        in_specs=[VMEM] * (n_row + 8),
        out_specs=(VMEM,) * (n_col + n_tok),
        scratch_shapes=[
            pltpu.VMEM((slots, rows, blk), f32),
            pltpu.VMEM((slots, rows, blk), f32),
            pltpu.VMEM((slots, blk, blk), f32),
        ],
    )(tab, places, back, *b_peers, slope, w1, o_sent[min(1, n_col - 1)], taken_t, grad2, half)
    i_sent, g_sent = list(sent[:n_col]), list(sent[n_col:])
    if n_col > 2:
        i_sent[2] = call(
            pass_kernel,
            "pass_share",
            out_shape=back_share,
            in_specs=[VMEM] + [ANY] * len(o_parts[1:]),
            out_specs=VMEM,
        )(i_sent[2], *o_parts[1:])
    i_parts = [send(i_sent[d], "col", d) for d in alone(n_col) + [1][: n_col - 1]]
    tok_parts = [send(g_sent[d], "tok", d) for d in range(n_tok)]

    result = S((share, row_blocks * blk), bf16)
    summed = S((slots, part, blk), f32)
    acc = pltpu.VMEM((row_blocks, share, blk), f32)
    output, grad_in, last = call(
        functools.partial(output_kernel, dims),
        "add_outputs",
        out_shape=(result, result, S((8, LANES), jnp.int32)),
        in_specs=[VMEM] * len(o_parts + i_parts),
        out_specs=(HBM, HBM, VMEM),
        scratch_shapes=[pltpu.VMEM(result.shape, bf16)] * 2
        + [acc, acc, pltpu.SemaphoreType.DMA((2,))],
    )(*o_parts, *i_parts)
    gw1, gw2 = call(
        grad_kernel,
        "add_grads",
        out_shape=(summed, summed),
        in_specs=[ANY] + [VMEM] * n_tok,
        out_specs=(VMEM,) * 2,
    )(last, *tok_parts[::-1])
    return (output, grad_in, gw1.reshape(1, 1, slots, part, blk), gw2.reshape(1, 1, slots, part, blk))


def solution(mesh):
    placed = (
        P("tok", "row"),
        P("row", "col", None, None, None),
        P("row", "col", None),
        P("row", "col", None),
        P("row", "col", None, None, None),
        P("row", "col", None),
        P("row", "col", None),
        P("tok", "row"),
    )
    return jax.shard_map(
        shards,
        mesh=mesh,
        in_specs=placed,
        out_specs=(
            P(("tok", "col"), "row"),
            P(("tok", "col"), "row"),
            P("row", "col", None, "tok", None),
            P("row", "col", None, "tok", None),
        ),
        check_vma=False,
    )
```

```python
import functools
import math

import jax
import jax.numpy as jnp
from jax import lax
from jax.experimental import pallas as pl
from jax.experimental.pallas import tpu as pltpu
from jax.sharding import PartitionSpec as P

FF = 32768
LANES = 128
f32 = jnp.float32
bf16 = jnp.bfloat16
VMEM = pl.BlockSpec(memory_space=pltpu.VMEM)
SMEM = pl.BlockSpec(memory_space=pltpu.SMEM)
ANY = pl.BlockSpec(memory_space=pl.ANY)
HBM = pl.BlockSpec(memory_space=pltpu.HBM)
TAKE_LIMIT = 62 * 1024 * 1024
LIMIT = 32 * 1024 * 1024

W1_ROW, W1_COL, W2_HID, W2_OUT = range(4)


def call(kernel, name, limit=LIMIT, **kwargs):
    return pl.pallas_call(
        kernel,
        name=name,
        compiler_params=pltpu.CompilerParams(vmem_limit_bytes=limit),
        cost_estimate=pl.CostEstimate(flops=1 << 25, bytes_accessed=1 << 19, transcendentals=0),
        **kwargs,
    )


def dot(a, b, contract):
    return lax.dot_general(a, b, ((contract[:1], contract[1:]), ((), ())), preferred_element_type=f32)


def cdf(v):
    return 0.5 * (1.0 + lax.erf(v * math.sqrt(0.5)))


def partner(i, d, n):
    return i ^ d if n & (n - 1) == 0 else (i + d) % n


def target(axis, d):
    n = lax.axis_size(axis)
    me = lax.axis_index(axis)
    return jnp.bitwise_xor(me, d) if n & (n - 1) == 0 else lax.rem(me + d, n)


def send(x, axis, d):
    n = lax.axis_size(axis)
    return lax.ppermute(x, axis, [(i, partner(i, d, n)) for i in range(n)]) if d else x


def cut(value, refs, k, axis):
    share = value.shape[0] // len(refs)
    for d, ref in enumerate(refs):
        begin = pl.multiple_of(target(axis, d) * share, share)
        ref[k * share : (k + 1) * share, :] = value[pl.ds(begin, share), :].astype(ref.dtype)


def table_row(tables, slots):
    lane = lax.broadcasted_iota(jnp.int32, (16, LANES), 1)
    row = jnp.zeros((16, LANES), f32)
    for which, table in enumerate(tables):
        for k in range(slots):
            row = jnp.where(lane == which * slots + k, table[k].astype(f32), row)
    return row.astype(bf16)


def numbers(ref, rows):
    return ref[rows : rows + 16, :].astype(f32)[:8].astype(jnp.int32)


def token_kernel(t0, t1, t2, t3, tokens, w1, message, tokens_v, w_v, sent, c0, c1, c2, c3, sems):
    slots, blk, _ = w_v.shape
    rows = tokens_v.shape[0]
    tables = (c0, c1, c2, c3)
    loads = [pltpu.make_async_copy(t, c, sems.at[i]) for i, (t, c) in enumerate(zip((t0, t1, t2, t3), tables))]
    loads.append(pltpu.make_async_copy(tokens, tokens_v, sems.at[4]))
    loads.append(pltpu.make_async_copy(w1, w_v, sems.at[5]))
    stores = []

    def store(begin, size):
        here = pl.ds(begin, size)
        stores.append(pltpu.make_async_copy(sent.at[here], message.at[here], sems.at[6 + len(stores)]))
        stores[-1].start()

    for c in loads:
        c.start()
    for c in loads[:4]:
        c.wait()
    sent[slots * rows :, :] = table_row(tables, slots)
    store(slots * rows, 16)
    for c in loads[4:]:
        c.wait()
    for k in range(slots):
        here = pl.ds(pl.multiple_of(c0[k] * blk, blk), blk)
        sent[k * rows : (k + 1) * rows, :] = dot(tokens_v[:, here], w_v[k], (1, 0)).astype(bf16)
        store(k * rows, rows)
    for c in stores:
        c.wait()


def first_places(tab):
    return tab[:8]


def places_of(tab, blocks, slots):
    place = lax.broadcasted_iota(jnp.int32, (2 * slots, LANES), 0)
    same = tab[8 : 8 + 2 * slots] == blocks[:1]
    return jnp.min(jnp.where(same, place, 2 * slots), axis=0, keepdims=True)


def start_taking(source, table, taken, sems):
    slots, _, blk = taken.shape
    copies = []
    for k in range(slots):
        begin = pl.multiple_of(table[k] * blk, blk)
        copies.append(pltpu.make_async_copy(source.at[:, pl.ds(begin, blk)], taken.at[k], sems.at[k]))
        copies[-1].start()
    return copies


def cotangent_kernel(
    c0, c1, c2, c3, tokens, grad_out, w1, w2, message, taken_t, cot, hid, back, tab, row, place_of, taken, sems
):
    slots, rows, blk = cot.shape
    copies = start_taking(grad_out, c3, cot, sems.at[0])
    copies_t = start_taking(tokens, c0, taken, sems.at[1])

    @pl.loop(0, place_of.shape[0])
    def _(block):
        place_of[block] = 2 * slots

    lane = lax.broadcasted_iota(jnp.int32, (8, LANES), 1)
    firsts = jnp.zeros((8, LANES), jnp.int32)
    for j in range(2 * slots):
        block = c1[j] if j < slots else c2[j - slots]
        place = jnp.minimum(place_of[block], j)
        place_of[block] = place
        firsts = jnp.where(lane == j, place, firsts)
        tab[8 + j : 9 + j, :] = jnp.full((1, LANES), block, jnp.int32)
    tab[:8] = firsts
    row[...] = table_row((c0, c1, c2, c3), slots)
    hid[...] = jnp.zeros(hid.shape, f32)
    back[...] = jnp.zeros(back.shape, f32)
    for k in range(slots):
        copies[k].wait()
        value = dot(cot[k], w2[k], (1, 1))
        message[k * rows : (k + 1) * rows, :] = value.astype(bf16)
        at = jnp.minimum(place_of[c2[k]], slots)
        back[at] = back[at] + value
    for k in range(slots):
        copies_t[k].wait()
        at = place_of[c1[k]]
        hid[at] = hid[at] + dot(taken[k], w1[k], (1, 0))
        taken_t[k] = taken[k].T


def add_peers(acc, own, numbers_at, peers, slots):
    count, rows, _ = acc.shape
    for j in range(count):
        acc[j] = own[j]
    for numbers_of, ref in zip(numbers_at, peers):
        for k, at in enumerate(numbers_of):

            @pl.when(at < count)
            def _():
                acc[at] = acc[at] + ref[k * rows : (k + 1) * rows, :].astype(f32)


def hidden_kernel(dims, tab, own, *refs):
    slots, n_row, n_col, n_tok = dims
    peers, refs = refs[: n_row - 1], refs[n_row - 1 :]
    cot, active, hid, places, grad, half = refs
    part = grad.shape[1] // n_tok
    other = 1 - lax.rem(lax.axis_index("tok"), 2)
    found = [places_of(tab, numbers(ref, slots * cot.shape[1]), slots) for ref in peers]
    places[...] = jnp.zeros(places.shape, jnp.int32)
    for i, place in enumerate(found):
        places[8 * i : 8 * i + 8] = jnp.broadcast_to(place, (8, LANES))
    at = [[place[0, W1_COL * slots + k] for k in range(slots)] for place in found]
    firsts = first_places(tab)
    firsts = [firsts[0, slots + k] for k in range(slots)]
    add_peers(hid, own, at, peers, slots)
    for k in range(slots):
        h = hid[firsts[k]]
        active[k] = (h * cdf(h)).astype(bf16)
        grad[k] = dot(active[k], cot[k], (0, 0))
        for j in range(n_tok // 2):
            begin = pl.multiple_of((2 * j + other) * part, part)
            here = (j * slots + k) * part
            half[here : here + part, :] = grad[k, pl.ds(begin, part), :].astype(bf16)


def slope_kernel(dims, tab, row, active, hid, w2, slope, *refs):
    slots, n_row, n_col, n_tok = dims
    outs, value = refs[:n_col], refs[n_col]
    for k in range(slots):
        value[k] = dot(active[k], w2[k], (1, 0))
        cut(value.at[k], outs, k, "col")
    for ref in outs:
        ref[ref.shape[0] - 16 :, :] = row[...]
    firsts = first_places(tab)
    for k in range(slots):
        h = hid[firsts[0, k]]
        slope[k] = cdf(h) + h * jnp.exp(-0.5 * h * h) * (1.0 / math.sqrt(2.0 * math.pi))


def back_kernel(dims, tab, places, own, *refs):
    slots, n_row, n_col, n_tok = dims
    peers, refs = refs[: n_row - 1], refs[n_row - 1 :]
    slope, w1, near, taken_t, grad2, half = refs[:6]
    refs = refs[6:]
    outs, refs = refs[:n_col], refs[n_col:]
    grads, (acc, value, grad) = refs[:n_tok], refs[n_tok:]
    part = grad.shape[1] // n_tok
    paired = n_tok % 2 == 0
    found = [places[8 * i : 8 * i + 8] for i in range(len(peers))]
    at = [[place[0, W2_HID * slots + k] for k in range(slots)] for place in found]
    firsts = first_places(tab)
    firsts = [firsts[0, k] for k in range(slots)]
    add_peers(acc, own, at, peers, slots)
    for k in range(slots):
        g = (acc[firsts[k]] * slope[k]).astype(bf16)
        grad[k] = dot(taken_t[k], g, (1, 0))
        cut(grad.at[k], grads, k, "tok")
        value[k] = dot(g, w1[k], (1, 1))
        cut(value.at[k], outs, k, "col")
    if n_col > 1:
        outs[1][outs[0].shape[0] :, :] = near[...]
    for d in range(0, n_tok, 2 if paired else 1):
        to = target("tok", d)
        begin = pl.multiple_of(to * part, part)
        for k in range(slots):
            total = grad2[k, pl.ds(begin, part), :]
            if paired:
                there = pl.multiple_of((lax.div(to, 2) * slots + k) * part, part)
                total = total + half[pl.ds(there, part), :].astype(f32)
            grads[d][(slots + k) * part : (slots + k + 1) * part, :] = total.astype(bf16)
        spare = grads[d].shape[0] - 2 * slots * part
        grads[d][2 * slots * part :, :] = jnp.zeros((spare, LANES), bf16)


def pass_kernel(share, *refs):
    refs[-1][...] = share[...]


def add_shares(parts, result, first):
    part = result.shape[1]
    for k in range(result.shape[0]):
        here = slice((first + k) * part, (first + k + 1) * part)
        result[k] = sum(ref[here, :].astype(f32) for ref in parts)


def halves(refs):
    joined, refs = list(refs[: len(refs) % 2]), list(refs[len(refs) % 2 :])
    count = len(refs) // 2
    rows = refs[count].shape[0]
    return refs[:count] + [j.at[rows:] for j in joined], refs[count:] + [j.at[:rows] for j in joined]


def output_kernel(dims, *refs):
    slots, n_row, n_col, n_tok = dims
    count = max(2, 2 * n_col - 1)
    outs, backs = halves(refs[:count])
    refs = refs[count:]
    outputs, last, results, (acc_out, acc_in, sems) = refs[:2], refs[2], refs[3:5], refs[5:]
    blk, share = acc_out.shape[-1], acc_out.shape[1]
    acc_out[...] = jnp.zeros(acc_out.shape, f32)
    acc_in[...] = jnp.zeros(acc_in.shape, f32)
    for out, back in zip(outs, backs):
        blocks = numbers(out, slots * share)
        last[...] = blocks
        for k in range(slots):
            here = slice(k * share, (k + 1) * share)
            for ref, which, acc in ((out, W2_OUT, acc_out), (back, W1_ROW, acc_in)):
                at = blocks[0, which * slots + k]
                acc[at] = acc[at] + ref[here, :].astype(f32)
    stores = []
    for i, acc in enumerate((acc_out, acc_in)):
        for b in range(acc.shape[0]):
            results[i][:, b * blk : (b + 1) * blk] = acc[b].astype(bf16)
        stores.append(pltpu.make_async_copy(results[i], outputs[i], sems.at[i]))
        stores[-1].start()
    for c in stores:
        c.wait()


def grad_kernel(after, *refs):
    del after
    parts, gw1, gw2 = refs[:-2], refs[-2], refs[-1]
    slots, part, _ = gw1.shape
    add_shares(parts, gw1, 0)
    add_shares([ref for ref in parts if ref.shape[0] > slots * part], gw2, slots)


def alone(n):
    return [0] + list(range(2, n))


def shards(tokens, w1_blocks, w1_rows, w1_cols, w2_blocks, w2_hidden, w2_outs, grad_out):
    slots, blk = w1_blocks.shape[2], w1_blocks.shape[-1]
    rows = tokens.shape[0]
    n_row, n_col, n_tok = (lax.axis_size(a) for a in ("row", "col", "tok"))
    dims = (slots, n_row, n_col, n_tok)
    row_blocks = tokens.shape[1] // blk
    col_blocks = FF // n_col // blk
    share, part = rows // n_col, blk // n_tok
    w1 = w1_blocks.reshape(slots, blk, blk)
    w2 = w2_blocks.reshape(slots, blk, blk)
    tables = [t.reshape(slots) for t in (w1_rows, w1_cols, w2_hidden, w2_outs)]

    S = jax.ShapeDtypeStruct
    message = S((slots * rows + 16, blk), bf16)
    wide, narrow = S((slots, rows, blk), f32), S((slots, rows, blk), bf16)

    p_send = call(
        token_kernel,
        "take_tokens",
        TAKE_LIMIT,
        out_shape=message,
        in_specs=[HBM] * 6,
        out_specs=HBM,
        scratch_shapes=[
            pltpu.VMEM(tokens.shape, bf16),
            pltpu.VMEM((slots, blk, blk), bf16),
            pltpu.VMEM((slots * rows + 16, blk), bf16),
        ]
        + [pltpu.SMEM((slots,), jnp.int32)] * 4
        + [pltpu.SemaphoreType.DMA((7 + slots,))],
    )(*tables, tokens, w1)
    p_peers = [send(p_send, "row", d) for d in range(1, n_row)]

    b_send, taken_t, cot, hid, back, tab, row = call(
        cotangent_kernel,
        "take_cotangent",
        out_shape=(
            S((slots * rows, blk), bf16),
            S((slots, blk, rows), bf16),
            narrow,
            S((2 * slots, rows, blk), f32),
            S((slots + 1, rows, blk), f32),
            S((8 + 2 * slots, LANES), jnp.int32),
            S((16, LANES), bf16),
        ),
        in_specs=[SMEM] * 4 + [HBM, HBM] + [VMEM] * 2,
        out_specs=(VMEM,) * 7,
        scratch_shapes=[
            pltpu.SMEM((col_blocks,), jnp.int32),
            pltpu.VMEM((slots, rows, blk), bf16),
            pltpu.SemaphoreType.DMA((2, slots)),
        ],
    )(*tables, tokens, grad_out, w1, w2)
    b_peers = [send(b_send, "row", d) for d in range(1, n_row)]

    single = S((slots * part, blk), bf16)
    double = S((2 * slots * part + 32, blk), bf16)
    grads = tuple(double if n_tok % 2 == 1 or d % 2 == 0 else single for d in range(n_tok))
    half = S((max(1, n_tok // 2) * slots * part, blk), bf16)
    peer_rows = 8 * max(1, n_row - 1)
    active, hid, places, grad2, half = call(
        functools.partial(hidden_kernel, dims),
        "hidden",
        out_shape=(
            narrow,
            S((2 * slots, rows, blk), f32),
            S((peer_rows, LANES), jnp.int32),
            S((slots, blk, blk), f32),
            half,
        ),
        in_specs=[VMEM] * (n_row + 2),
        out_specs=(VMEM,) * 5,
    )(tab, hid, *p_peers, cot)
    if n_tok % 2 == 0:
        half = lax.ppermute(half, "tok", [(i, i ^ 1) for i in range(n_tok)])
    out_share, back_share = S((slots * share + 16, blk), bf16), S((slots * share, blk), bf16)
    slope, *o_sent = call(
        functools.partial(slope_kernel, dims),
        "slope",
        out_shape=(wide,) + (out_share,) * n_col,
        in_specs=[VMEM] * 5,
        out_specs=(VMEM,) * (1 + n_col),
        scratch_shapes=[pltpu.VMEM((slots, rows, blk), f32)],
    )(tab, row, active, hid, w2)
    o_parts = [send(o_sent[d], "col", d) for d in alone(n_col)]

    outs = [back_share] * n_col
    if n_col > 1:
        outs[1] = S((2 * slots * share + 16, blk), bf16)
    sent = call(
        functools.partial(back_kernel, dims),
        "back",
        out_shape=(*outs, *grads),
        in_specs=[VMEM] * (n_row + 8),
        out_specs=(VMEM,) * (n_col + n_tok),
        scratch_shapes=[
            pltpu.VMEM((slots, rows, blk), f32),
            pltpu.VMEM((slots, rows, blk), f32),
            pltpu.VMEM((slots, blk, blk), f32),
        ],
    )(tab, places, back, *b_peers, slope, w1, o_sent[min(1, n_col - 1)], taken_t, grad2, half)
    i_sent, g_sent = list(sent[:n_col]), list(sent[n_col:])
    if n_col > 2:
        i_sent[2] = call(
            pass_kernel,
            "pass_share",
            out_shape=back_share,
            in_specs=[VMEM] + [ANY] * len(o_parts[1:]),
            out_specs=VMEM,
        )(i_sent[2], *o_parts[1:])
    i_parts = [send(i_sent[d], "col", d) for d in alone(n_col)]
    joined = [send(i_sent[1], "col", 1)] if n_col > 1 else []
    tok_parts = [send(g_sent[d], "tok", d) for d in range(n_tok)]

    result = S((share, row_blocks * blk), bf16)
    summed = S((slots, part, blk), f32)
    acc = pltpu.VMEM((row_blocks, share, blk), f32)
    output, grad_in, last = call(
        functools.partial(output_kernel, dims),
        "add_outputs",
        out_shape=(result, result, S((8, LANES), jnp.int32)),
        in_specs=[VMEM] * len(joined + o_parts + i_parts),
        out_specs=(HBM, HBM, VMEM),
        scratch_shapes=[pltpu.VMEM(result.shape, bf16)] * 2
        + [acc, acc, pltpu.SemaphoreType.DMA((2,))],
    )(*joined, *o_parts, *i_parts)
    gw1, gw2 = call(
        grad_kernel,
        "add_grads",
        out_shape=(summed, summed),
        in_specs=[ANY] + [VMEM] * n_tok,
        out_specs=(VMEM,) * 2,
    )(last, *tok_parts[::-1])
    return (output, grad_in, gw1.reshape(1, 1, slots, part, blk), gw2.reshape(1, 1, slots, part, blk))


def solution(mesh):
    placed = (
        P("tok", "row"),
        P("row", "col", None, None, None),
        P("row", "col", None),
        P("row", "col", None),
        P("row", "col", None, None, None),
        P("row", "col", None),
        P("row", "col", None),
        P("tok", "row"),
    )
    return jax.shard_map(
        shards,
        mesh=mesh,
        in_specs=placed,
        out_specs=(
            P(("tok", "col"), "row"),
            P(("tok", "col"), "row"),
            P("row", "col", None, "tok", None),
            P("row", "col", None, "tok", None),
        ),
        check_vma=False,
    )
```

```python
import functools
import math

import jax
import jax.numpy as jnp
from jax import lax
from jax.experimental import pallas as pl
from jax.experimental.pallas import tpu as pltpu
from jax.sharding import PartitionSpec as P

FF = 32768
LANES = 128
f32 = jnp.float32
bf16 = jnp.bfloat16
VMEM = pl.BlockSpec(memory_space=pltpu.VMEM)
SMEM = pl.BlockSpec(memory_space=pltpu.SMEM)
ANY = pl.BlockSpec(memory_space=pl.ANY)
HBM = pl.BlockSpec(memory_space=pltpu.HBM)
TAKE_LIMIT = 62 * 1024 * 1024
LIMIT = 32 * 1024 * 1024

W1_ROW, W1_COL, W2_HID, W2_OUT = range(4)


def call(kernel, name, limit=LIMIT, **kwargs):
    return pl.pallas_call(
        kernel,
        name=name,
        compiler_params=pltpu.CompilerParams(vmem_limit_bytes=limit),
        cost_estimate=pl.CostEstimate(flops=1 << 25, bytes_accessed=1 << 19, transcendentals=0),
        **kwargs,
    )


def dot(a, b, contract):
    return lax.dot_general(a, b, ((contract[:1], contract[1:]), ((), ())), preferred_element_type=f32)


def cdf(v):
    return 0.5 * (1.0 + lax.erf(v * math.sqrt(0.5)))


def partner(i, d, n):
    return i ^ d if n & (n - 1) == 0 else (i + d) % n


def target(axis, d):
    n = lax.axis_size(axis)
    me = lax.axis_index(axis)
    return jnp.bitwise_xor(me, d) if n & (n - 1) == 0 else lax.rem(me + d, n)


def send(x, axis, d):
    n = lax.axis_size(axis)
    return lax.ppermute(x, axis, [(i, partner(i, d, n)) for i in range(n)]) if d else x


def cut(value, refs, k, axis):
    share = value.shape[0] // len(refs)
    for d, ref in enumerate(refs):
        begin = pl.multiple_of(target(axis, d) * share, share)
        ref[k * share : (k + 1) * share, :] = value[pl.ds(begin, share), :].astype(ref.dtype)


def table_row(tables, slots):
    lane = lax.broadcasted_iota(jnp.int32, (16, LANES), 1)
    row = jnp.zeros((16, LANES), f32)
    for which, table in enumerate(tables):
        for k in range(slots):
            row = jnp.where(lane == which * slots + k, table[k].astype(f32), row)
    return row.astype(bf16)


def numbers(ref, rows):
    return ref[rows : rows + 16, :].astype(f32)[:8].astype(jnp.int32)


def token_kernel(t0, t1, t2, t3, tokens, w1, message, tokens_v, w_v, sent, c0, c1, c2, c3, sems):
    slots, blk, _ = w_v.shape
    rows = tokens_v.shape[0]
    tables = (c0, c1, c2, c3)
    loads = [pltpu.make_async_copy(t, c, sems.at[i]) for i, (t, c) in enumerate(zip((t0, t1, t2, t3), tables))]
    loads.append(pltpu.make_async_copy(tokens, tokens_v, sems.at[4]))
    loads.append(pltpu.make_async_copy(w1, w_v, sems.at[5]))
    stores = []

    def store(begin, size):
        here = pl.ds(begin, size)
        stores.append(pltpu.make_async_copy(sent.at[here], message.at[here], sems.at[6 + len(stores)]))
        stores[-1].start()

    for c in loads:
        c.start()
    for c in loads[:4]:
        c.wait()
    sent[slots * rows :, :] = table_row(tables, slots)
    store(slots * rows, 16)
    for c in loads[4:]:
        c.wait()
    for k in range(slots):
        here = pl.ds(pl.multiple_of(c0[k] * blk, blk), blk)
        sent[k * rows : (k + 1) * rows, :] = dot(tokens_v[:, here], w_v[k], (1, 0)).astype(bf16)
        store(k * rows, rows)
    for c in stores:
        c.wait()


def first_places(tab):
    return tab[:8]


def places_of(tab, blocks, slots):
    place = lax.broadcasted_iota(jnp.int32, (2 * slots, LANES), 0)
    same = tab[8 : 8 + 2 * slots] == blocks[:1]
    return jnp.min(jnp.where(same, place, 2 * slots), axis=0, keepdims=True)


def start_taking(source, table, taken, sems):
    slots, _, blk = taken.shape
    copies = []
    for k in range(slots):
        begin = pl.multiple_of(table[k] * blk, blk)
        copies.append(pltpu.make_async_copy(source.at[:, pl.ds(begin, blk)], taken.at[k], sems.at[k]))
        copies[-1].start()
    return copies


def cotangent_kernel(
    c0, c1, c2, c3, tokens, grad_out, w1, w2, message, taken_t, cot, hid, back, tab, row, place_of, taken, sems
):
    slots, rows, blk = cot.shape
    copies = start_taking(grad_out, c3, cot, sems.at[0])
    copies_t = start_taking(tokens, c0, taken, sems.at[1])

    @pl.loop(0, place_of.shape[0])
    def _(block):
        place_of[block] = 2 * slots

    lane = lax.broadcasted_iota(jnp.int32, (8, LANES), 1)
    firsts = jnp.zeros((8, LANES), jnp.int32)
    for j in range(2 * slots):
        block = c1[j] if j < slots else c2[j - slots]
        place = jnp.minimum(place_of[block], j)
        place_of[block] = place
        firsts = jnp.where(lane == j, place, firsts)
        tab[8 + j : 9 + j, :] = jnp.full((1, LANES), block, jnp.int32)
    tab[:8] = firsts
    row[...] = table_row((c0, c1, c2, c3), slots)
    hid[...] = jnp.zeros(hid.shape, f32)
    back[...] = jnp.zeros(back.shape, f32)
    for k in range(slots):
        copies[k].wait()
        value = dot(cot[k], w2[k], (1, 1))
        message[k * rows : (k + 1) * rows, :] = value.astype(bf16)
        at = jnp.minimum(place_of[c2[k]], slots)
        back[at] = back[at] + value
    for k in range(slots):
        copies_t[k].wait()
        at = place_of[c1[k]]
        hid[at] = hid[at] + dot(taken[k], w1[k], (1, 0))
        taken_t[k] = taken[k].T


def add_peers(acc, own, numbers_at, peers, slots):
    count, rows, _ = acc.shape
    for j in range(count):
        acc[j] = own[j]
    for numbers_of, ref in zip(numbers_at, peers):
        for k, at in enumerate(numbers_of):

            @pl.when(at < count)
            def _():
                acc[at] = acc[at] + ref[k * rows : (k + 1) * rows, :].astype(f32)


def hidden_kernel(dims, tab, own, *refs):
    slots, n_row, n_col, n_tok = dims
    peers, refs = refs[: n_row - 1], refs[n_row - 1 :]
    cot, active, hid, places, grad, half = refs
    rows = half.shape[0] // slots
    begin = pl.multiple_of((1 - lax.div(lax.axis_index("tok"), max(1, n_tok // 2))) * rows, rows)
    found = [places_of(tab, numbers(ref, slots * cot.shape[1]), slots) for ref in peers]
    places[...] = jnp.zeros(places.shape, jnp.int32)
    for i, place in enumerate(found):
        places[8 * i : 8 * i + 8] = jnp.broadcast_to(place, (8, LANES))
    at = [[place[0, W1_COL * slots + k] for k in range(slots)] for place in found]
    firsts = first_places(tab)
    firsts = [firsts[0, slots + k] for k in range(slots)]
    add_peers(hid, own, at, peers, slots)
    for k in range(slots):
        h = hid[firsts[k]]
        active[k] = (h * cdf(h)).astype(bf16)
        grad[k] = dot(active[k], cot[k], (0, 0))
        if n_tok > 1:
            half[k * rows : (k + 1) * rows, :] = grad[k, pl.ds(begin, rows), :].astype(bf16)


def slope_kernel(dims, tab, row, active, hid, w2, slope, *refs):
    slots, n_row, n_col, n_tok = dims
    outs, value = refs[:n_col], refs[n_col]
    for k in range(slots):
        value[k] = dot(active[k], w2[k], (1, 0))
        cut(value.at[k], outs, k, "col")
    for ref in outs:
        ref[ref.shape[0] - 16 :, :] = row[...]
    firsts = first_places(tab)
    for k in range(slots):
        h = hid[firsts[0, k]]
        slope[k] = cdf(h) + h * jnp.exp(-0.5 * h * h) * (1.0 / math.sqrt(2.0 * math.pi))


def back_kernel(dims, tab, places, own, *refs):
    slots, n_row, n_col, n_tok = dims
    peers, refs = refs[: n_row - 1], refs[n_row - 1 :]
    slope, w1, near, taken_t = refs[:4]
    refs = refs[4:]
    outs, refs = refs[:n_col], refs[n_col:]
    grads, (acc, value, grad) = refs[:n_tok], refs[n_tok:]
    found = [places[8 * i : 8 * i + 8] for i in range(len(peers))]
    at = [[place[0, W2_HID * slots + k] for k in range(slots)] for place in found]
    firsts = first_places(tab)
    firsts = [firsts[0, k] for k in range(slots)]
    add_peers(acc, own, at, peers, slots)
    for k in range(slots):
        g = (acc[firsts[k]] * slope[k]).astype(bf16)
        grad[k] = dot(taken_t[k], g, (1, 0))
        cut(grad.at[k], grads, k, "tok")
        value[k] = dot(g, w1[k], (1, 1))
        cut(value.at[k], outs, k, "col")
    if n_col > 1:
        outs[1][outs[0].shape[0] :, :] = near[...]
    for ref in grads:
        rows = slots * grad.shape[1] // n_tok
        if ref.shape[0] > rows:
            ref[rows:, :] = jnp.zeros((ref.shape[0] - rows, LANES), bf16)


def join_kernel(dims, grad2, half, *refs):
    slots, n_row, n_col, n_tok = dims
    side = max(1, n_tok // 2)
    part = grad2.shape[1] // n_tok
    shares, joined = refs[:side], refs[-side:]
    for d in range(side):
        to = target("tok", d)
        begin = pl.multiple_of(to * part, part)
        size = shares[d].shape[0]
        joined[d][:size, :] = shares[d][...]
        for k in range(slots):
            total = grad2[k, pl.ds(begin, part), :]
            if n_tok > 1:
                there = pl.multiple_of(k * side * part + lax.rem(to, side) * part, part)
                total = total + half[pl.ds(there, part), :].astype(f32)
            joined[d][size + k * part : size + (k + 1) * part, :] = total.astype(bf16)


def add_shares(parts, result, first):
    part = result.shape[1]
    for k in range(result.shape[0]):
        here = slice((first + k) * part, (first + k + 1) * part)
        result[k] = sum(ref[here, :].astype(f32) for ref in parts)


def halves(refs):
    joined, refs = list(refs[: len(refs) % 2]), list(refs[len(refs) % 2 :])
    count = len(refs) // 2
    rows = refs[count].shape[0]
    return refs[:count] + [j.at[rows:] for j in joined], refs[count:] + [j.at[:rows] for j in joined]


def output_kernel(dims, sum1, sum2, *refs):
    slots, n_row, n_col, n_tok = dims
    count = max(2, 2 * n_col - 1)
    outs, backs = halves(refs[:count])
    refs = refs[count:]
    outputs, gw1, gw2, results, (acc_out, acc_in, sems) = refs[:2], refs[2], refs[3], refs[4:6], refs[6:]
    blk, share = acc_out.shape[-1], acc_out.shape[1]
    stores = [pltpu.make_async_copy(sum1, gw1, sems.at[2]), pltpu.make_async_copy(sum2, gw2, sems.at[3])]
    for c in stores:
        c.start()
    acc_out[...] = jnp.zeros(acc_out.shape, f32)
    acc_in[...] = jnp.zeros(acc_in.shape, f32)
    for out, back in zip(outs, backs):
        blocks = numbers(out, slots * share)
        for k in range(slots):
            here = slice(k * share, (k + 1) * share)
            for ref, which, acc in ((out, W2_OUT, acc_out), (back, W1_ROW, acc_in)):
                at = blocks[0, which * slots + k]
                acc[at] = acc[at] + ref[here, :].astype(f32)
    for i, acc in enumerate((acc_out, acc_in)):
        for b in range(acc.shape[0]):
            results[i][:, b * blk : (b + 1) * blk] = acc[b].astype(bf16)
        stores.append(pltpu.make_async_copy(results[i], outputs[i], sems.at[i]))
        stores[-1].start()
    for c in stores:
        c.wait()


def grad_kernel(*refs):
    parts, gw1, gw2 = refs[:-2], refs[-2], refs[-1]
    slots, part, _ = gw1.shape
    add_shares(parts, gw1, 0)
    add_shares([ref for ref in parts if ref.shape[0] == 2 * slots * part], gw2, slots)


def alone(n):
    return [0] + list(range(2, n))


def shards(tokens, w1_blocks, w1_rows, w1_cols, w2_blocks, w2_hidden, w2_outs, grad_out):
    slots, blk = w1_blocks.shape[2], w1_blocks.shape[-1]
    rows = tokens.shape[0]
    n_row, n_col, n_tok = (lax.axis_size(a) for a in ("row", "col", "tok"))
    dims = (slots, n_row, n_col, n_tok)
    row_blocks = tokens.shape[1] // blk
    col_blocks = FF // n_col // blk
    share, part = rows // n_col, blk // n_tok
    w1 = w1_blocks.reshape(slots, blk, blk)
    w2 = w2_blocks.reshape(slots, blk, blk)
    tables = [t.reshape(slots) for t in (w1_rows, w1_cols, w2_hidden, w2_outs)]

    S = jax.ShapeDtypeStruct
    message = S((slots * rows + 16, blk), bf16)
    wide, narrow = S((slots, rows, blk), f32), S((slots, rows, blk), bf16)

    p_send = call(
        token_kernel,
        "take_tokens",
        TAKE_LIMIT,
        out_shape=message,
        in_specs=[HBM] * 6,
        out_specs=HBM,
        scratch_shapes=[
            pltpu.VMEM(tokens.shape, bf16),
            pltpu.VMEM((slots, blk, blk), bf16),
            pltpu.VMEM((slots * rows + 16, blk), bf16),
        ]
        + [pltpu.SMEM((slots,), jnp.int32)] * 4
        + [pltpu.SemaphoreType.DMA((7 + slots,))],
    )(*tables, tokens, w1)
    p_peers = [send(p_send, "row", d) for d in range(1, n_row)]

    b_send, taken_t, cot, hid, back, tab, row = call(
        cotangent_kernel,
        "take_cotangent",
        out_shape=(
            S((slots * rows, blk), bf16),
            S((slots, blk, rows), bf16),
            narrow,
            S((2 * slots, rows, blk), f32),
            S((slots + 1, rows, blk), f32),
            S((8 + 2 * slots, LANES), jnp.int32),
            S((16, LANES), bf16),
        ),
        in_specs=[SMEM] * 4 + [HBM, HBM] + [VMEM] * 2,
        out_specs=(VMEM,) * 7,
        scratch_shapes=[
            pltpu.SMEM((col_blocks,), jnp.int32),
            pltpu.VMEM((slots, rows, blk), bf16),
            pltpu.SemaphoreType.DMA((2, slots)),
        ],
    )(*tables, tokens, grad_out, w1, w2)
    b_peers = [send(b_send, "row", d) for d in range(1, n_row)]

    single = S((slots * part, blk), bf16)
    side = max(1, n_tok // 2)
    across = S((slots * part + 32, blk), bf16)
    grads = tuple(single if d < side else across for d in range(n_tok))
    half = S((slots * side * part, blk), bf16)
    peer_rows = 8 * max(1, n_row - 1)
    active, hid, places, grad2, half = call(
        functools.partial(hidden_kernel, dims),
        "hidden",
        out_shape=(
            narrow,
            S((2 * slots, rows, blk), f32),
            S((peer_rows, LANES), jnp.int32),
            S((slots, blk, blk), f32),
            half,
        ),
        in_specs=[VMEM] * (n_row + 2),
        out_specs=(VMEM,) * 5,
    )(tab, hid, *p_peers, cot)
    if n_tok > 1:
        half = lax.ppermute(half, "tok", [(i, (i + side) % n_tok) for i in range(n_tok)])
    out_share, back_share = S((slots * share + 16, blk), bf16), S((slots * share, blk), bf16)
    slope, *o_sent = call(
        functools.partial(slope_kernel, dims),
        "slope",
        out_shape=(wide,) + (out_share,) * n_col,
        in_specs=[VMEM] * 5,
        out_specs=(VMEM,) * (1 + n_col),
        scratch_shapes=[pltpu.VMEM((slots, rows, blk), f32)],
    )(tab, row, active, hid, w2)
    o_parts = [send(o_sent[d], "col", d) for d in alone(n_col)]

    outs = [back_share] * n_col
    if n_col > 1:
        outs[1] = S((2 * slots * share + 16, blk), bf16)
    sent = call(
        functools.partial(back_kernel, dims),
        "back",
        out_shape=(*outs, *grads),
        in_specs=[VMEM] * (n_row + 6),
        out_specs=(VMEM,) * (n_col + n_tok),
        scratch_shapes=[
            pltpu.VMEM((slots, rows, blk), f32),
            pltpu.VMEM((slots, rows, blk), f32),
            pltpu.VMEM((slots, blk, blk), f32),
        ],
    )(tab, places, back, *b_peers, slope, w1, o_sent[min(1, n_col - 1)], taken_t)
    i_sent, g_sent = list(sent[:n_col]), list(sent[n_col:])
    early = o_parts[1:]
    g_sent[:side] = call(
        functools.partial(join_kernel, dims),
        "join_shares",
        out_shape=(S((2 * slots * part, blk), bf16),) * side,
        in_specs=[VMEM] * (2 + side) + [ANY] * len(early),
        out_specs=(VMEM,) * side,
    )(grad2, half, *g_sent[:side], *early)
    i_parts = [send(i_sent[d], "col", d) for d in alone(n_col)]
    joined = [send(i_sent[1], "col", 1)] if n_col > 1 else []
    tok_parts = [send(g_sent[d], "tok", d) for d in range(n_tok)]

    result = S((share, row_blocks * blk), bf16)
    summed = S((slots, part, blk), f32)
    acc = pltpu.VMEM((row_blocks, share, blk), f32)
    summed = S((slots, part, blk), f32)
    sums = call(
        grad_kernel,
        "add_grads",
        out_shape=(summed, summed),
        in_specs=[VMEM] * n_tok,
        out_specs=(VMEM,) * 2,
    )(*tok_parts[::-1])
    output, grad_in, gw1, gw2 = call(
        functools.partial(output_kernel, dims),
        "add_outputs",
        out_shape=(result, result, summed, summed),
        in_specs=[VMEM] * len([*sums, *joined, *o_parts, *i_parts]),
        out_specs=(HBM,) * 4,
        scratch_shapes=[pltpu.VMEM(result.shape, bf16)] * 2
        + [acc, acc, pltpu.SemaphoreType.DMA((4,))],
    )(*sums, *joined, *o_parts, *i_parts)
    return (output, grad_in, gw1.reshape(1, 1, slots, part, blk), gw2.reshape(1, 1, slots, part, blk))


def solution(mesh):
    placed = (
        P("tok", "row"),
        P("row", "col", None, None, None),
        P("row", "col", None),
        P("row", "col", None),
        P("row", "col", None, None, None),
        P("row", "col", None),
        P("row", "col", None),
        P("tok", "row"),
    )
    return jax.shard_map(
        shards,
        mesh=mesh,
        in_specs=placed,
        out_specs=(
            P(("tok", "col"), "row"),
            P(("tok", "col"), "row"),
            P("row", "col", None, "tok", None),
            P("row", "col", None, "tok", None),
        ),
        check_vma=False,
    )
```

```python
import functools
import math

import jax
import jax.numpy as jnp
from jax import lax
from jax.experimental import pallas as pl
from jax.experimental.pallas import tpu as pltpu
from jax.sharding import PartitionSpec as P

FF = 32768
LANES = 128
f32 = jnp.float32
bf16 = jnp.bfloat16
VMEM = pl.BlockSpec(memory_space=pltpu.VMEM)
SMEM = pl.BlockSpec(memory_space=pltpu.SMEM)
ANY = pl.BlockSpec(memory_space=pl.ANY)
HBM = pl.BlockSpec(memory_space=pltpu.HBM)
TAKE_LIMIT = 62 * 1024 * 1024
LIMIT = 32 * 1024 * 1024

W1_ROW, W1_COL, W2_HID, W2_OUT = range(4)


def call(kernel, name, limit=LIMIT, **kwargs):
    return pl.pallas_call(
        kernel,
        name=name,
        compiler_params=pltpu.CompilerParams(vmem_limit_bytes=limit),
        cost_estimate=pl.CostEstimate(flops=1 << 25, bytes_accessed=1 << 19, transcendentals=0),
        **kwargs,
    )


def dot(a, b, contract):
    return lax.dot_general(a, b, ((contract[:1], contract[1:]), ((), ())), preferred_element_type=f32)


def cdf(v):
    return 0.5 * (1.0 + lax.erf(v * math.sqrt(0.5)))


def partner(i, d, n):
    return i ^ d if n & (n - 1) == 0 else (i + d) % n


def target(axis, d):
    n = lax.axis_size(axis)
    me = lax.axis_index(axis)
    return jnp.bitwise_xor(me, d) if n & (n - 1) == 0 else lax.rem(me + d, n)


def send(x, axis, d):
    n = lax.axis_size(axis)
    return lax.ppermute(x, axis, [(i, partner(i, d, n)) for i in range(n)]) if d else x


def cut(value, refs, k, axis):
    share = value.shape[0] // len(refs)
    for d, ref in enumerate(refs):
        begin = pl.multiple_of(target(axis, d) * share, share)
        ref[k * share : (k + 1) * share, :] = value[pl.ds(begin, share), :].astype(ref.dtype)


def table_row(tables, slots):
    lane = lax.broadcasted_iota(jnp.int32, (16, LANES), 1)
    row = jnp.zeros((16, LANES), f32)
    for which, table in enumerate(tables):
        for k in range(slots):
            row = jnp.where(lane == which * slots + k, table[k].astype(f32), row)
    return row.astype(bf16)


def numbers(ref, rows):
    return ref[rows : rows + 16, :].astype(f32)[:8].astype(jnp.int32)


def token_kernel(t0, t1, t2, t3, tokens, w1, message, tokens_v, w_v, sent, c0, c1, c2, c3, sems):
    slots, blk, _ = w_v.shape
    rows = tokens_v.shape[0]
    tables = (c0, c1, c2, c3)
    loads = [pltpu.make_async_copy(t, c, sems.at[i]) for i, (t, c) in enumerate(zip((t0, t1, t2, t3), tables))]
    loads.append(pltpu.make_async_copy(tokens, tokens_v, sems.at[4]))
    loads.append(pltpu.make_async_copy(w1, w_v, sems.at[5]))
    stores = []

    def store(begin, size):
        here = pl.ds(begin, size)
        stores.append(pltpu.make_async_copy(sent.at[here], message.at[here], sems.at[6 + len(stores)]))
        stores[-1].start()

    for c in loads:
        c.start()
    for c in loads[:4]:
        c.wait()
    sent[slots * rows :, :] = table_row(tables, slots)
    store(slots * rows, 16)
    for c in loads[4:]:
        c.wait()
    for k in range(slots):
        here = pl.ds(pl.multiple_of(c0[k] * blk, blk), blk)
        sent[k * rows : (k + 1) * rows, :] = dot(tokens_v[:, here], w_v[k], (1, 0)).astype(bf16)
        store(k * rows, rows)
    for c in stores:
        c.wait()


def first_places(tab):
    return tab[:8]


def places_of(tab, blocks, slots):
    place = lax.broadcasted_iota(jnp.int32, (2 * slots, LANES), 0)
    same = tab[8 : 8 + 2 * slots] == blocks[:1]
    return jnp.min(jnp.where(same, place, 2 * slots), axis=0, keepdims=True)


def start_taking(source, table, taken, sems):
    slots, _, blk = taken.shape
    copies = []
    for k in range(slots):
        begin = pl.multiple_of(table[k] * blk, blk)
        copies.append(pltpu.make_async_copy(source.at[:, pl.ds(begin, blk)], taken.at[k], sems.at[k]))
        copies[-1].start()
    return copies


def cotangent_kernel(
    c0, c1, c2, c3, tokens, grad_out, w1, w2, message, taken_t, cot, hid, back, tab, row, place_of, taken, sems
):
    slots, rows, blk = cot.shape
    copies = start_taking(grad_out, c3, cot, sems.at[0])
    copies_t = start_taking(tokens, c0, taken, sems.at[1])

    @pl.loop(0, place_of.shape[0])
    def _(block):
        place_of[block] = 2 * slots

    lane = lax.broadcasted_iota(jnp.int32, (8, LANES), 1)
    firsts = jnp.zeros((8, LANES), jnp.int32)
    for j in range(2 * slots):
        block = c1[j] if j < slots else c2[j - slots]
        place = jnp.minimum(place_of[block], j)
        place_of[block] = place
        firsts = jnp.where(lane == j, place, firsts)
        tab[8 + j : 9 + j, :] = jnp.full((1, LANES), block, jnp.int32)
    tab[:8] = firsts
    row[...] = table_row((c0, c1, c2, c3), slots)
    hid[...] = jnp.zeros(hid.shape, f32)
    back[...] = jnp.zeros(back.shape, f32)
    for k in range(slots):
        copies[k].wait()
        value = dot(cot[k], w2[k], (1, 1))
        message[k * rows : (k + 1) * rows, :] = value.astype(bf16)
        at = jnp.minimum(place_of[c2[k]], slots)
        back[at] = back[at] + value
    for k in range(slots):
        copies_t[k].wait()
        at = place_of[c1[k]]
        hid[at] = hid[at] + dot(taken[k], w1[k], (1, 0))
        taken_t[k] = taken[k].T


def add_peers(acc, own, numbers_at, peers, slots):
    count, rows, _ = acc.shape
    for j in range(count):
        acc[j] = own[j]
    for numbers_of, ref in zip(numbers_at, peers):
        for k, at in enumerate(numbers_of):

            @pl.when(at < count)
            def _():
                acc[at] = acc[at] + ref[k * rows : (k + 1) * rows, :].astype(f32)


def hidden_kernel(dims, tab, own, *refs):
    slots, n_row, n_col, n_tok = dims
    peers, refs = refs[: n_row - 1], refs[n_row - 1 :]
    cot, active, hid, places, grad, half = refs
    rows = half.shape[0] // slots
    begin = pl.multiple_of((1 - lax.div(lax.axis_index("tok"), max(1, n_tok // 2))) * rows, rows)
    found = [places_of(tab, numbers(ref, slots * cot.shape[1]), slots) for ref in peers]
    places[...] = jnp.zeros(places.shape, jnp.int32)
    for i, place in enumerate(found):
        places[8 * i : 8 * i + 8] = jnp.broadcast_to(place, (8, LANES))
    at = [[place[0, W1_COL * slots + k] for k in range(slots)] for place in found]
    firsts = first_places(tab)
    firsts = [firsts[0, slots + k] for k in range(slots)]
    add_peers(hid, own, at, peers, slots)
    for k in range(slots):
        h = hid[firsts[k]]
        active[k] = (h * cdf(h)).astype(bf16)
        grad[k] = dot(active[k], cot[k], (0, 0))
        if n_tok > 1:
            half[k * rows : (k + 1) * rows, :] = grad[k, pl.ds(begin, rows), :].astype(bf16)


def slope_kernel(dims, tab, row, active, hid, w2, slope, *refs):
    slots, n_row, n_col, n_tok = dims
    outs, value = refs[:n_col], refs[n_col]
    for k in range(slots):
        value[k] = dot(active[k], w2[k], (1, 0))
        cut(value.at[k], outs, k, "col")
    for ref in outs:
        ref[ref.shape[0] - 16 :, :] = row[...]
    firsts = first_places(tab)
    for k in range(slots):
        h = hid[firsts[0, k]]
        slope[k] = cdf(h) + h * jnp.exp(-0.5 * h * h) * (1.0 / math.sqrt(2.0 * math.pi))


def back_kernel(dims, tab, places, own, *refs):
    slots, n_row, n_col, n_tok = dims
    peers, refs = refs[: n_row - 1], refs[n_row - 1 :]
    slope, w1, taken_t = refs[:3]
    refs = refs[3:]
    outs, refs = refs[:n_col], refs[n_col:]
    grads, (acc, value, grad) = refs[:n_tok], refs[n_tok:]
    found = [places[8 * i : 8 * i + 8] for i in range(len(peers))]
    at = [[place[0, W2_HID * slots + k] for k in range(slots)] for place in found]
    firsts = first_places(tab)
    firsts = [firsts[0, k] for k in range(slots)]
    add_peers(acc, own, at, peers, slots)
    for k in range(slots):
        g = (acc[firsts[k]] * slope[k]).astype(bf16)
        grad[k] = dot(taken_t[k], g, (1, 0))
        cut(grad.at[k], grads, k, "tok")
        value[k] = dot(g, w1[k], (1, 1))
        cut(value.at[k], outs, k, "col")
    for ref in grads:
        rows = slots * grad.shape[1] // n_tok
        if ref.shape[0] > rows:
            ref[rows:, :] = jnp.zeros((ref.shape[0] - rows, LANES), bf16)


def join_kernel(dims, grad2, half, *refs):
    slots, n_row, n_col, n_tok = dims
    side = max(1, n_tok // 2)
    part = grad2.shape[1] // n_tok
    shares, joined = refs[:side], refs[-side:]
    for d in range(side):
        to = target("tok", d)
        begin = pl.multiple_of(to * part, part)
        size = shares[d].shape[0]
        joined[d][:size, :] = shares[d][...]
        for k in range(slots):
            total = grad2[k, pl.ds(begin, part), :]
            if n_tok > 1:
                there = pl.multiple_of(k * side * part + lax.rem(to, side) * part, part)
                total = total + half[pl.ds(there, part), :].astype(f32)
            joined[d][size + k * part : size + (k + 1) * part, :] = total.astype(bf16)


def add_shares(parts, result, first):
    part = result.shape[1]
    for k in range(result.shape[0]):
        here = slice((first + k) * part, (first + k + 1) * part)
        result[k] = sum(ref[here, :].astype(f32) for ref in parts)


def output_kernel(dims, sum1, sum2, *refs):
    slots, n_row, n_col, n_tok = dims
    outs, backs, refs = refs[:n_col], refs[n_col : 2 * n_col], refs[2 * n_col :]
    outputs, gw1, gw2, results, (acc_out, acc_in, sems) = refs[:2], refs[2], refs[3], refs[4:6], refs[6:]
    blk, share = acc_out.shape[-1], acc_out.shape[1]
    stores = [pltpu.make_async_copy(sum1, gw1, sems.at[2]), pltpu.make_async_copy(sum2, gw2, sems.at[3])]
    for c in stores:
        c.start()
    acc_out[...] = jnp.zeros(acc_out.shape, f32)
    acc_in[...] = jnp.zeros(acc_in.shape, f32)
    for out, back in zip(outs, backs):
        blocks = numbers(out, slots * share)
        for k in range(slots):
            here = slice(k * share, (k + 1) * share)
            for ref, which, acc in ((out, W2_OUT, acc_out), (back, W1_ROW, acc_in)):
                at = blocks[0, which * slots + k]
                acc[at] = acc[at] + ref[here, :].astype(f32)
    for i, acc in enumerate((acc_out, acc_in)):
        for b in range(acc.shape[0]):
            results[i][:, b * blk : (b + 1) * blk] = acc[b].astype(bf16)
        stores.append(pltpu.make_async_copy(results[i], outputs[i], sems.at[i]))
        stores[-1].start()
    for c in stores:
        c.wait()


def grad_kernel(*refs):
    parts, gw1, gw2 = refs[:-2], refs[-2], refs[-1]
    slots, part, _ = gw1.shape
    add_shares(parts, gw1, 0)
    add_shares([ref for ref in parts if ref.shape[0] == 2 * slots * part], gw2, slots)


def near_last(n):
    return [0] + list(range(2, n)) + [1][: n - 1]


def shards(tokens, w1_blocks, w1_rows, w1_cols, w2_blocks, w2_hidden, w2_outs, grad_out):
    slots, blk = w1_blocks.shape[2], w1_blocks.shape[-1]
    rows = tokens.shape[0]
    n_row, n_col, n_tok = (lax.axis_size(a) for a in ("row", "col", "tok"))
    dims = (slots, n_row, n_col, n_tok)
    row_blocks = tokens.shape[1] // blk
    col_blocks = FF // n_col // blk
    share, part = rows // n_col, blk // n_tok
    w1 = w1_blocks.reshape(slots, blk, blk)
    w2 = w2_blocks.reshape(slots, blk, blk)
    tables = [t.reshape(slots) for t in (w1_rows, w1_cols, w2_hidden, w2_outs)]

    S = jax.ShapeDtypeStruct
    message = S((slots * rows + 16, blk), bf16)
    wide, narrow = S((slots, rows, blk), f32), S((slots, rows, blk), bf16)

    p_send = call(
        token_kernel,
        "take_tokens",
        TAKE_LIMIT,
        out_shape=message,
        in_specs=[HBM] * 6,
        out_specs=HBM,
        scratch_shapes=[
            pltpu.VMEM(tokens.shape, bf16),
            pltpu.VMEM((slots, blk, blk), bf16),
            pltpu.VMEM((slots * rows + 16, blk), bf16),
        ]
        + [pltpu.SMEM((slots,), jnp.int32)] * 4
        + [pltpu.SemaphoreType.DMA((7 + slots,))],
    )(*tables, tokens, w1)
    p_peers = [send(p_send, "row", d) for d in range(1, n_row)]

    b_send, taken_t, cot, hid, back, tab, row = call(
        cotangent_kernel,
        "take_cotangent",
        out_shape=(
            S((slots * rows, blk), bf16),
            S((slots, blk, rows), bf16),
            narrow,
            S((2 * slots, rows, blk), f32),
            S((slots + 1, rows, blk), f32),
            S((8 + 2 * slots, LANES), jnp.int32),
            S((16, LANES), bf16),
        ),
        in_specs=[SMEM] * 4 + [HBM, HBM] + [VMEM] * 2,
        out_specs=(VMEM,) * 7,
        scratch_shapes=[
            pltpu.SMEM((col_blocks,), jnp.int32),
            pltpu.VMEM((slots, rows, blk), bf16),
            pltpu.SemaphoreType.DMA((2, slots)),
        ],
    )(*tables, tokens, grad_out, w1, w2)
    b_peers = [send(b_send, "row", d) for d in range(1, n_row)]

    single = S((slots * part, blk), bf16)
    side = max(1, n_tok // 2)
    across = S((slots * part + 32, blk), bf16)
    grads = tuple(single if d < side else across for d in range(n_tok))
    half = S((slots * side * part, blk), bf16)
    peer_rows = 8 * max(1, n_row - 1)
    active, hid, places, grad2, half = call(
        functools.partial(hidden_kernel, dims),
        "hidden",
        out_shape=(
            narrow,
            S((2 * slots, rows, blk), f32),
            S((peer_rows, LANES), jnp.int32),
            S((slots, blk, blk), f32),
            half,
        ),
        in_specs=[VMEM] * (n_row + 2),
        out_specs=(VMEM,) * 5,
    )(tab, hid, *p_peers, cot)
    if n_tok > 1:
        half = lax.ppermute(half, "tok", [(i, (i + side) % n_tok) for i in range(n_tok)])
    out_share, back_share = S((slots * share + 16, blk), bf16), S((slots * share, blk), bf16)
    slope, *o_sent = call(
        functools.partial(slope_kernel, dims),
        "slope",
        out_shape=(wide,) + (out_share,) * n_col,
        in_specs=[VMEM] * 5,
        out_specs=(VMEM,) * (1 + n_col),
        scratch_shapes=[pltpu.VMEM((slots, rows, blk), f32)],
    )(tab, row, active, hid, w2)
    o_parts = [send(o_sent[d], "col", d) for d in near_last(n_col)]

    sent = call(
        functools.partial(back_kernel, dims),
        "back",
        out_shape=(back_share,) * n_col + grads,
        in_specs=[VMEM] * (n_row + 5),
        out_specs=(VMEM,) * (n_col + n_tok),
        scratch_shapes=[
            pltpu.VMEM((slots, rows, blk), f32),
            pltpu.VMEM((slots, rows, blk), f32),
            pltpu.VMEM((slots, blk, blk), f32),
        ],
    )(tab, places, back, *b_peers, slope, w1, taken_t)
    i_sent, g_sent = list(sent[:n_col]), list(sent[n_col:])
    early = o_parts[1:]
    g_sent[:side] = call(
        functools.partial(join_kernel, dims),
        "join_shares",
        out_shape=(S((2 * slots * part, blk), bf16),) * side,
        in_specs=[VMEM] * (2 + side) + [ANY] * len(early),
        out_specs=(VMEM,) * side,
    )(grad2, half, *g_sent[:side], *early)
    i_parts = [send(i_sent[d], "col", d) for d in near_last(n_col)]
    tok_parts = [send(g_sent[d], "tok", d) for d in range(n_tok)]

    result = S((share, row_blocks * blk), bf16)
    summed = S((slots, part, blk), f32)
    acc = pltpu.VMEM((row_blocks, share, blk), f32)
    summed = S((slots, part, blk), f32)
    sums = call(
        grad_kernel,
        "add_grads",
        out_shape=(summed, summed),
        in_specs=[VMEM] * n_tok,
        out_specs=(VMEM,) * 2,
    )(*tok_parts[:1], *tok_parts[2:], *tok_parts[1:2])
    output, grad_in, gw1, gw2 = call(
        functools.partial(output_kernel, dims),
        "add_outputs",
        out_shape=(result, result, summed, summed),
        in_specs=[VMEM] * len([*sums, *o_parts, *i_parts]),
        out_specs=(HBM,) * 4,
        scratch_shapes=[pltpu.VMEM(result.shape, bf16)] * 2
        + [acc, acc, pltpu.SemaphoreType.DMA((4,))],
    )(*sums, *o_parts, *i_parts)
    return (output, grad_in, gw1.reshape(1, 1, slots, part, blk), gw2.reshape(1, 1, slots, part, blk))


def solution(mesh):
    placed = (
        P("tok", "row"),
        P("row", "col", None, None, None),
        P("row", "col", None),
        P("row", "col", None),
        P("row", "col", None, None, None),
        P("row", "col", None),
        P("row", "col", None),
        P("tok", "row"),
    )
    return jax.shard_map(
        shards,
        mesh=mesh,
        in_specs=placed,
        out_specs=(
            P(("tok", "col"), "row"),
            P(("tok", "col"), "row"),
            P("row", "col", None, "tok", None),
            P("row", "col", None, "tok", None),
        ),
        check_vma=False,
    )
```

```python
import functools
import math

import jax
import jax.numpy as jnp
from jax import lax
from jax.experimental import pallas as pl
from jax.experimental.pallas import tpu as pltpu
from jax.sharding import PartitionSpec as P

FF = 32768
LANES = 128
f32 = jnp.float32
bf16 = jnp.bfloat16
VMEM = pl.BlockSpec(memory_space=pltpu.VMEM)
SMEM = pl.BlockSpec(memory_space=pltpu.SMEM)
ANY = pl.BlockSpec(memory_space=pl.ANY)
HBM = pl.BlockSpec(memory_space=pltpu.HBM)
TAKE_LIMIT = 62 * 1024 * 1024
LIMIT = 32 * 1024 * 1024

W1_ROW, W1_COL, W2_HID, W2_OUT = range(4)


def call(kernel, name, limit=LIMIT, **kwargs):
    return pl.pallas_call(
        kernel,
        name=name,
        compiler_params=pltpu.CompilerParams(vmem_limit_bytes=limit),
        cost_estimate=pl.CostEstimate(flops=1 << 25, bytes_accessed=1 << 19, transcendentals=0),
        **kwargs,
    )


def dot(a, b, contract):
    return lax.dot_general(a, b, ((contract[:1], contract[1:]), ((), ())), preferred_element_type=f32)


def cdf(v):
    return 0.5 * (1.0 + lax.erf(v * math.sqrt(0.5)))


def partner(i, d, n):
    return i ^ d if n & (n - 1) == 0 else (i + d) % n


def target(axis, d):
    n = lax.axis_size(axis)
    me = lax.axis_index(axis)
    return jnp.bitwise_xor(me, d) if n & (n - 1) == 0 else lax.rem(me + d, n)


def send(x, axis, d):
    n = lax.axis_size(axis)
    return lax.ppermute(x, axis, [(i, partner(i, d, n)) for i in range(n)]) if d else x


def cut(value, refs, k, axis):
    share = value.shape[0] // len(refs)
    for d, ref in enumerate(refs):
        begin = pl.multiple_of(target(axis, d) * share, share)
        ref[k * share : (k + 1) * share, :] = value[pl.ds(begin, share), :].astype(ref.dtype)


def table_row(tables, slots):
    lane = lax.broadcasted_iota(jnp.int32, (16, LANES), 1)
    row = jnp.zeros((16, LANES), f32)
    for which, table in enumerate(tables):
        for k in range(slots):
            row = jnp.where(lane == which * slots + k, table[k].astype(f32), row)
    return row.astype(bf16)


def numbers(ref, rows):
    return ref[rows : rows + 16, :].astype(f32)[:8].astype(jnp.int32)


def token_kernel(t0, t1, t2, t3, tokens, w1, message, tokens_v, w_v, sent, c0, c1, c2, c3, sems):
    slots, blk, _ = w_v.shape
    rows = tokens_v.shape[0]
    tables = (c0, c1, c2, c3)
    loads = [pltpu.make_async_copy(t, c, sems.at[i]) for i, (t, c) in enumerate(zip((t0, t1, t2, t3), tables))]
    loads.append(pltpu.make_async_copy(tokens, tokens_v, sems.at[4]))
    loads.append(pltpu.make_async_copy(w1, w_v, sems.at[5]))
    stores = []

    def store(begin, size):
        here = pl.ds(begin, size)
        stores.append(pltpu.make_async_copy(sent.at[here], message.at[here], sems.at[6 + len(stores)]))
        stores[-1].start()

    for c in loads:
        c.start()
    for c in loads[:4]:
        c.wait()
    sent[slots * rows :, :] = table_row(tables, slots)
    store(slots * rows, 16)
    for c in loads[4:]:
        c.wait()
    for k in range(slots):
        here = pl.ds(pl.multiple_of(c0[k] * blk, blk), blk)
        sent[k * rows : (k + 1) * rows, :] = dot(tokens_v[:, here], w_v[k], (1, 0)).astype(bf16)
        store(k * rows, rows)
    for c in stores:
        c.wait()


def first_places(tab):
    return tab[:8]


def places_of(tab, blocks, slots):
    place = lax.broadcasted_iota(jnp.int32, (2 * slots, LANES), 0)
    same = tab[8 : 8 + 2 * slots] == blocks[:1]
    return jnp.min(jnp.where(same, place, 2 * slots), axis=0, keepdims=True)


def start_taking(source, table, taken, sems):
    slots, _, blk = taken.shape
    copies = []
    for k in range(slots):
        begin = pl.multiple_of(table[k] * blk, blk)
        copies.append(pltpu.make_async_copy(source.at[:, pl.ds(begin, blk)], taken.at[k], sems.at[k]))
        copies[-1].start()
    return copies


def cotangent_kernel(
    c0, c1, c2, c3, tokens, grad_out, w1, w2, message, taken_t, cot, hid, back, tab, row, place_of, taken, sems
):
    slots, rows, blk = cot.shape
    copies = start_taking(grad_out, c3, cot, sems.at[0])
    copies_t = start_taking(tokens, c0, taken, sems.at[1])

    @pl.loop(0, place_of.shape[0])
    def _(block):
        place_of[block] = 2 * slots

    lane = lax.broadcasted_iota(jnp.int32, (8, LANES), 1)
    firsts = jnp.zeros((8, LANES), jnp.int32)
    for j in range(2 * slots):
        block = c1[j] if j < slots else c2[j - slots]
        place = jnp.minimum(place_of[block], j)
        place_of[block] = place
        firsts = jnp.where(lane == j, place, firsts)
        tab[8 + j : 9 + j, :] = jnp.full((1, LANES), block, jnp.int32)
    tab[:8] = firsts
    row[...] = table_row((c0, c1, c2, c3), slots)
    hid[...] = jnp.zeros(hid.shape, f32)
    back[...] = jnp.zeros(back.shape, f32)
    for k in range(slots):
        copies[k].wait()
        value = dot(cot[k], w2[k], (1, 1))
        message[k * rows : (k + 1) * rows, :] = value.astype(bf16)
        at = jnp.minimum(place_of[c2[k]], slots)
        back[at] = back[at] + value
    for k in range(slots):
        copies_t[k].wait()
        at = place_of[c1[k]]
        hid[at] = hid[at] + dot(taken[k], w1[k], (1, 0))
        taken_t[k] = taken[k].T


def add_peers(acc, own, numbers_at, peers, slots):
    count, rows, _ = acc.shape
    for j in range(count):
        acc[j] = own[j]
    for numbers_of, ref in zip(numbers_at, peers):
        for k, at in enumerate(numbers_of):

            @pl.when(at < count)
            def _():
                acc[at] = acc[at] + ref[k * rows : (k + 1) * rows, :].astype(f32)


def hidden_kernel(dims, tab, own, *refs):
    slots, n_row, n_col, n_tok = dims
    peers, refs = refs[: n_row - 1], refs[n_row - 1 :]
    cot, active, hid, places, grad, half = refs
    rows = half.shape[0] // slots
    begin = pl.multiple_of((1 - lax.div(lax.axis_index("tok"), max(1, n_tok // 2))) * rows, rows)
    found = [places_of(tab, numbers(ref, slots * cot.shape[1]), slots) for ref in peers]
    places[...] = jnp.zeros(places.shape, jnp.int32)
    for i, place in enumerate(found):
        places[8 * i : 8 * i + 8] = jnp.broadcast_to(place, (8, LANES))
    at = [[place[0, W1_COL * slots + k] for k in range(slots)] for place in found]
    firsts = first_places(tab)
    firsts = [firsts[0, slots + k] for k in range(slots)]
    add_peers(hid, own, at, peers, slots)
    for k in range(slots):
        h = hid[firsts[k]]
        active[k] = (h * cdf(h)).astype(bf16)
        grad[k] = dot(active[k], cot[k], (0, 0))
        if n_tok > 1:
            half[k * rows : (k + 1) * rows, :] = grad[k, pl.ds(begin, rows), :].astype(bf16)


def slope_kernel(dims, tab, row, active, hid, w2, slope, *refs):
    slots, n_row, n_col, n_tok = dims
    outs, value = refs[:n_col], refs[n_col]
    for k in range(slots):
        value[k] = dot(active[k], w2[k], (1, 0))
        cut(value.at[k], outs, k, "col")
    for ref in outs:
        ref[ref.shape[0] - 16 :, :] = row[...]
    firsts = first_places(tab)
    for k in range(slots):
        h = hid[firsts[0, k]]
        slope[k] = cdf(h) + h * jnp.exp(-0.5 * h * h) * (1.0 / math.sqrt(2.0 * math.pi))


def back_kernel(dims, tab, places, own, *refs):
    slots, n_row, n_col, n_tok = dims
    peers, refs = refs[: n_row - 1], refs[n_row - 1 :]
    slope, w1, taken_t = refs[:3]
    refs = refs[3:]
    outs, refs = refs[:n_col], refs[n_col:]
    grads, (acc, value, grad) = refs[:n_tok], refs[n_tok:]
    found = [places[8 * i : 8 * i + 8] for i in range(len(peers))]
    at = [[place[0, W2_HID * slots + k] for k in range(slots)] for place in found]
    firsts = first_places(tab)
    firsts = [firsts[0, k] for k in range(slots)]
    add_peers(acc, own, at, peers, slots)
    for k in range(slots):
        g = (acc[firsts[k]] * slope[k]).astype(bf16)
        grad[k] = dot(taken_t[k], g, (1, 0))
        cut(grad.at[k], grads, k, "tok")
        value[k] = dot(g, w1[k], (1, 1))
        cut(value.at[k], outs, k, "col")
    for ref in grads:
        rows = slots * grad.shape[1] // n_tok
        if ref.shape[0] > rows:
            ref[rows:, :] = jnp.zeros((ref.shape[0] - rows, LANES), bf16)


def join_kernel(dims, grad2, half, *refs):
    slots, n_row, n_col, n_tok = dims
    side = max(1, n_tok // 2)
    part = grad2.shape[1] // n_tok
    shares, joined = refs[:side], refs[-side:]
    for d in range(side):
        to = target("tok", d)
        begin = pl.multiple_of(to * part, part)
        size = shares[d].shape[0]
        joined[d][:size, :] = shares[d][...]
        for k in range(slots):
            total = grad2[k, pl.ds(begin, part), :]
            if n_tok > 1:
                there = pl.multiple_of(k * side * part + lax.rem(to, side) * part, part)
                total = total + half[pl.ds(there, part), :].astype(f32)
            joined[d][size + k * part : size + (k + 1) * part, :] = total.astype(bf16)


def add_shares(parts, result, first):
    part = result.shape[1]
    for k in range(result.shape[0]):
        here = slice((first + k) * part, (first + k + 1) * part)
        result[k] = sum(ref[here, :].astype(f32) for ref in parts)


def place_shares(shares, tables, acc):
    slots = len(tables[0])
    share = acc.shape[1]
    acc[...] = jnp.zeros(acc.shape, f32)
    for ref, table in zip(shares, tables):
        for k in range(slots):
            acc[table[k]] = acc[table[k]] + ref[k * share : (k + 1) * share, :].astype(f32)


def store_rows(acc, result, output, sem):
    blk = acc.shape[-1]
    for b in range(acc.shape[0]):
        result[:, b * blk : (b + 1) * blk] = acc[b].astype(bf16)
    copy = pltpu.make_async_copy(result, output, sem)
    copy.start()
    return copy


def tables_of(parts, rows, which, slots):
    return [[table[0, which * slots + k] for k in range(slots)] for table in [numbers(ref, rows) for ref in parts]]


def output_kernel(dims, *refs):
    slots, n_row, n_col, n_tok = dims
    parts, (output, last, result, acc, sem) = refs[:n_col], refs[n_col:]
    rows = slots * acc.shape[1]
    last[...] = jnp.zeros(last.shape, jnp.int32)
    place_shares(parts, tables_of(parts, rows, W2_OUT, slots), acc)
    store_rows(acc, result, output, sem).wait()


def input_kernel(dims, after, sum1, sum2, *refs):
    del after
    slots, n_row, n_col, n_tok = dims
    outs, backs, refs = refs[:n_col], refs[n_col : 2 * n_col], refs[2 * n_col :]
    grad_in, gw1, gw2, result, acc, sems = refs
    stores = [pltpu.make_async_copy(sum1, gw1, sems.at[0]), pltpu.make_async_copy(sum2, gw2, sems.at[1])]
    for c in stores:
        c.start()
    rows = slots * acc.shape[1]
    place_shares(backs, tables_of(outs, rows, W1_ROW, slots), acc)
    stores.append(store_rows(acc, result, grad_in, sems.at[2]))
    for c in stores:
        c.wait()


def grad_kernel(*refs):
    parts, gw1, gw2 = refs[:-2], refs[-2], refs[-1]
    slots, part, _ = gw1.shape
    add_shares(parts, gw1, 0)
    add_shares([ref for ref in parts if ref.shape[0] == 2 * slots * part], gw2, slots)


def near_last(n):
    return [0] + list(range(2, n)) + [1][: n - 1]


def shards(tokens, w1_blocks, w1_rows, w1_cols, w2_blocks, w2_hidden, w2_outs, grad_out):
    slots, blk = w1_blocks.shape[2], w1_blocks.shape[-1]
    rows = tokens.shape[0]
    n_row, n_col, n_tok = (lax.axis_size(a) for a in ("row", "col", "tok"))
    dims = (slots, n_row, n_col, n_tok)
    row_blocks = tokens.shape[1] // blk
    col_blocks = FF // n_col // blk
    share, part = rows // n_col, blk // n_tok
    w1 = w1_blocks.reshape(slots, blk, blk)
    w2 = w2_blocks.reshape(slots, blk, blk)
    tables = [t.reshape(slots) for t in (w1_rows, w1_cols, w2_hidden, w2_outs)]

    S = jax.ShapeDtypeStruct
    message = S((slots * rows + 16, blk), bf16)
    wide, narrow = S((slots, rows, blk), f32), S((slots, rows, blk), bf16)

    p_send = call(
        token_kernel,
        "take_tokens",
        TAKE_LIMIT,
        out_shape=message,
        in_specs=[HBM] * 6,
        out_specs=HBM,
        scratch_shapes=[
            pltpu.VMEM(tokens.shape, bf16),
            pltpu.VMEM((slots, blk, blk), bf16),
            pltpu.VMEM((slots * rows + 16, blk), bf16),
        ]
        + [pltpu.SMEM((slots,), jnp.int32)] * 4
        + [pltpu.SemaphoreType.DMA((7 + slots,))],
    )(*tables, tokens, w1)
    p_peers = [send(p_send, "row", d) for d in range(1, n_row)]

    b_send, taken_t, cot, hid, back, tab, row = call(
        cotangent_kernel,
        "take_cotangent",
        out_shape=(
            S((slots * rows, blk), bf16),
            S((slots, blk, rows), bf16),
            narrow,
            S((2 * slots, rows, blk), f32),
            S((slots + 1, rows, blk), f32),
            S((8 + 2 * slots, LANES), jnp.int32),
            S((16, LANES), bf16),
        ),
        in_specs=[SMEM] * 4 + [HBM, HBM] + [VMEM] * 2,
        out_specs=(VMEM,) * 7,
        scratch_shapes=[
            pltpu.SMEM((col_blocks,), jnp.int32),
            pltpu.VMEM((slots, rows, blk), bf16),
            pltpu.SemaphoreType.DMA((2, slots)),
        ],
    )(*tables, tokens, grad_out, w1, w2)
    b_peers = [send(b_send, "row", d) for d in range(1, n_row)]

    single = S((slots * part, blk), bf16)
    side = max(1, n_tok // 2)
    spare = [16, 16]
    grads = tuple(single if d < side else S((slots * part + spare[d % 2], blk), bf16) for d in range(n_tok))
    half = S((slots * side * part, blk), bf16)
    peer_rows = 8 * max(1, n_row - 1)
    active, hid, places, grad2, half = call(
        functools.partial(hidden_kernel, dims),
        "hidden",
        out_shape=(
            narrow,
            S((2 * slots, rows, blk), f32),
            S((peer_rows, LANES), jnp.int32),
            S((slots, blk, blk), f32),
            half,
        ),
        in_specs=[VMEM] * (n_row + 2),
        out_specs=(VMEM,) * 5,
    )(tab, hid, *p_peers, cot)
    if n_tok > 1:
        half = lax.ppermute(half, "tok", [(i, (i + side) % n_tok) for i in range(n_tok)])
    out_share, back_share = S((slots * share + 16, blk), bf16), S((slots * share, blk), bf16)
    slope, *o_sent = call(
        functools.partial(slope_kernel, dims),
        "slope",
        out_shape=(wide,) + (out_share,) * n_col,
        in_specs=[VMEM] * 5,
        out_specs=(VMEM,) * (1 + n_col),
        scratch_shapes=[pltpu.VMEM((slots, rows, blk), f32)],
    )(tab, row, active, hid, w2)
    o_parts = [send(o_sent[d], "col", d) for d in near_last(n_col)]

    sent = call(
        functools.partial(back_kernel, dims),
        "back",
        out_shape=(back_share,) * n_col + grads,
        in_specs=[VMEM] * (n_row + 5),
        out_specs=(VMEM,) * (n_col + n_tok),
        scratch_shapes=[
            pltpu.VMEM((slots, rows, blk), f32),
            pltpu.VMEM((slots, rows, blk), f32),
            pltpu.VMEM((slots, blk, blk), f32),
        ],
    )(tab, places, back, *b_peers, slope, w1, taken_t)
    i_sent, g_sent = list(sent[:n_col]), list(sent[n_col:])
    early = o_parts[1:]
    g_sent[:side] = call(
        functools.partial(join_kernel, dims),
        "join_shares",
        out_shape=(S((2 * slots * part, blk), bf16),) * side,
        in_specs=[VMEM] * (2 + side) + [ANY] * len(early),
        out_specs=(VMEM,) * side,
    )(grad2, half, *g_sent[:side], *early)
    i_parts = [send(i_sent[d], "col", d) for d in near_last(n_col)]
    tok_parts = [send(g_sent[d], "tok", d) for d in range(n_tok)]

    result = S((share, row_blocks * blk), bf16)
    summed = S((slots, part, blk), f32)
    acc = pltpu.VMEM((row_blocks, share, blk), f32)
    summed = S((slots, part, blk), f32)
    sums = call(
        grad_kernel,
        "add_grads",
        out_shape=(summed, summed),
        in_specs=[VMEM] * n_tok,
        out_specs=(VMEM,) * 2,
    )(*tok_parts[:1], *tok_parts[2:], *tok_parts[1:2])
    output, last = call(
        functools.partial(output_kernel, dims),
        "add_outputs",
        out_shape=(result, S((8, LANES), jnp.int32)),
        in_specs=[VMEM] * n_col,
        out_specs=(HBM, VMEM),
        scratch_shapes=[pltpu.VMEM(result.shape, bf16), acc, pltpu.SemaphoreType.DMA],
    )(*o_parts)
    grad_in, gw1, gw2 = call(
        functools.partial(input_kernel, dims),
        "add_inputs",
        out_shape=(result, summed, summed),
        in_specs=[ANY] + [VMEM] * len([*sums, *o_parts, *i_parts]),
        out_specs=(HBM,) * 3,
        scratch_shapes=[pltpu.VMEM(result.shape, bf16), acc, pltpu.SemaphoreType.DMA((3,))],
    )(last, *sums, *o_parts, *i_parts)
    return (output, grad_in, gw1.reshape(1, 1, slots, part, blk), gw2.reshape(1, 1, slots, part, blk))


def solution(mesh):
    placed = (
        P("tok", "row"),
        P("row", "col", None, None, None),
        P("row", "col", None),
        P("row", "col", None),
        P("row", "col", None, None, None),
        P("row", "col", None),
        P("row", "col", None),
        P("tok", "row"),
    )
    return jax.shard_map(
        shards,
        mesh=mesh,
        in_specs=placed,
        out_specs=(
            P(("tok", "col"), "row"),
            P(("tok", "col"), "row"),
            P("row", "col", None, "tok", None),
            P("row", "col", None, "tok", None),
        ),
        check_vma=False,
    )
```

```python
import functools
import math

import jax
import jax.numpy as jnp
from jax import lax
from jax.experimental import pallas as pl
from jax.experimental.pallas import tpu as pltpu
from jax.sharding import PartitionSpec as P

FF = 32768
LANES = 128
f32 = jnp.float32
bf16 = jnp.bfloat16
VMEM = pl.BlockSpec(memory_space=pltpu.VMEM)
SMEM = pl.BlockSpec(memory_space=pltpu.SMEM)
ANY = pl.BlockSpec(memory_space=pl.ANY)
HBM = pl.BlockSpec(memory_space=pltpu.HBM)
TAKE_LIMIT = 62 * 1024 * 1024
LIMIT = 32 * 1024 * 1024

W1_ROW, W1_COL, W2_HID, W2_OUT = range(4)


def call(kernel, name, limit=LIMIT, **kwargs):
    return pl.pallas_call(
        kernel,
        name=name,
        compiler_params=pltpu.CompilerParams(vmem_limit_bytes=limit),
        cost_estimate=pl.CostEstimate(flops=1 << 25, bytes_accessed=1 << 19, transcendentals=0),
        **kwargs,
    )


def dot(a, b, contract):
    return lax.dot_general(a, b, ((contract[:1], contract[1:]), ((), ())), preferred_element_type=f32)


def cdf(v):
    return 0.5 * (1.0 + lax.erf(v * math.sqrt(0.5)))


def partner(i, d, n):
    return i ^ d if n & (n - 1) == 0 else (i + d) % n


def target(axis, d):
    n = lax.axis_size(axis)
    me = lax.axis_index(axis)
    return jnp.bitwise_xor(me, d) if n & (n - 1) == 0 else lax.rem(me + d, n)


def send(x, axis, d):
    n = lax.axis_size(axis)
    return lax.ppermute(x, axis, [(i, partner(i, d, n)) for i in range(n)]) if d else x


def cut(value, refs, k, axis):
    share = value.shape[0] // len(refs)
    for d, ref in enumerate(refs):
        begin = pl.multiple_of(target(axis, d) * share, share)
        ref[k * share : (k + 1) * share, :] = value[pl.ds(begin, share), :].astype(ref.dtype)


def table_row(tables, slots):
    lane = lax.broadcasted_iota(jnp.int32, (16, LANES), 1)
    row = jnp.zeros((16, LANES), f32)
    for which, table in enumerate(tables):
        for k in range(slots):
            row = jnp.where(lane == which * slots + k, table[k].astype(f32), row)
    return row.astype(bf16)


def numbers(ref, rows):
    return ref[rows : rows + 16, :].astype(f32)[:8].astype(jnp.int32)


def token_kernel(t0, t1, t2, t3, tokens, w1, message, tokens_v, w_v, sent, c0, c1, c2, c3, sems):
    slots, blk, _ = w_v.shape
    rows = tokens_v.shape[0]
    tables = (c0, c1, c2, c3)
    loads = [pltpu.make_async_copy(t, c, sems.at[i]) for i, (t, c) in enumerate(zip((t0, t1, t2, t3), tables))]
    loads.append(pltpu.make_async_copy(tokens, tokens_v, sems.at[4]))
    loads.append(pltpu.make_async_copy(w1, w_v, sems.at[5]))
    stores = []

    def store(begin, size):
        here = pl.ds(begin, size)
        stores.append(pltpu.make_async_copy(sent.at[here], message.at[here], sems.at[6 + len(stores)]))
        stores[-1].start()

    for c in loads:
        c.start()
    for c in loads[:4]:
        c.wait()
    sent[slots * rows :, :] = table_row(tables, slots)
    store(slots * rows, 16)
    for c in loads[4:]:
        c.wait()
    for k in range(slots):
        here = pl.ds(pl.multiple_of(c0[k] * blk, blk), blk)
        sent[k * rows : (k + 1) * rows, :] = dot(tokens_v[:, here], w_v[k], (1, 0)).astype(bf16)
        store(k * rows, rows)
    for c in stores:
        c.wait()


def first_places(tab):
    return tab[:8]


def places_of(tab, blocks, slots):
    place = lax.broadcasted_iota(jnp.int32, (2 * slots, LANES), 0)
    same = tab[8 : 8 + 2 * slots] == blocks[:1]
    return jnp.min(jnp.where(same, place, 2 * slots), axis=0, keepdims=True)


def start_taking(source, table, taken, sems):
    slots, _, blk = taken.shape
    copies = []
    for k in range(slots):
        begin = pl.multiple_of(table[k] * blk, blk)
        copies.append(pltpu.make_async_copy(source.at[:, pl.ds(begin, blk)], taken.at[k], sems.at[k]))
        copies[-1].start()
    return copies


def cotangent_kernel(
    c0, c1, c2, c3, tokens, grad_out, w1, w2, message, taken_t, cot, hid, back, tab, row, place_of, taken, sems
):
    slots, rows, blk = cot.shape
    copies = start_taking(grad_out, c3, cot, sems.at[0])
    copies_t = start_taking(tokens, c0, taken, sems.at[1])

    @pl.loop(0, place_of.shape[0])
    def _(block):
        place_of[block] = 2 * slots

    lane = lax.broadcasted_iota(jnp.int32, (8, LANES), 1)
    firsts = jnp.zeros((8, LANES), jnp.int32)
    for j in range(2 * slots):
        block = c1[j] if j < slots else c2[j - slots]
        place = jnp.minimum(place_of[block], j)
        place_of[block] = place
        firsts = jnp.where(lane == j, place, firsts)
        tab[8 + j : 9 + j, :] = jnp.full((1, LANES), block, jnp.int32)
    tab[:8] = firsts
    row[...] = table_row((c0, c1, c2, c3), slots)
    hid[...] = jnp.zeros(hid.shape, f32)
    back[...] = jnp.zeros(back.shape, f32)
    for k in range(slots):
        copies[k].wait()
        value = dot(cot[k], w2[k], (1, 1))
        message[k * rows : (k + 1) * rows, :] = value.astype(bf16)
        at = jnp.minimum(place_of[c2[k]], slots)
        back[at] = back[at] + value
    for k in range(slots):
        copies_t[k].wait()
        at = place_of[c1[k]]
        hid[at] = hid[at] + dot(taken[k], w1[k], (1, 0))
        taken_t[k] = taken[k].T


def add_peers(acc, own, numbers_at, peers, slots):
    count, rows, _ = acc.shape
    for j in range(count):
        acc[j] = own[j]
    for numbers_of, ref in zip(numbers_at, peers):
        for k, at in enumerate(numbers_of):

            @pl.when(at < count)
            def _():
                acc[at] = acc[at] + ref[k * rows : (k + 1) * rows, :].astype(f32)


def hidden_kernel(dims, tab, own, *refs):
    slots, n_row, n_col, n_tok = dims
    peers, refs = refs[: n_row - 1], refs[n_row - 1 :]
    cot, active, hid, places, grad, half = refs
    rows = half.shape[0] // slots
    begin = pl.multiple_of((1 - lax.div(lax.axis_index("tok"), max(1, n_tok // 2))) * rows, rows)
    found = [places_of(tab, numbers(ref, slots * cot.shape[1]), slots) for ref in peers]
    places[...] = jnp.zeros(places.shape, jnp.int32)
    for i, place in enumerate(found):
        places[8 * i : 8 * i + 8] = jnp.broadcast_to(place, (8, LANES))
    at = [[place[0, W1_COL * slots + k] for k in range(slots)] for place in found]
    firsts = first_places(tab)
    firsts = [firsts[0, slots + k] for k in range(slots)]
    add_peers(hid, own, at, peers, slots)
    for k in range(slots):
        h = hid[firsts[k]]
        active[k] = (h * cdf(h)).astype(bf16)
        grad[k] = dot(active[k], cot[k], (0, 0))
        if n_tok > 1:
            half[k * rows : (k + 1) * rows, :] = grad[k, pl.ds(begin, rows), :].astype(bf16)


def slope_kernel(dims, tab, row, active, hid, w2, slope, *refs):
    slots, n_row, n_col, n_tok = dims
    outs, value = refs[:n_col], refs[n_col]
    for k in range(slots):
        value[k] = dot(active[k], w2[k], (1, 0))
        cut(value.at[k], outs, k, "col")
    for ref in outs:
        ref[ref.shape[0] - 16 :, :] = row[...]
    firsts = first_places(tab)
    for k in range(slots):
        h = hid[firsts[0, k]]
        slope[k] = cdf(h) + h * jnp.exp(-0.5 * h * h) * (1.0 / math.sqrt(2.0 * math.pi))


def back_kernel(dims, tab, places, own, *refs):
    slots, n_row, n_col, n_tok = dims
    peers, refs = refs[: n_row - 1], refs[n_row - 1 :]
    slope, w1, taken_t = refs[:3]
    refs = refs[3:]
    outs, refs = refs[:n_col], refs[n_col:]
    grads, (acc, value, grad) = refs[:n_tok], refs[n_tok:]
    found = [places[8 * i : 8 * i + 8] for i in range(len(peers))]
    at = [[place[0, W2_HID * slots + k] for k in range(slots)] for place in found]
    firsts = first_places(tab)
    firsts = [firsts[0, k] for k in range(slots)]
    add_peers(acc, own, at, peers, slots)
    for k in range(slots):
        g = (acc[firsts[k]] * slope[k]).astype(bf16)
        grad[k] = dot(taken_t[k], g, (1, 0))
        cut(grad.at[k], grads, k, "tok")
        value[k] = dot(g, w1[k], (1, 1))
        cut(value.at[k], outs, k, "col")


def pair_kernel(dims, grad2, half, *refs):
    slots, n_row, n_col, n_tok = dims
    side = max(1, n_tok // 2)
    part = grad2.shape[1] // n_tok
    for d, ref in enumerate(refs[-side:]):
        to = target("tok", d)
        begin = pl.multiple_of(to * part, part)
        for k in range(slots):
            total = grad2[k, pl.ds(begin, part), :]
            if n_tok > 1:
                there = pl.multiple_of(k * side * part + lax.rem(to, side) * part, part)
                total = total + half[pl.ds(there, part), :].astype(f32)
            ref[k * part : (k + 1) * part, :] = total.astype(bf16)


def add_shares(parts, result):
    part = result.shape[1]
    for k in range(result.shape[0]):
        result[k] = sum(ref[k * part : (k + 1) * part, :].astype(f32) for ref in parts)


def place_shares(shares, tables, acc):
    slots = len(tables[0])
    share = acc.shape[1]
    acc[...] = jnp.zeros(acc.shape, f32)
    for ref, table in zip(shares, tables):
        for k in range(slots):
            acc[table[k]] = acc[table[k]] + ref[k * share : (k + 1) * share, :].astype(f32)


def store_rows(acc, result, output, sem):
    blk = acc.shape[-1]
    for b in range(acc.shape[0]):
        result[:, b * blk : (b + 1) * blk] = acc[b].astype(bf16)
    copy = pltpu.make_async_copy(result, output, sem)
    copy.start()
    return copy


def tables_of(parts, rows, which, slots):
    return [[table[0, which * slots + k] for k in range(slots)] for table in [numbers(ref, rows) for ref in parts]]


def output_kernel(dims, *refs):
    slots, n_row, n_col, n_tok = dims
    parts, (output, last, result, acc, sem) = refs[:n_col], refs[n_col + 1 :]
    rows = slots * acc.shape[1]
    last[...] = jnp.zeros(last.shape, jnp.int32)
    place_shares(parts, tables_of(parts, rows, W2_OUT, slots), acc)
    store_rows(acc, result, output, sem).wait()


def input_kernel(dims, after, sum1, sum2, *refs):
    del after
    slots, n_row, n_col, n_tok = dims
    outs, backs, refs = refs[:n_col], refs[n_col : 2 * n_col], refs[2 * n_col :]
    grad_in, gw1, gw2, result, acc, sems = refs
    stores = [pltpu.make_async_copy(sum1, gw1, sems.at[0]), pltpu.make_async_copy(sum2, gw2, sems.at[1])]
    for c in stores:
        c.start()
    rows = slots * acc.shape[1]
    place_shares(backs, tables_of(outs, rows, W1_ROW, slots), acc)
    stores.append(store_rows(acc, result, grad_in, sems.at[2]))
    for c in stores:
        c.wait()


def grad_kernel(side, *refs):
    add_shares(refs[:side], refs[-1])
    add_shares(refs[side:-2], refs[-2])


def near_last(n):
    return [0] + list(range(2, n)) + [1][: n - 1]


def shards(tokens, w1_blocks, w1_rows, w1_cols, w2_blocks, w2_hidden, w2_outs, grad_out):
    slots, blk = w1_blocks.shape[2], w1_blocks.shape[-1]
    rows = tokens.shape[0]
    n_row, n_col, n_tok = (lax.axis_size(a) for a in ("row", "col", "tok"))
    dims = (slots, n_row, n_col, n_tok)
    row_blocks = tokens.shape[1] // blk
    col_blocks = FF // n_col // blk
    share, part = rows // n_col, blk // n_tok
    w1 = w1_blocks.reshape(slots, blk, blk)
    w2 = w2_blocks.reshape(slots, blk, blk)
    tables = [t.reshape(slots) for t in (w1_rows, w1_cols, w2_hidden, w2_outs)]

    S = jax.ShapeDtypeStruct
    message = S((slots * rows + 16, blk), bf16)
    wide, narrow = S((slots, rows, blk), f32), S((slots, rows, blk), bf16)

    p_send = call(
        token_kernel,
        "take_tokens",
        TAKE_LIMIT,
        out_shape=message,
        in_specs=[HBM] * 6,
        out_specs=HBM,
        scratch_shapes=[
            pltpu.VMEM(tokens.shape, bf16),
            pltpu.VMEM((slots, blk, blk), bf16),
            pltpu.VMEM((slots * rows + 16, blk), bf16),
        ]
        + [pltpu.SMEM((slots,), jnp.int32)] * 4
        + [pltpu.SemaphoreType.DMA((7 + slots,))],
    )(*tables, tokens, w1)
    p_peers = [send(p_send, "row", d) for d in range(1, n_row)]

    b_send, taken_t, cot, hid, back, tab, row = call(
        cotangent_kernel,
        "take_cotangent",
        out_shape=(
            S((slots * rows, blk), bf16),
            S((slots, blk, rows), bf16),
            narrow,
            S((2 * slots, rows, blk), f32),
            S((slots + 1, rows, blk), f32),
            S((8 + 2 * slots, LANES), jnp.int32),
            S((16, LANES), bf16),
        ),
        in_specs=[SMEM] * 4 + [HBM, HBM] + [VMEM] * 2,
        out_specs=(VMEM,) * 7,
        scratch_shapes=[
            pltpu.SMEM((col_blocks,), jnp.int32),
            pltpu.VMEM((slots, rows, blk), bf16),
            pltpu.SemaphoreType.DMA((2, slots)),
        ],
    )(*tables, tokens, grad_out, w1, w2)
    b_peers = [send(b_send, "row", d) for d in range(1, n_row)]

    single = S((slots * part, blk), bf16)
    side = max(1, n_tok // 2)
    grads = (single,) * n_tok
    half = S((slots * side * part, blk), bf16)
    peer_rows = 8 * max(1, n_row - 1)
    active, hid, places, grad2, half = call(
        functools.partial(hidden_kernel, dims),
        "hidden",
        out_shape=(
            narrow,
            S((2 * slots, rows, blk), f32),
            S((peer_rows, LANES), jnp.int32),
            S((slots, blk, blk), f32),
            half,
        ),
        in_specs=[VMEM] * (n_row + 2),
        out_specs=(VMEM,) * 5,
    )(tab, hid, *p_peers, cot)
    if n_tok > 1:
        half = lax.ppermute(half, "tok", [(i, (i + side) % n_tok) for i in range(n_tok)])
    out_share, back_share = S((slots * share + 16, blk), bf16), S((slots * share, blk), bf16)
    slope, *o_sent = call(
        functools.partial(slope_kernel, dims),
        "slope",
        out_shape=(wide,) + (out_share,) * n_col,
        in_specs=[VMEM] * 5,
        out_specs=(VMEM,) * (1 + n_col),
        scratch_shapes=[pltpu.VMEM((slots, rows, blk), f32)],
    )(tab, row, active, hid, w2)
    o_parts = [send(o_sent[d], "col", d) for d in near_last(n_col)]

    sent = call(
        functools.partial(back_kernel, dims),
        "back",
        out_shape=(back_share,) * n_col + grads,
        in_specs=[VMEM] * (n_row + 5),
        out_specs=(VMEM,) * (n_col + n_tok),
        scratch_shapes=[
            pltpu.VMEM((slots, rows, blk), f32),
            pltpu.VMEM((slots, rows, blk), f32),
            pltpu.VMEM((slots, blk, blk), f32),
        ],
    )(tab, places, back, *b_peers, slope, w1, taken_t)
    i_sent, g_sent = list(sent[:n_col]), list(sent[n_col:])
    early = o_parts[1:]
    g2_sent = call(
        functools.partial(pair_kernel, dims),
        "add_pairs",
        out_shape=(single,) * side,
        in_specs=[VMEM] * 2 + [ANY] * len(early),
        out_specs=(VMEM,) * side,
    )(grad2, half, *early)
    i_parts = [send(i_sent[d], "col", d) for d in near_last(n_col)]
    tok_parts = [send(g_sent[d], "tok", d) for d in range(n_tok)]
    g2_parts = [send(g2_sent[d], "tok", d) for d in range(side)]

    result = S((share, row_blocks * blk), bf16)
    summed = S((slots, part, blk), f32)
    acc = pltpu.VMEM((row_blocks, share, blk), f32)
    summed = S((slots, part, blk), f32)
    sums = call(
        functools.partial(grad_kernel, side),
        "add_grads",
        out_shape=(summed, summed),
        in_specs=[VMEM] * (side + n_tok),
        out_specs=(VMEM,) * 2,
    )(*g2_parts, *tok_parts[:1], *tok_parts[2:], *tok_parts[1:2])
    output, last = call(
        functools.partial(output_kernel, dims),
        "add_outputs",
        out_shape=(result, S((8, LANES), jnp.int32)),
        in_specs=[VMEM] * n_col + [ANY] * 1,
        out_specs=(HBM, VMEM),
        scratch_shapes=[pltpu.VMEM(result.shape, bf16), acc, pltpu.SemaphoreType.DMA],
    )(*o_parts, i_parts[1])
    grad_in, gw1, gw2 = call(
        functools.partial(input_kernel, dims),
        "add_inputs",
        out_shape=(result, summed, summed),
        in_specs=[ANY] + [VMEM] * len([*sums, *o_parts, *i_parts]),
        out_specs=(HBM,) * 3,
        scratch_shapes=[pltpu.VMEM(result.shape, bf16), acc, pltpu.SemaphoreType.DMA((3,))],
    )(last, *sums, *o_parts, *i_parts)
    return (output, grad_in, gw1.reshape(1, 1, slots, part, blk), gw2.reshape(1, 1, slots, part, blk))


def solution(mesh):
    placed = (
        P("tok", "row"),
        P("row", "col", None, None, None),
        P("row", "col", None),
        P("row", "col", None),
        P("row", "col", None, None, None),
        P("row", "col", None),
        P("row", "col", None),
        P("tok", "row"),
    )
    return jax.shard_map(
        shards,
        mesh=mesh,
        in_specs=placed,
        out_specs=(
            P(("tok", "col"), "row"),
            P(("tok", "col"), "row"),
            P("row", "col", None, "tok", None),
            P("row", "col", None, "tok", None),
        ),
        check_vma=False,
    )
```

```python
import functools
import math

import jax
import jax.numpy as jnp
from jax import lax
from jax.experimental import pallas as pl
from jax.experimental.pallas import tpu as pltpu
from jax.sharding import PartitionSpec as P

FF = 32768
LANES = 128
f32 = jnp.float32
bf16 = jnp.bfloat16
VMEM = pl.BlockSpec(memory_space=pltpu.VMEM)
SMEM = pl.BlockSpec(memory_space=pltpu.SMEM)
ANY = pl.BlockSpec(memory_space=pl.ANY)
HBM = pl.BlockSpec(memory_space=pltpu.HBM)
TAKE_LIMIT = 62 * 1024 * 1024
LIMIT = 32 * 1024 * 1024

W1_ROW, W1_COL, W2_HID, W2_OUT = range(4)


def call(kernel, name, limit=LIMIT, **kwargs):
    return pl.pallas_call(
        kernel,
        name=name,
        compiler_params=pltpu.CompilerParams(vmem_limit_bytes=limit),
        cost_estimate=pl.CostEstimate(flops=1 << 25, bytes_accessed=1 << 19, transcendentals=0),
        **kwargs,
    )


def dot(a, b, contract):
    return lax.dot_general(a, b, ((contract[:1], contract[1:]), ((), ())), preferred_element_type=f32)


def cdf(v):
    return 0.5 * (1.0 + lax.erf(v * math.sqrt(0.5)))


def partner(i, d, n):
    return i ^ d if n & (n - 1) == 0 else (i + d) % n


def target(axis, d):
    n = lax.axis_size(axis)
    me = lax.axis_index(axis)
    return jnp.bitwise_xor(me, d) if n & (n - 1) == 0 else lax.rem(me + d, n)


def send(x, axis, d):
    n = lax.axis_size(axis)
    return lax.ppermute(x, axis, [(i, partner(i, d, n)) for i in range(n)]) if d else x


def cut(value, refs, k, axis):
    share = value.shape[0] // len(refs)
    for d, ref in enumerate(refs):
        begin = pl.multiple_of(target(axis, d) * share, share)
        ref[k * share : (k + 1) * share, :] = value[pl.ds(begin, share), :].astype(ref.dtype)


def table_row(tables, slots):
    lane = lax.broadcasted_iota(jnp.int32, (16, LANES), 1)
    row = jnp.zeros((16, LANES), f32)
    for which, table in enumerate(tables):
        for k in range(slots):
            row = jnp.where(lane == which * slots + k, table[k].astype(f32), row)
    return row.astype(bf16)


def numbers(ref, rows):
    return ref[rows : rows + 16, :].astype(f32)[:8].astype(jnp.int32)


def token_kernel(t0, t1, t2, t3, tokens, w1, message, tokens_v, w_v, sent, c0, c1, c2, c3, sems):
    slots, blk, _ = w_v.shape
    rows = tokens_v.shape[0]
    tables = (c0, c1, c2, c3)
    loads = [pltpu.make_async_copy(t, c, sems.at[i]) for i, (t, c) in enumerate(zip((t0, t1, t2, t3), tables))]
    loads.append(pltpu.make_async_copy(tokens, tokens_v, sems.at[4]))
    loads.append(pltpu.make_async_copy(w1, w_v, sems.at[5]))
    stores = []

    def store(begin, size):
        here = pl.ds(begin, size)
        stores.append(pltpu.make_async_copy(sent.at[here], message.at[here], sems.at[6 + len(stores)]))
        stores[-1].start()

    for c in loads:
        c.start()
    for c in loads[:4]:
        c.wait()
    sent[slots * rows :, :] = table_row(tables, slots)
    store(slots * rows, 16)
    for c in loads[4:]:
        c.wait()
    for k in range(slots):
        here = pl.ds(pl.multiple_of(c0[k] * blk, blk), blk)
        sent[k * rows : (k + 1) * rows, :] = dot(tokens_v[:, here], w_v[k], (1, 0)).astype(bf16)
        store(k * rows, rows)
    for c in stores:
        c.wait()


def first_places(tab):
    return tab[:8]


def places_of(tab, blocks, slots):
    place = lax.broadcasted_iota(jnp.int32, (2 * slots, LANES), 0)
    same = tab[8 : 8 + 2 * slots] == blocks[:1]
    return jnp.min(jnp.where(same, place, 2 * slots), axis=0, keepdims=True)


def start_taking(source, table, taken, sems):
    slots, _, blk = taken.shape
    copies = []
    for k in range(slots):
        begin = pl.multiple_of(table[k] * blk, blk)
        copies.append(pltpu.make_async_copy(source.at[:, pl.ds(begin, blk)], taken.at[k], sems.at[k]))
        copies[-1].start()
    return copies


def cotangent_kernel(
    c0, c1, c2, c3, tokens, grad_out, w1, w2, message, taken_t, cot, hid, back, tab, row, place_of, taken, sems
):
    slots, rows, blk = cot.shape
    copies = start_taking(grad_out, c3, cot, sems.at[0])
    copies_t = start_taking(tokens, c0, taken, sems.at[1])

    @pl.loop(0, place_of.shape[0])
    def _(block):
        place_of[block] = 2 * slots

    lane = lax.broadcasted_iota(jnp.int32, (8, LANES), 1)
    firsts = jnp.zeros((8, LANES), jnp.int32)
    for j in range(2 * slots):
        block = c1[j] if j < slots else c2[j - slots]
        place = jnp.minimum(place_of[block], j)
        place_of[block] = place
        firsts = jnp.where(lane == j, place, firsts)
        tab[8 + j : 9 + j, :] = jnp.full((1, LANES), block, jnp.int32)
    tab[:8] = firsts
    row[...] = table_row((c0, c1, c2, c3), slots)
    hid[...] = jnp.zeros(hid.shape, f32)
    back[...] = jnp.zeros(back.shape, f32)
    for k in range(slots):
        copies[k].wait()
        value = dot(cot[k], w2[k], (1, 1))
        message[k * rows : (k + 1) * rows, :] = value.astype(bf16)
        at = jnp.minimum(place_of[c2[k]], slots)
        back[at] = back[at] + value
    for k in range(slots):
        copies_t[k].wait()
        at = place_of[c1[k]]
        hid[at] = hid[at] + dot(taken[k], w1[k], (1, 0))
        taken_t[k] = taken[k].T


def add_peers(acc, own, numbers_at, peers, slots):
    count, rows, _ = acc.shape
    for j in range(count):
        acc[j] = own[j]
    for numbers_of, ref in zip(numbers_at, peers):
        for k, at in enumerate(numbers_of):

            @pl.when(at < count)
            def _():
                acc[at] = acc[at] + ref[k * rows : (k + 1) * rows, :].astype(f32)


def hidden_kernel(dims, tab, own, *refs):
    slots, n_row, n_col, n_tok = dims
    peers, refs = refs[: n_row - 1], refs[n_row - 1 :]
    cot, active, hid, places, grad, half = refs
    rows = half.shape[0] // slots
    begin = pl.multiple_of((1 - lax.div(lax.axis_index("tok"), max(1, n_tok // 2))) * rows, rows)
    found = [places_of(tab, numbers(ref, slots * cot.shape[1]), slots) for ref in peers]
    places[...] = jnp.zeros(places.shape, jnp.int32)
    for i, place in enumerate(found):
        places[8 * i : 8 * i + 8] = jnp.broadcast_to(place, (8, LANES))
    at = [[place[0, W1_COL * slots + k] for k in range(slots)] for place in found]
    firsts = first_places(tab)
    firsts = [firsts[0, slots + k] for k in range(slots)]
    add_peers(hid, own, at, peers, slots)
    for k in range(slots):
        h = hid[firsts[k]]
        active[k] = (h * cdf(h)).astype(bf16)
        grad[k] = dot(active[k], cot[k], (0, 0))
        if n_tok > 1:
            half[k * rows : (k + 1) * rows, :] = grad[k, pl.ds(begin, rows), :].astype(bf16)


def slope_kernel(dims, tab, row, active, hid, w2, slope, *refs):
    slots, n_row, n_col, n_tok = dims
    outs, value = refs[:n_col], refs[n_col]
    for k in range(slots):
        value[k] = dot(active[k], w2[k], (1, 0))
        cut(value.at[k], outs, k, "col")
    for ref in outs:
        ref[ref.shape[0] - 16 :, :] = row[...]
    firsts = first_places(tab)
    for k in range(slots):
        h = hid[firsts[0, k]]
        slope[k] = cdf(h) + h * jnp.exp(-0.5 * h * h) * (1.0 / math.sqrt(2.0 * math.pi))


def back_kernel(dims, tab, places, own, *refs):
    slots, n_row, n_col, n_tok = dims
    peers, refs = refs[: n_row - 1], refs[n_row - 1 :]
    slope, w1, taken_t = refs[:3]
    refs = refs[3:]
    outs, refs = refs[:n_col], refs[n_col:]
    grads, (acc, value, grad) = refs[:n_tok], refs[n_tok:]
    found = [places[8 * i : 8 * i + 8] for i in range(len(peers))]
    at = [[place[0, W2_HID * slots + k] for k in range(slots)] for place in found]
    firsts = first_places(tab)
    firsts = [firsts[0, k] for k in range(slots)]
    add_peers(acc, own, at, peers, slots)
    for k in range(slots):
        g = (acc[firsts[k]] * slope[k]).astype(bf16)
        grad[k] = dot(taken_t[k], g, (1, 0))
        cut(grad.at[k], grads, k, "tok")
        value[k] = dot(g, w1[k], (1, 1))
        cut(value.at[k], outs, k, "col")


def pair_kernel(dims, grad2, half, *refs):
    slots, n_row, n_col, n_tok = dims
    side = max(1, n_tok // 2)
    part = grad2.shape[1] // n_tok
    for d, ref in enumerate(refs[-side:]):
        to = target("tok", d)
        begin = pl.multiple_of(to * part, part)
        for k in range(slots):
            total = grad2[k, pl.ds(begin, part), :]
            if n_tok > 1:
                there = pl.multiple_of(k * side * part + lax.rem(to, side) * part, part)
                total = total + half[pl.ds(there, part), :].astype(f32)
            ref[k * part : (k + 1) * part, :] = total.astype(bf16)


def add_shares(parts, result):
    part = result.shape[1]
    for k in range(result.shape[0]):
        result[k] = sum(ref[k * part : (k + 1) * part, :].astype(f32) for ref in parts)


def place_shares(shares, tables, acc):
    slots = len(tables[0])
    share = acc.shape[1]
    acc[...] = jnp.zeros(acc.shape, f32)
    for ref, table in zip(shares, tables):
        for k in range(slots):
            acc[table[k]] = acc[table[k]] + ref[k * share : (k + 1) * share, :].astype(f32)


def store_rows(acc, result, output, sem):
    blk = acc.shape[-1]
    for b in range(acc.shape[0]):
        result[:, b * blk : (b + 1) * blk] = acc[b].astype(bf16)
    copy = pltpu.make_async_copy(result, output, sem)
    copy.start()
    return copy


def tables_of(parts, rows, which, slots):
    return [[table[0, which * slots + k] for k in range(slots)] for table in [numbers(ref, rows) for ref in parts]]


def output_kernel(dims, *refs):
    slots, n_row, n_col, n_tok = dims
    parts, (output, last, result, acc, sem) = refs[:n_col], refs[-5:]
    rows = slots * acc.shape[1]
    last[...] = jnp.zeros(last.shape, jnp.int32)
    place_shares(parts, tables_of(parts, rows, W2_OUT, slots), acc)
    store_rows(acc, result, output, sem).wait()


def input_kernel(dims, after, sum1, sum2, *refs):
    del after
    slots, n_row, n_col, n_tok = dims
    outs, backs, refs = refs[:n_col], refs[n_col : 2 * n_col], refs[2 * n_col :]
    grad_in, gw1, gw2, result, acc, sems = refs
    stores = [pltpu.make_async_copy(sum1, gw1, sems.at[0]), pltpu.make_async_copy(sum2, gw2, sems.at[1])]
    for c in stores:
        c.start()
    rows = slots * acc.shape[1]
    place_shares(backs, tables_of(outs, rows, W1_ROW, slots), acc)
    stores.append(store_rows(acc, result, grad_in, sems.at[2]))
    for c in stores:
        c.wait()


def grad_kernel(side, *refs):
    add_shares(refs[:side], refs[-1])
    add_shares(refs[side:-2], refs[-2])


def near_last(n):
    return [0] + list(range(2, n)) + [1][: n - 1]


def shards(tokens, w1_blocks, w1_rows, w1_cols, w2_blocks, w2_hidden, w2_outs, grad_out):
    slots, blk = w1_blocks.shape[2], w1_blocks.shape[-1]
    rows = tokens.shape[0]
    n_row, n_col, n_tok = (lax.axis_size(a) for a in ("row", "col", "tok"))
    dims = (slots, n_row, n_col, n_tok)
    row_blocks = tokens.shape[1] // blk
    col_blocks = FF // n_col // blk
    share, part = rows // n_col, blk // n_tok
    w1 = w1_blocks.reshape(slots, blk, blk)
    w2 = w2_blocks.reshape(slots, blk, blk)
    tables = [t.reshape(slots) for t in (w1_rows, w1_cols, w2_hidden, w2_outs)]

    S = jax.ShapeDtypeStruct
    message = S((slots * rows + 16, blk), bf16)
    wide, narrow = S((slots, rows, blk), f32), S((slots, rows, blk), bf16)

    p_send = call(
        token_kernel,
        "take_tokens",
        TAKE_LIMIT,
        out_shape=message,
        in_specs=[HBM] * 6,
        out_specs=HBM,
        scratch_shapes=[
            pltpu.VMEM(tokens.shape, bf16),
            pltpu.VMEM((slots, blk, blk), bf16),
            pltpu.VMEM((slots * rows + 16, blk), bf16),
        ]
        + [pltpu.SMEM((slots,), jnp.int32)] * 4
        + [pltpu.SemaphoreType.DMA((7 + slots,))],
    )(*tables, tokens, w1)
    p_peers = [send(p_send, "row", d) for d in range(1, n_row)]

    b_send, taken_t, cot, hid, back, tab, row = call(
        cotangent_kernel,
        "take_cotangent",
        out_shape=(
            S((slots * rows, blk), bf16),
            S((slots, blk, rows), bf16),
            narrow,
            S((2 * slots, rows, blk), f32),
            S((slots + 1, rows, blk), f32),
            S((8 + 2 * slots, LANES), jnp.int32),
            S((16, LANES), bf16),
        ),
        in_specs=[SMEM] * 4 + [HBM, HBM] + [VMEM] * 2,
        out_specs=(VMEM,) * 7,
        scratch_shapes=[
            pltpu.SMEM((col_blocks,), jnp.int32),
            pltpu.VMEM((slots, rows, blk), bf16),
            pltpu.SemaphoreType.DMA((2, slots)),
        ],
    )(*tables, tokens, grad_out, w1, w2)
    b_peers = [send(b_send, "row", d) for d in range(1, n_row)]

    single = S((slots * part, blk), bf16)
    side = max(1, n_tok // 2)
    grads = (single,) * n_tok
    half = S((slots * side * part, blk), bf16)
    peer_rows = 8 * max(1, n_row - 1)
    active, hid, places, grad2, half = call(
        functools.partial(hidden_kernel, dims),
        "hidden",
        out_shape=(
            narrow,
            S((2 * slots, rows, blk), f32),
            S((peer_rows, LANES), jnp.int32),
            S((slots, blk, blk), f32),
            half,
        ),
        in_specs=[VMEM] * (n_row + 2),
        out_specs=(VMEM,) * 5,
    )(tab, hid, *p_peers, cot)
    if n_tok > 1:
        half = lax.ppermute(half, "tok", [(i, (i + side) % n_tok) for i in range(n_tok)])
    out_share, back_share = S((slots * share + 16, blk), bf16), S((slots * share, blk), bf16)
    slope, *o_sent = call(
        functools.partial(slope_kernel, dims),
        "slope",
        out_shape=(wide,) + (out_share,) * n_col,
        in_specs=[VMEM] * 5,
        out_specs=(VMEM,) * (1 + n_col),
        scratch_shapes=[pltpu.VMEM((slots, rows, blk), f32)],
    )(tab, row, active, hid, w2)
    o_parts = [send(o_sent[d], "col", d) for d in near_last(n_col)]

    sent = call(
        functools.partial(back_kernel, dims),
        "back",
        out_shape=(back_share,) * n_col + grads,
        in_specs=[VMEM] * (n_row + 5),
        out_specs=(VMEM,) * (n_col + n_tok),
        scratch_shapes=[
            pltpu.VMEM((slots, rows, blk), f32),
            pltpu.VMEM((slots, rows, blk), f32),
            pltpu.VMEM((slots, blk, blk), f32),
        ],
    )(tab, places, back, *b_peers, slope, w1, taken_t)
    i_sent, g_sent = list(sent[:n_col]), list(sent[n_col:])
    early = o_parts[1:]
    g2_sent = call(
        functools.partial(pair_kernel, dims),
        "add_pairs",
        out_shape=(single,) * side,
        in_specs=[VMEM] * 2 + [ANY] * len(early),
        out_specs=(VMEM,) * side,
    )(grad2, half, *early)
    i_parts = [send(i_sent[d], "col", d) for d in near_last(n_col)]
    tok_parts = [send(g_sent[d], "tok", d) for d in range(n_tok)]
    g2_parts = [send(g2_sent[d], "tok", d) for d in range(side)]

    result = S((share, row_blocks * blk), bf16)
    summed = S((slots, part, blk), f32)
    acc = pltpu.VMEM((row_blocks, share, blk), f32)
    summed = S((slots, part, blk), f32)
    sums = call(
        functools.partial(grad_kernel, side),
        "add_grads",
        out_shape=(summed, summed),
        in_specs=[VMEM] * (side + n_tok),
        out_specs=(VMEM,) * 2,
    )(*g2_parts, *tok_parts[:1], *tok_parts[2:], *tok_parts[1:2])
    ahead = tok_parts[2:3] + i_parts[1:3]
    output, last = call(
        functools.partial(output_kernel, dims),
        "add_outputs",
        out_shape=(result, S((8, LANES), jnp.int32)),
        in_specs=[VMEM] * n_col + [ANY] * len(ahead),
        out_specs=(HBM, VMEM),
        scratch_shapes=[pltpu.VMEM(result.shape, bf16), acc, pltpu.SemaphoreType.DMA],
    )(*o_parts, *ahead)
    grad_in, gw1, gw2 = call(
        functools.partial(input_kernel, dims),
        "add_inputs",
        out_shape=(result, summed, summed),
        in_specs=[ANY] + [VMEM] * len([*sums, *o_parts, *i_parts]),
        out_specs=(HBM,) * 3,
        scratch_shapes=[pltpu.VMEM(result.shape, bf16), acc, pltpu.SemaphoreType.DMA((3,))],
    )(last, *sums, *o_parts, *i_parts)
    return (output, grad_in, gw1.reshape(1, 1, slots, part, blk), gw2.reshape(1, 1, slots, part, blk))


def solution(mesh):
    placed = (
        P("tok", "row"),
        P("row", "col", None, None, None),
        P("row", "col", None),
        P("row", "col", None),
        P("row", "col", None, None, None),
        P("row", "col", None),
        P("row", "col", None),
        P("tok", "row"),
    )
    return jax.shard_map(
        shards,
        mesh=mesh,
        in_specs=placed,
        out_specs=(
            P(("tok", "col"), "row"),
            P(("tok", "col"), "row"),
            P("row", "col", None, "tok", None),
            P("row", "col", None, "tok", None),
        ),
        check_vma=False,
    )
```

```python
import functools
import math

import jax
import jax.numpy as jnp
from jax import lax
from jax.experimental import pallas as pl
from jax.experimental.pallas import tpu as pltpu
from jax.sharding import PartitionSpec as P

FF = 32768
LANES = 128
f32 = jnp.float32
bf16 = jnp.bfloat16
VMEM = pl.BlockSpec(memory_space=pltpu.VMEM)
SMEM = pl.BlockSpec(memory_space=pltpu.SMEM)
ANY = pl.BlockSpec(memory_space=pl.ANY)
HBM = pl.BlockSpec(memory_space=pltpu.HBM)
TAKE_LIMIT = 62 * 1024 * 1024
LIMIT = 32 * 1024 * 1024

W1_ROW, W1_COL, W2_HID, W2_OUT = range(4)


def call(kernel, name, limit=LIMIT, **kwargs):
    return pl.pallas_call(
        kernel,
        name=name,
        compiler_params=pltpu.CompilerParams(vmem_limit_bytes=limit),
        cost_estimate=pl.CostEstimate(flops=1 << 25, bytes_accessed=1 << 19, transcendentals=0),
        **kwargs,
    )


def dot(a, b, contract):
    return lax.dot_general(a, b, ((contract[:1], contract[1:]), ((), ())), preferred_element_type=f32)


def cdf(v):
    return 0.5 * (1.0 + lax.erf(v * math.sqrt(0.5)))


def partner(i, d, n):
    return i ^ d if n & (n - 1) == 0 else (i + d) % n


def target(axis, d):
    n = lax.axis_size(axis)
    me = lax.axis_index(axis)
    return jnp.bitwise_xor(me, d) if n & (n - 1) == 0 else lax.rem(me + d, n)


def send(x, axis, d):
    n = lax.axis_size(axis)
    return lax.ppermute(x, axis, [(i, partner(i, d, n)) for i in range(n)]) if d else x


def cut(value, refs, k, axis):
    share = value.shape[0] // len(refs)
    for d, ref in enumerate(refs):
        begin = pl.multiple_of(target(axis, d) * share, share)
        ref[k * share : (k + 1) * share, :] = value[pl.ds(begin, share), :].astype(ref.dtype)


def table_row(tables, slots):
    lane = lax.broadcasted_iota(jnp.int32, (16, LANES), 1)
    row = jnp.zeros((16, LANES), f32)
    for which, table in enumerate(tables):
        for k in range(slots):
            row = jnp.where(lane == which * slots + k, table[k].astype(f32), row)
    return row.astype(bf16)


def numbers(ref, rows):
    return ref[rows : rows + 16, :].astype(f32)[:8].astype(jnp.int32)


def token_kernel(t0, t1, t2, t3, tokens, w1, message, tokens_v, w_v, sent, c0, c1, c2, c3, sems):
    slots, blk, _ = w_v.shape
    rows = tokens_v.shape[0]
    tables = (c0, c1, c2, c3)
    loads = [pltpu.make_async_copy(t, c, sems.at[i]) for i, (t, c) in enumerate(zip((t0, t1, t2, t3), tables))]
    loads.append(pltpu.make_async_copy(tokens, tokens_v, sems.at[4]))
    loads.append(pltpu.make_async_copy(w1, w_v, sems.at[5]))
    stores = []

    def store(begin, size):
        here = pl.ds(begin, size)
        stores.append(pltpu.make_async_copy(sent.at[here], message.at[here], sems.at[6 + len(stores)]))
        stores[-1].start()

    for c in loads:
        c.start()
    for c in loads[:4]:
        c.wait()
    sent[slots * rows :, :] = table_row(tables, slots)
    store(slots * rows, 16)
    for c in loads[4:]:
        c.wait()
    for k in range(slots):
        here = pl.ds(pl.multiple_of(c0[k] * blk, blk), blk)
        sent[k * rows : (k + 1) * rows, :] = dot(tokens_v[:, here], w_v[k], (1, 0)).astype(bf16)
        store(k * rows, rows)
    for c in stores:
        c.wait()


def first_places(tab):
    return tab[:8]


def places_of(tab, blocks, slots):
    place = lax.broadcasted_iota(jnp.int32, (2 * slots, LANES), 0)
    same = tab[8 : 8 + 2 * slots] == blocks[:1]
    return jnp.min(jnp.where(same, place, 2 * slots), axis=0, keepdims=True)


def start_taking(source, table, taken, sems):
    slots, _, blk = taken.shape
    copies = []
    for k in range(slots):
        begin = pl.multiple_of(table[k] * blk, blk)
        copies.append(pltpu.make_async_copy(source.at[:, pl.ds(begin, blk)], taken.at[k], sems.at[k]))
        copies[-1].start()
    return copies


def cotangent_kernel(
    c0, c1, c2, c3, tokens, grad_out, w1, w2, message, taken_t, cot, hid, back, tab, row, place_of, taken, sems
):
    slots, rows, blk = cot.shape
    copies = start_taking(grad_out, c3, cot, sems.at[0])
    copies_t = start_taking(tokens, c0, taken, sems.at[1])

    @pl.loop(0, place_of.shape[0])
    def _(block):
        place_of[block] = 2 * slots

    lane = lax.broadcasted_iota(jnp.int32, (8, LANES), 1)
    firsts = jnp.zeros((8, LANES), jnp.int32)
    for j in range(2 * slots):
        block = c1[j] if j < slots else c2[j - slots]
        place = jnp.minimum(place_of[block], j)
        place_of[block] = place
        firsts = jnp.where(lane == j, place, firsts)
        tab[8 + j : 9 + j, :] = jnp.full((1, LANES), block, jnp.int32)
    tab[:8] = firsts
    row[...] = table_row((c0, c1, c2, c3), slots)
    hid[...] = jnp.zeros(hid.shape, f32)
    back[...] = jnp.zeros(back.shape, f32)
    for k in range(slots):
        copies[k].wait()
        value = dot(cot[k], w2[k], (1, 1))
        message[k * rows : (k + 1) * rows, :] = value.astype(bf16)
        at = jnp.minimum(place_of[c2[k]], slots)
        back[at] = back[at] + value
    for k in range(slots):
        copies_t[k].wait()
        at = place_of[c1[k]]
        hid[at] = hid[at] + dot(taken[k], w1[k], (1, 0))
        taken_t[k] = taken[k].T


def add_peers(acc, own, numbers_at, peers, slots):
    count, rows, _ = acc.shape
    for j in range(count):
        acc[j] = own[j]
    for numbers_of, ref in zip(numbers_at, peers):
        for k, at in enumerate(numbers_of):

            @pl.when(at < count)
            def _():
                acc[at] = acc[at] + ref[k * rows : (k + 1) * rows, :].astype(f32)


def hidden_kernel(dims, tab, own, *refs):
    slots, n_row, n_col, n_tok = dims
    peers, refs = refs[: n_row - 1], refs[n_row - 1 :]
    cot, active, hid, places, grad, half = refs
    rows = half.shape[0] // slots
    begin = pl.multiple_of((1 - lax.div(lax.axis_index("tok"), max(1, n_tok // 2))) * rows, rows)
    found = [places_of(tab, numbers(ref, slots * cot.shape[1]), slots) for ref in peers]
    places[...] = jnp.zeros(places.shape, jnp.int32)
    for i, place in enumerate(found):
        places[8 * i : 8 * i + 8] = jnp.broadcast_to(place, (8, LANES))
    at = [[place[0, W1_COL * slots + k] for k in range(slots)] for place in found]
    firsts = first_places(tab)
    firsts = [firsts[0, slots + k] for k in range(slots)]
    add_peers(hid, own, at, peers, slots)
    for k in range(slots):
        h = hid[firsts[k]]
        active[k] = (h * cdf(h)).astype(bf16)
        grad[k] = dot(active[k], cot[k], (0, 0))
        if n_tok > 1:
            half[k * rows : (k + 1) * rows, :] = grad[k, pl.ds(begin, rows), :].astype(bf16)


def slope_kernel(dims, tab, row, active, hid, w2, slope, *refs):
    slots, n_row, n_col, n_tok = dims
    outs, value = refs[:n_col], refs[n_col]
    for k in range(slots):
        value[k] = dot(active[k], w2[k], (1, 0))
        cut(value.at[k], outs, k, "col")
    for ref in outs:
        ref[ref.shape[0] - 16 :, :] = row[...]
    firsts = first_places(tab)
    for k in range(slots):
        h = hid[firsts[0, k]]
        slope[k] = cdf(h) + h * jnp.exp(-0.5 * h * h) * (1.0 / math.sqrt(2.0 * math.pi))


def back_kernel(dims, tab, places, own, *refs):
    slots, n_row, n_col, n_tok = dims
    peers, refs = refs[: n_row - 1], refs[n_row - 1 :]
    slope, w1, taken_t = refs[:3]
    refs = refs[3:]
    outs, refs = refs[:n_col], refs[n_col:]
    grads, (acc, value, grad) = refs[:n_tok], refs[n_tok:]
    found = [places[8 * i : 8 * i + 8] for i in range(len(peers))]
    at = [[place[0, W2_HID * slots + k] for k in range(slots)] for place in found]
    firsts = first_places(tab)
    firsts = [firsts[0, k] for k in range(slots)]
    add_peers(acc, own, at, peers, slots)
    for k in range(slots):
        g = (acc[firsts[k]] * slope[k]).astype(bf16)
        grad[k] = dot(taken_t[k], g, (1, 0))
        cut(grad.at[k], grads, k, "tok")
        value[k] = dot(g, w1[k], (1, 1))
        cut(value.at[k], outs, k, "col")
    for ref in grads:
        rows = slots * grad.shape[1] // n_tok
        if ref.shape[0] > rows:
            ref[rows:, :] = jnp.zeros((ref.shape[0] - rows, LANES), bf16)


def join_kernel(dims, grad2, half, *refs):
    slots, n_row, n_col, n_tok = dims
    side = max(1, n_tok // 2)
    part = grad2.shape[1] // n_tok
    shares, joined = refs[:side], refs[-side:]
    for d in range(side):
        to = target("tok", d)
        begin = pl.multiple_of(to * part, part)
        size = shares[d].shape[0]
        joined[d][:size, :] = shares[d][...]
        for k in range(slots):
            total = grad2[k, pl.ds(begin, part), :]
            if n_tok > 1:
                there = pl.multiple_of(k * side * part + lax.rem(to, side) * part, part)
                total = total + half[pl.ds(there, part), :].astype(f32)
            joined[d][size + k * part : size + (k + 1) * part, :] = total.astype(bf16)


def add_shares(parts, result, first):
    part = result.shape[1]
    for k in range(result.shape[0]):
        here = slice((first + k) * part, (first + k + 1) * part)
        result[k] = sum(ref[here, :].astype(f32) for ref in parts)


def place_shares(shares, tables, acc):
    slots = len(tables[0])
    share = acc.shape[1]
    acc[...] = jnp.zeros(acc.shape, f32)
    for ref, table in zip(shares, tables):
        for k in range(slots):
            acc[table[k]] = acc[table[k]] + ref[k * share : (k + 1) * share, :].astype(f32)


def store_rows(acc, result, output, sem):
    blk = acc.shape[-1]
    for b in range(acc.shape[0]):
        result[:, b * blk : (b + 1) * blk] = acc[b].astype(bf16)
    copy = pltpu.make_async_copy(result, output, sem)
    copy.start()
    return copy


def tables_of(parts, rows, which, slots):
    return [[table[0, which * slots + k] for k in range(slots)] for table in [numbers(ref, rows) for ref in parts]]


def output_kernel(dims, *refs):
    slots, n_row, n_col, n_tok = dims
    parts, (output, last, result, acc, sem) = refs[:n_col], refs[n_col:]
    rows = slots * acc.shape[1]
    last[...] = jnp.zeros(last.shape, jnp.int32)
    place_shares(parts, tables_of(parts, rows, W2_OUT, slots), acc)
    store_rows(acc, result, output, sem).wait()


def input_kernel(dims, after, sum1, sum2, *refs):
    del after
    slots, n_row, n_col, n_tok = dims
    outs, backs, refs = refs[:n_col], refs[n_col : 2 * n_col], refs[2 * n_col :]
    grad_in, gw1, gw2, result, acc, sems = refs
    stores = [pltpu.make_async_copy(sum1, gw1, sems.at[0]), pltpu.make_async_copy(sum2, gw2, sems.at[1])]
    for c in stores:
        c.start()
    rows = slots * acc.shape[1]
    place_shares(backs, tables_of(outs, rows, W1_ROW, slots), acc)
    stores.append(store_rows(acc, result, grad_in, sems.at[2]))
    for c in stores:
        c.wait()


def grad_kernel(*refs):
    parts, gw1, gw2 = refs[:-2], refs[-2], refs[-1]
    slots, part, _ = gw1.shape
    add_shares(parts, gw1, 0)
    add_shares([ref for ref in parts if ref.shape[0] == 2 * slots * part], gw2, slots)


def near_last(n):
    return [0] + list(range(2, n)) + [1][: n - 1]


def shards(tokens, w1_blocks, w1_rows, w1_cols, w2_blocks, w2_hidden, w2_outs, grad_out):
    slots, blk = w1_blocks.shape[2], w1_blocks.shape[-1]
    rows = tokens.shape[0]
    n_row, n_col, n_tok = (lax.axis_size(a) for a in ("row", "col", "tok"))
    dims = (slots, n_row, n_col, n_tok)
    row_blocks = tokens.shape[1] // blk
    col_blocks = FF // n_col // blk
    share, part = rows // n_col, blk // n_tok
    w1 = w1_blocks.reshape(slots, blk, blk)
    w2 = w2_blocks.reshape(slots, blk, blk)
    tables = [t.reshape(slots) for t in (w1_rows, w1_cols, w2_hidden, w2_outs)]

    S = jax.ShapeDtypeStruct
    message = S((slots * rows + 16, blk), bf16)
    wide, narrow = S((slots, rows, blk), f32), S((slots, rows, blk), bf16)

    p_send = call(
        token_kernel,
        "take_tokens",
        TAKE_LIMIT,
        out_shape=message,
        in_specs=[HBM] * 6,
        out_specs=HBM,
        scratch_shapes=[
            pltpu.VMEM(tokens.shape, bf16),
            pltpu.VMEM((slots, blk, blk), bf16),
            pltpu.VMEM((slots * rows + 16, blk), bf16),
        ]
        + [pltpu.SMEM((slots,), jnp.int32)] * 4
        + [pltpu.SemaphoreType.DMA((7 + slots,))],
    )(*tables, tokens, w1)
    p_peers = [send(p_send, "row", d) for d in range(1, n_row)]

    b_send, taken_t, cot, hid, back, tab, row = call(
        cotangent_kernel,
        "take_cotangent",
        out_shape=(
            S((slots * rows, blk), bf16),
            S((slots, blk, rows), bf16),
            narrow,
            S((2 * slots, rows, blk), f32),
            S((slots + 1, rows, blk), f32),
            S((8 + 2 * slots, LANES), jnp.int32),
            S((16, LANES), bf16),
        ),
        in_specs=[SMEM] * 4 + [HBM, HBM] + [VMEM] * 2,
        out_specs=(VMEM,) * 7,
        scratch_shapes=[
            pltpu.SMEM((col_blocks,), jnp.int32),
            pltpu.VMEM((slots, rows, blk), bf16),
            pltpu.SemaphoreType.DMA((2, slots)),
        ],
    )(*tables, tokens, grad_out, w1, w2)
    b_peers = [send(b_send, "row", d) for d in range(1, n_row)]

    single = S((slots * part, blk), bf16)
    side = max(1, n_tok // 2)
    spare = [16, 16]
    grads = tuple(single if d < side else S((slots * part + spare[d % 2], blk), bf16) for d in range(n_tok))
    half = S((slots * side * part, blk), bf16)
    peer_rows = 8 * max(1, n_row - 1)
    active, hid, places, grad2, half = call(
        functools.partial(hidden_kernel, dims),
        "hidden",
        out_shape=(
            narrow,
            S((2 * slots, rows, blk), f32),
            S((peer_rows, LANES), jnp.int32),
            S((slots, blk, blk), f32),
            half,
        ),
        in_specs=[VMEM] * (n_row + 2),
        out_specs=(VMEM,) * 5,
    )(tab, hid, *p_peers, cot)
    if n_tok > 1:
        half = lax.ppermute(half, "tok", [(i, (i + side) % n_tok) for i in range(n_tok)])
    out_share, back_share = S((slots * share + 16, blk), bf16), S((slots * share, blk), bf16)
    slope, *o_sent = call(
        functools.partial(slope_kernel, dims),
        "slope",
        out_shape=(wide,) + (out_share,) * n_col,
        in_specs=[VMEM] * 5,
        out_specs=(VMEM,) * (1 + n_col),
        scratch_shapes=[pltpu.VMEM((slots, rows, blk), f32)],
    )(tab, row, active, hid, w2)
    o_parts = [send(o_sent[d], "col", d) for d in near_last(n_col)]

    sent = call(
        functools.partial(back_kernel, dims),
        "back",
        out_shape=(back_share,) * n_col + grads,
        in_specs=[VMEM] * (n_row + 5),
        out_specs=(VMEM,) * (n_col + n_tok),
        scratch_shapes=[
            pltpu.VMEM((slots, rows, blk), f32),
            pltpu.VMEM((slots, rows, blk), f32),
            pltpu.VMEM((slots, blk, blk), f32),
        ],
    )(tab, places, back, *b_peers, slope, w1, taken_t)
    i_sent, g_sent = list(sent[:n_col]), list(sent[n_col:])
    early = o_parts[1:]
    g_sent[:side] = call(
        functools.partial(join_kernel, dims),
        "join_shares",
        out_shape=(S((2 * slots * part, blk), bf16),) * side,
        in_specs=[VMEM] * (2 + side) + [ANY] * len(early),
        out_specs=(VMEM,) * side,
    )(grad2, half, *g_sent[:side], *early)
    i_parts = [send(i_sent[d], "col", d) for d in near_last(n_col)]
    tok_parts = [send(g_sent[d], "tok", d) for d in range(n_tok)]

    result = S((share, row_blocks * blk), bf16)
    summed = S((slots, part, blk), f32)
    acc = pltpu.VMEM((row_blocks, share, blk), f32)
    summed = S((slots, part, blk), f32)
    sums = call(
        grad_kernel,
        "add_grads",
        out_shape=(summed, summed),
        in_specs=[VMEM] * n_tok,
        out_specs=(VMEM,) * 2,
    )(*tok_parts[::-1])
    output, last = call(
        functools.partial(output_kernel, dims),
        "add_outputs",
        out_shape=(result, S((8, LANES), jnp.int32)),
        in_specs=[VMEM] * n_col,
        out_specs=(HBM, VMEM),
        scratch_shapes=[pltpu.VMEM(result.shape, bf16), acc, pltpu.SemaphoreType.DMA],
    )(*o_parts)
    grad_in, gw1, gw2 = call(
        functools.partial(input_kernel, dims),
        "add_inputs",
        out_shape=(result, summed, summed),
        in_specs=[ANY] + [VMEM] * len([*sums, *o_parts, *i_parts]),
        out_specs=(HBM,) * 3,
        scratch_shapes=[pltpu.VMEM(result.shape, bf16), acc, pltpu.SemaphoreType.DMA((3,))],
    )(last, *sums, *o_parts, *i_parts)
    return (output, grad_in, gw1.reshape(1, 1, slots, part, blk), gw2.reshape(1, 1, slots, part, blk))


def solution(mesh):
    placed = (
        P("tok", "row"),
        P("row", "col", None, None, None),
        P("row", "col", None),
        P("row", "col", None),
        P("row", "col", None, None, None),
        P("row", "col", None),
        P("row", "col", None),
        P("tok", "row"),
    )
    return jax.shard_map(
        shards,
        mesh=mesh,
        in_specs=placed,
        out_specs=(
            P(("tok", "col"), "row"),
            P(("tok", "col"), "row"),
            P("row", "col", None, "tok", None),
            P("row", "col", None, "tok", None),
        ),
        check_vma=False,
    )
```

```python
import functools
import math

import jax
import jax.numpy as jnp
from jax import lax
from jax.experimental import pallas as pl
from jax.experimental.pallas import tpu as pltpu
from jax.sharding import PartitionSpec as P

FF = 32768
LANES = 128
f32 = jnp.float32
bf16 = jnp.bfloat16
VMEM = pl.BlockSpec(memory_space=pltpu.VMEM)
SMEM = pl.BlockSpec(memory_space=pltpu.SMEM)
ANY = pl.BlockSpec(memory_space=pl.ANY)
HBM = pl.BlockSpec(memory_space=pltpu.HBM)
TAKE_LIMIT = 62 * 1024 * 1024
LIMIT = 32 * 1024 * 1024

W1_ROW, W1_COL, W2_HID, W2_OUT = range(4)


def call(kernel, name, limit=LIMIT, **kwargs):
    return pl.pallas_call(
        kernel,
        name=name,
        compiler_params=pltpu.CompilerParams(vmem_limit_bytes=limit),
        cost_estimate=pl.CostEstimate(flops=1 << 25, bytes_accessed=1 << 19, transcendentals=0),
        **kwargs,
    )


def dot(a, b, contract):
    return lax.dot_general(a, b, ((contract[:1], contract[1:]), ((), ())), preferred_element_type=f32)


def cdf(v):
    return 0.5 * (1.0 + lax.erf(v * math.sqrt(0.5)))


def partner(i, d, n):
    return i ^ d if n & (n - 1) == 0 else (i + d) % n


def target(axis, d):
    n = lax.axis_size(axis)
    me = lax.axis_index(axis)
    return jnp.bitwise_xor(me, d) if n & (n - 1) == 0 else lax.rem(me + d, n)


def send(x, axis, d):
    n = lax.axis_size(axis)
    return lax.ppermute(x, axis, [(i, partner(i, d, n)) for i in range(n)]) if d else x


def cut(value, refs, k, axis):
    share = value.shape[0] // len(refs)
    for d, ref in enumerate(refs):
        begin = pl.multiple_of(target(axis, d) * share, share)
        ref[k * share : (k + 1) * share, :] = value[pl.ds(begin, share), :].astype(ref.dtype)


def table_row(tables, slots):
    lane = lax.broadcasted_iota(jnp.int32, (16, LANES), 1)
    row = jnp.zeros((16, LANES), f32)
    for which, table in enumerate(tables):
        for k in range(slots):
            row = jnp.where(lane == which * slots + k, table[k].astype(f32), row)
    return row.astype(bf16)


def numbers(ref, rows):
    return ref[rows : rows + 16, :].astype(f32)[:8].astype(jnp.int32)


def token_kernel(t0, t1, t2, t3, tokens, w1, message, tokens_v, w_v, sent, c0, c1, c2, c3, sems):
    slots, blk, _ = w_v.shape
    rows = tokens_v.shape[0]
    tables = (c0, c1, c2, c3)
    loads = [pltpu.make_async_copy(t, c, sems.at[i]) for i, (t, c) in enumerate(zip((t0, t1, t2, t3), tables))]
    loads.append(pltpu.make_async_copy(tokens, tokens_v, sems.at[4]))
    loads.append(pltpu.make_async_copy(w1, w_v, sems.at[5]))
    stores = []

    def store(begin, size):
        here = pl.ds(begin, size)
        stores.append(pltpu.make_async_copy(sent.at[here], message.at[here], sems.at[6 + len(stores)]))
        stores[-1].start()

    for c in loads:
        c.start()
    for c in loads[:4]:
        c.wait()
    sent[slots * rows :, :] = table_row(tables, slots)
    store(slots * rows, 16)
    for c in loads[4:]:
        c.wait()
    for k in range(slots):
        here = pl.ds(pl.multiple_of(c0[k] * blk, blk), blk)
        sent[k * rows : (k + 1) * rows, :] = dot(tokens_v[:, here], w_v[k], (1, 0)).astype(bf16)
        store(k * rows, rows)
    for c in stores:
        c.wait()


def first_places(tab):
    return tab[:8]


def places_of(tab, blocks, slots):
    place = lax.broadcasted_iota(jnp.int32, (2 * slots, LANES), 0)
    same = tab[8 : 8 + 2 * slots] == blocks[:1]
    return jnp.min(jnp.where(same, place, 2 * slots), axis=0, keepdims=True)


def start_taking(source, table, taken, sems):
    slots, _, blk = taken.shape
    copies = []
    for k in range(slots):
        begin = pl.multiple_of(table[k] * blk, blk)
        copies.append(pltpu.make_async_copy(source.at[:, pl.ds(begin, blk)], taken.at[k], sems.at[k]))
        copies[-1].start()
    return copies


def cotangent_kernel(
    c0, c1, c2, c3, tokens, grad_out, w1, w2, message, taken_t, cot, hid, back, tab, row, place_of, taken, sems
):
    slots, rows, blk = cot.shape
    copies = start_taking(grad_out, c3, cot, sems.at[0])
    copies_t = start_taking(tokens, c0, taken, sems.at[1])

    @pl.loop(0, place_of.shape[0])
    def _(block):
        place_of[block] = 2 * slots

    lane = lax.broadcasted_iota(jnp.int32, (8, LANES), 1)
    firsts = jnp.zeros((8, LANES), jnp.int32)
    for j in range(2 * slots):
        block = c1[j] if j < slots else c2[j - slots]
        place = jnp.minimum(place_of[block], j)
        place_of[block] = place
        firsts = jnp.where(lane == j, place, firsts)
        tab[8 + j : 9 + j, :] = jnp.full((1, LANES), block, jnp.int32)
    tab[:8] = firsts
    row[...] = table_row((c0, c1, c2, c3), slots)
    hid[...] = jnp.zeros(hid.shape, f32)
    back[...] = jnp.zeros(back.shape, f32)
    for k in range(slots):
        copies[k].wait()
        value = dot(cot[k], w2[k], (1, 1))
        message[k * rows : (k + 1) * rows, :] = value.astype(bf16)
        at = jnp.minimum(place_of[c2[k]], slots)
        back[at] = back[at] + value
    for k in range(slots):
        copies_t[k].wait()
        at = place_of[c1[k]]
        hid[at] = hid[at] + dot(taken[k], w1[k], (1, 0))
        taken_t[k] = taken[k].T


def add_peers(acc, own, numbers_at, peers, slots):
    count, rows, _ = acc.shape
    for j in range(count):
        acc[j] = own[j]
    for numbers_of, ref in zip(numbers_at, peers):
        for k, at in enumerate(numbers_of):

            @pl.when(at < count)
            def _():
                acc[at] = acc[at] + ref[k * rows : (k + 1) * rows, :].astype(f32)


def hidden_kernel(dims, tab, own, *refs):
    slots, n_row, n_col, n_tok = dims
    peers, refs = refs[: n_row - 1], refs[n_row - 1 :]
    cot, active, hid, places, grad, half = refs
    rows = half.shape[0] // slots
    begin = pl.multiple_of((1 - lax.div(lax.axis_index("tok"), max(1, n_tok // 2))) * rows, rows)
    found = [places_of(tab, numbers(ref, slots * cot.shape[1]), slots) for ref in peers]
    places[...] = jnp.zeros(places.shape, jnp.int32)
    for i, place in enumerate(found):
        places[8 * i : 8 * i + 8] = jnp.broadcast_to(place, (8, LANES))
    at = [[place[0, W1_COL * slots + k] for k in range(slots)] for place in found]
    firsts = first_places(tab)
    firsts = [firsts[0, slots + k] for k in range(slots)]
    add_peers(hid, own, at, peers, slots)
    for k in range(slots):
        h = hid[firsts[k]]
        active[k] = (h * cdf(h)).astype(bf16)
        grad[k] = dot(active[k], cot[k], (0, 0))
        if n_tok > 1:
            half[k * rows : (k + 1) * rows, :] = grad[k, pl.ds(begin, rows), :].astype(bf16)


def slope_kernel(dims, tab, row, active, hid, w2, slope, *refs):
    slots, n_row, n_col, n_tok = dims
    outs, value = refs[:n_col], refs[n_col]
    for k in range(slots):
        value[k] = dot(active[k], w2[k], (1, 0))
        cut(value.at[k], outs, k, "col")
    for ref in outs:
        ref[ref.shape[0] - 16 :, :] = row[...]
    firsts = first_places(tab)
    for k in range(slots):
        h = hid[firsts[0, k]]
        slope[k] = cdf(h) + h * jnp.exp(-0.5 * h * h) * (1.0 / math.sqrt(2.0 * math.pi))


def back_kernel(dims, tab, places, own, *refs):
    slots, n_row, n_col, n_tok = dims
    peers, refs = refs[: n_row - 1], refs[n_row - 1 :]
    slope, w1, taken_t = refs[:3]
    refs = refs[3:]
    outs, refs = refs[:n_col], refs[n_col:]
    grads, (acc, value, grad) = refs[:n_tok], refs[n_tok:]
    found = [places[8 * i : 8 * i + 8] for i in range(len(peers))]
    at = [[place[0, W2_HID * slots + k] for k in range(slots)] for place in found]
    firsts = first_places(tab)
    firsts = [firsts[0, k] for k in range(slots)]
    add_peers(acc, own, at, peers, slots)
    for k in range(slots):
        g = (acc[firsts[k]] * slope[k]).astype(bf16)
        grad[k] = dot(taken_t[k], g, (1, 0))
        cut(grad.at[k], grads, k, "tok")
        value[k] = dot(g, w1[k], (1, 1))
        cut(value.at[k], outs, k, "col")
    for ref in grads:
        rows = slots * grad.shape[1] // n_tok
        if ref.shape[0] > rows:
            ref[rows:, :] = jnp.zeros((ref.shape[0] - rows, LANES), bf16)


def join_kernel(dims, grad2, half, *refs):
    slots, n_row, n_col, n_tok = dims
    side = max(1, n_tok // 2)
    part = grad2.shape[1] // n_tok
    shares, joined = refs[:side], refs[-side:]
    for d in range(side):
        to = target("tok", d)
        begin = pl.multiple_of(to * part, part)
        size = shares[d].shape[0]
        joined[d][:size, :] = shares[d][...]
        for k in range(slots):
            total = grad2[k, pl.ds(begin, part), :]
            if n_tok > 1:
                there = pl.multiple_of(k * side * part + lax.rem(to, side) * part, part)
                total = total + half[pl.ds(there, part), :].astype(f32)
            joined[d][size + k * part : size + (k + 1) * part, :] = total.astype(bf16)


def add_shares(parts, result, first):
    part = result.shape[1]
    for k in range(result.shape[0]):
        here = slice((first + k) * part, (first + k + 1) * part)
        result[k] = sum(ref[here, :].astype(f32) for ref in parts)


def place_shares(shares, tables, acc):
    slots = len(tables[0])
    share = acc.shape[1]
    acc[...] = jnp.zeros(acc.shape, f32)
    for ref, table in zip(shares, tables):
        for k in range(slots):
            acc[table[k]] = acc[table[k]] + ref[k * share : (k + 1) * share, :].astype(f32)


def store_rows(acc, result, output, sem):
    blk = acc.shape[-1]
    for b in range(acc.shape[0]):
        result[:, b * blk : (b + 1) * blk] = acc[b].astype(bf16)
    copy = pltpu.make_async_copy(result, output, sem)
    copy.start()
    return copy


def tables_of(parts, rows, which, slots):
    return [[table[0, which * slots + k] for k in range(slots)] for table in [numbers(ref, rows) for ref in parts]]


def output_kernel(dims, *refs):
    slots, n_row, n_col, n_tok = dims
    parts, (output, last, result, acc, sem) = refs[:n_col], refs[n_col:]
    rows = slots * acc.shape[1]
    last[...] = jnp.zeros(last.shape, jnp.int32)
    place_shares(parts, tables_of(parts, rows, W2_OUT, slots), acc)
    store_rows(acc, result, output, sem).wait()


def input_kernel(dims, after, sum1, sum2, *refs):
    del after
    slots, n_row, n_col, n_tok = dims
    outs, backs, refs = refs[:n_col], refs[n_col : 2 * n_col], refs[2 * n_col :]
    grad_in, gw1, gw2, result, acc, sems = refs
    stores = [pltpu.make_async_copy(sum1, gw1, sems.at[0]), pltpu.make_async_copy(sum2, gw2, sems.at[1])]
    for c in stores:
        c.start()
    rows = slots * acc.shape[1]
    place_shares(backs, tables_of(outs, rows, W1_ROW, slots), acc)
    stores.append(store_rows(acc, result, grad_in, sems.at[2]))
    for c in stores:
        c.wait()


def grad_kernel(*refs):
    parts, gw1, gw2 = refs[:-2], refs[-2], refs[-1]
    slots, part, _ = gw1.shape
    add_shares(parts, gw1, 0)
    add_shares([ref for ref in parts if ref.shape[0] == 2 * slots * part], gw2, slots)


def near_last(n):
    return [0] + list(range(n - 1, 1, -1)) + [1][: n - 1]


def shards(tokens, w1_blocks, w1_rows, w1_cols, w2_blocks, w2_hidden, w2_outs, grad_out):
    slots, blk = w1_blocks.shape[2], w1_blocks.shape[-1]
    rows = tokens.shape[0]
    n_row, n_col, n_tok = (lax.axis_size(a) for a in ("row", "col", "tok"))
    dims = (slots, n_row, n_col, n_tok)
    row_blocks = tokens.shape[1] // blk
    col_blocks = FF // n_col // blk
    share, part = rows // n_col, blk // n_tok
    w1 = w1_blocks.reshape(slots, blk, blk)
    w2 = w2_blocks.reshape(slots, blk, blk)
    tables = [t.reshape(slots) for t in (w1_rows, w1_cols, w2_hidden, w2_outs)]

    S = jax.ShapeDtypeStruct
    message = S((slots * rows + 16, blk), bf16)
    wide, narrow = S((slots, rows, blk), f32), S((slots, rows, blk), bf16)

    p_send = call(
        token_kernel,
        "take_tokens",
        TAKE_LIMIT,
        out_shape=message,
        in_specs=[HBM] * 6,
        out_specs=HBM,
        scratch_shapes=[
            pltpu.VMEM(tokens.shape, bf16),
            pltpu.VMEM((slots, blk, blk), bf16),
            pltpu.VMEM((slots * rows + 16, blk), bf16),
        ]
        + [pltpu.SMEM((slots,), jnp.int32)] * 4
        + [pltpu.SemaphoreType.DMA((7 + slots,))],
    )(*tables, tokens, w1)
    p_peers = [send(p_send, "row", d) for d in range(1, n_row)]

    b_send, taken_t, cot, hid, back, tab, row = call(
        cotangent_kernel,
        "take_cotangent",
        out_shape=(
            S((slots * rows, blk), bf16),
            S((slots, blk, rows), bf16),
            narrow,
            S((2 * slots, rows, blk), f32),
            S((slots + 1, rows, blk), f32),
            S((8 + 2 * slots, LANES), jnp.int32),
            S((16, LANES), bf16),
        ),
        in_specs=[SMEM] * 4 + [HBM, HBM] + [VMEM] * 2,
        out_specs=(VMEM,) * 7,
        scratch_shapes=[
            pltpu.SMEM((col_blocks,), jnp.int32),
            pltpu.VMEM((slots, rows, blk), bf16),
            pltpu.SemaphoreType.DMA((2, slots)),
        ],
    )(*tables, tokens, grad_out, w1, w2)
    b_peers = [send(b_send, "row", d) for d in range(1, n_row)]

    single = S((slots * part, blk), bf16)
    side = max(1, n_tok // 2)
    spare = [16, 16]
    grads = tuple(single if d < side else S((slots * part + spare[d % 2], blk), bf16) for d in range(n_tok))
    half = S((slots * side * part, blk), bf16)
    peer_rows = 8 * max(1, n_row - 1)
    active, hid, places, grad2, half = call(
        functools.partial(hidden_kernel, dims),
        "hidden",
        out_shape=(
            narrow,
            S((2 * slots, rows, blk), f32),
            S((peer_rows, LANES), jnp.int32),
            S((slots, blk, blk), f32),
            half,
        ),
        in_specs=[VMEM] * (n_row + 2),
        out_specs=(VMEM,) * 5,
    )(tab, hid, *p_peers, cot)
    if n_tok > 1:
        half = lax.ppermute(half, "tok", [(i, (i + side) % n_tok) for i in range(n_tok)])
    out_share, back_share = S((slots * share + 16, blk), bf16), S((slots * share, blk), bf16)
    slope, *o_sent = call(
        functools.partial(slope_kernel, dims),
        "slope",
        out_shape=(wide,) + (out_share,) * n_col,
        in_specs=[VMEM] * 5,
        out_specs=(VMEM,) * (1 + n_col),
        scratch_shapes=[pltpu.VMEM((slots, rows, blk), f32)],
    )(tab, row, active, hid, w2)
    o_parts = [send(o_sent[d], "col", d) for d in near_last(n_col)]

    sent = call(
        functools.partial(back_kernel, dims),
        "back",
        out_shape=(back_share,) * n_col + grads,
        in_specs=[VMEM] * (n_row + 5),
        out_specs=(VMEM,) * (n_col + n_tok),
        scratch_shapes=[
            pltpu.VMEM((slots, rows, blk), f32),
            pltpu.VMEM((slots, rows, blk), f32),
            pltpu.VMEM((slots, blk, blk), f32),
        ],
    )(tab, places, back, *b_peers, slope, w1, taken_t)
    i_sent, g_sent = list(sent[:n_col]), list(sent[n_col:])
    early = o_parts[1:]
    g_sent[:side] = call(
        functools.partial(join_kernel, dims),
        "join_shares",
        out_shape=(S((2 * slots * part, blk), bf16),) * side,
        in_specs=[VMEM] * (2 + side) + [ANY] * len(early),
        out_specs=(VMEM,) * side,
    )(grad2, half, *g_sent[:side], *early)
    i_parts = [send(i_sent[d], "col", d) for d in near_last(n_col)]
    tok_parts = [send(g_sent[d], "tok", d) for d in range(n_tok)]

    result = S((share, row_blocks * blk), bf16)
    summed = S((slots, part, blk), f32)
    acc = pltpu.VMEM((row_blocks, share, blk), f32)
    summed = S((slots, part, blk), f32)
    sums = call(
        grad_kernel,
        "add_grads",
        out_shape=(summed, summed),
        in_specs=[VMEM] * n_tok,
        out_specs=(VMEM,) * 2,
    )(*tok_parts[:1], *tok_parts[2:], *tok_parts[1:2])
    output, last = call(
        functools.partial(output_kernel, dims),
        "add_outputs",
        out_shape=(result, S((8, LANES), jnp.int32)),
        in_specs=[VMEM] * n_col,
        out_specs=(HBM, VMEM),
        scratch_shapes=[pltpu.VMEM(result.shape, bf16), acc, pltpu.SemaphoreType.DMA],
    )(*o_parts)
    grad_in, gw1, gw2 = call(
        functools.partial(input_kernel, dims),
        "add_inputs",
        out_shape=(result, summed, summed),
        in_specs=[ANY] + [VMEM] * len([*sums, *o_parts, *i_parts]),
        out_specs=(HBM,) * 3,
        scratch_shapes=[pltpu.VMEM(result.shape, bf16), acc, pltpu.SemaphoreType.DMA((3,))],
    )(last, *sums, *o_parts, *i_parts)
    return (output, grad_in, gw1.reshape(1, 1, slots, part, blk), gw2.reshape(1, 1, slots, part, blk))


def solution(mesh):
    placed = (
        P("tok", "row"),
        P("row", "col", None, None, None),
        P("row", "col", None),
        P("row", "col", None),
        P("row", "col", None, None, None),
        P("row", "col", None),
        P("row", "col", None),
        P("tok", "row"),
    )
    return jax.shard_map(
        shards,
        mesh=mesh,
        in_specs=placed,
        out_specs=(
            P(("tok", "col"), "row"),
            P(("tok", "col"), "row"),
            P("row", "col", None, "tok", None),
            P("row", "col", None, "tok", None),
        ),
        check_vma=False,
    )
```

```python
import functools
import math

import jax
import jax.numpy as jnp
from jax import lax
from jax.experimental import pallas as pl
from jax.experimental.pallas import tpu as pltpu
from jax.sharding import PartitionSpec as P

FF = 32768
LANES = 128
f32 = jnp.float32
bf16 = jnp.bfloat16
VMEM = pl.BlockSpec(memory_space=pltpu.VMEM)
SMEM = pl.BlockSpec(memory_space=pltpu.SMEM)
ANY = pl.BlockSpec(memory_space=pl.ANY)
HBM = pl.BlockSpec(memory_space=pltpu.HBM)
TAKE_LIMIT = 62 * 1024 * 1024
LIMIT = 32 * 1024 * 1024

W1_ROW, W1_COL, W2_HID, W2_OUT = range(4)


def call(kernel, name, limit=LIMIT, **kwargs):
    return pl.pallas_call(
        kernel,
        name=name,
        compiler_params=pltpu.CompilerParams(vmem_limit_bytes=limit),
        cost_estimate=pl.CostEstimate(flops=1 << 25, bytes_accessed=1 << 19, transcendentals=0),
        **kwargs,
    )


def dot(a, b, contract):
    return lax.dot_general(a, b, ((contract[:1], contract[1:]), ((), ())), preferred_element_type=f32)


def cdf(v):
    return 0.5 * (1.0 + lax.erf(v * math.sqrt(0.5)))


def partner(i, d, n):
    return i ^ d if n & (n - 1) == 0 else (i + d) % n


def target(axis, d):
    n = lax.axis_size(axis)
    me = lax.axis_index(axis)
    return jnp.bitwise_xor(me, d) if n & (n - 1) == 0 else lax.rem(me + d, n)


def send(x, axis, d):
    n = lax.axis_size(axis)
    return lax.ppermute(x, axis, [(i, partner(i, d, n)) for i in range(n)]) if d else x


def cut(value, refs, k, axis):
    share = value.shape[0] // len(refs)
    for d, ref in enumerate(refs):
        begin = pl.multiple_of(target(axis, d) * share, share)
        ref[k * share : (k + 1) * share, :] = value[pl.ds(begin, share), :].astype(ref.dtype)


def table_row(tables, slots):
    lane = lax.broadcasted_iota(jnp.int32, (16, LANES), 1)
    row = jnp.zeros((16, LANES), f32)
    for which, table in enumerate(tables):
        for k in range(slots):
            row = jnp.where(lane == which * slots + k, table[k].astype(f32), row)
    return row.astype(bf16)


def numbers(ref, rows):
    return ref[rows : rows + 16, :].astype(f32)[:8].astype(jnp.int32)


def token_kernel(t0, t1, t2, t3, tokens, w1, message, tokens_v, w_v, sent, c0, c1, c2, c3, sems):
    slots, blk, _ = w_v.shape
    rows = tokens_v.shape[0]
    tables = (c0, c1, c2, c3)
    loads = [pltpu.make_async_copy(t, c, sems.at[i]) for i, (t, c) in enumerate(zip((t0, t1, t2, t3), tables))]
    loads.append(pltpu.make_async_copy(tokens, tokens_v, sems.at[4]))
    loads.append(pltpu.make_async_copy(w1, w_v, sems.at[5]))
    stores = []

    def store(begin, size):
        here = pl.ds(begin, size)
        stores.append(pltpu.make_async_copy(sent.at[here], message.at[here], sems.at[6 + len(stores)]))
        stores[-1].start()

    for c in loads:
        c.start()
    for c in loads[:4]:
        c.wait()
    sent[slots * rows :, :] = table_row(tables, slots)
    store(slots * rows, 16)
    for c in loads[4:]:
        c.wait()
    for k in range(slots):
        here = pl.ds(pl.multiple_of(c0[k] * blk, blk), blk)
        sent[k * rows : (k + 1) * rows, :] = dot(tokens_v[:, here], w_v[k], (1, 0)).astype(bf16)
        store(k * rows, rows)
    for c in stores:
        c.wait()


def first_places(tab):
    return tab[:8]


def places_of(tab, blocks, slots):
    place = lax.broadcasted_iota(jnp.int32, (2 * slots, LANES), 0)
    same = tab[8 : 8 + 2 * slots] == blocks[:1]
    return jnp.min(jnp.where(same, place, 2 * slots), axis=0, keepdims=True)


def start_taking(source, table, taken, sems):
    slots, _, blk = taken.shape
    copies = []
    for k in range(slots):
        begin = pl.multiple_of(table[k] * blk, blk)
        copies.append(pltpu.make_async_copy(source.at[:, pl.ds(begin, blk)], taken.at[k], sems.at[k]))
        copies[-1].start()
    return copies


def cotangent_kernel(
    c0, c1, c2, c3, tokens, grad_out, w1, w2, message, taken_t, cot, hid, back, tab, row, place_of, taken, sems
):
    slots, rows, blk = cot.shape
    copies = start_taking(grad_out, c3, cot, sems.at[0])
    copies_t = start_taking(tokens, c0, taken, sems.at[1])

    @pl.loop(0, place_of.shape[0])
    def _(block):
        place_of[block] = 2 * slots

    lane = lax.broadcasted_iota(jnp.int32, (8, LANES), 1)
    firsts = jnp.zeros((8, LANES), jnp.int32)
    for j in range(2 * slots):
        block = c1[j] if j < slots else c2[j - slots]
        place = jnp.minimum(place_of[block], j)
        place_of[block] = place
        firsts = jnp.where(lane == j, place, firsts)
        tab[8 + j : 9 + j, :] = jnp.full((1, LANES), block, jnp.int32)
    tab[:8] = firsts
    row[...] = table_row((c0, c1, c2, c3), slots)
    hid[...] = jnp.zeros(hid.shape, f32)
    back[...] = jnp.zeros(back.shape, f32)
    for k in range(slots):
        copies[k].wait()
        value = dot(cot[k], w2[k], (1, 1))
        message[k * rows : (k + 1) * rows, :] = value.astype(bf16)
        at = jnp.minimum(place_of[c2[k]], slots)
        back[at] = back[at] + value
    for k in range(slots):
        copies_t[k].wait()
        at = place_of[c1[k]]
        hid[at] = hid[at] + dot(taken[k], w1[k], (1, 0))
        taken_t[k] = taken[k].T


def add_peers(acc, own, numbers_at, peers, slots):
    count, rows, _ = acc.shape
    for j in range(count):
        acc[j] = own[j]
    for numbers_of, ref in zip(numbers_at, peers):
        for k, at in enumerate(numbers_of):

            @pl.when(at < count)
            def _():
                acc[at] = acc[at] + ref[k * rows : (k + 1) * rows, :].astype(f32)


def hidden_kernel(dims, tab, own, *refs):
    slots, n_row, n_col, n_tok = dims
    peers, refs = refs[: n_row - 1], refs[n_row - 1 :]
    cot, active, hid, places, grad, half = refs
    rows = half.shape[0] // slots
    begin = pl.multiple_of((1 - lax.div(lax.axis_index("tok"), max(1, n_tok // 2))) * rows, rows)
    found = [places_of(tab, numbers(ref, slots * cot.shape[1]), slots) for ref in peers]
    places[...] = jnp.zeros(places.shape, jnp.int32)
    for i, place in enumerate(found):
        places[8 * i : 8 * i + 8] = jnp.broadcast_to(place, (8, LANES))
    at = [[place[0, W1_COL * slots + k] for k in range(slots)] for place in found]
    firsts = first_places(tab)
    firsts = [firsts[0, slots + k] for k in range(slots)]
    add_peers(hid, own, at, peers, slots)
    for k in range(slots):
        h = hid[firsts[k]]
        active[k] = (h * cdf(h)).astype(bf16)
        grad[k] = dot(active[k], cot[k], (0, 0))
        if n_tok > 1:
            half[k * rows : (k + 1) * rows, :] = grad[k, pl.ds(begin, rows), :].astype(bf16)


def slope_kernel(dims, tab, row, active, hid, w2, slope, *refs):
    slots, n_row, n_col, n_tok = dims
    outs, value = refs[:n_col], refs[n_col]
    for k in range(slots):
        value[k] = dot(active[k], w2[k], (1, 0))
        cut(value.at[k], outs, k, "col")
    for ref in outs:
        ref[ref.shape[0] - 16 :, :] = row[...]
    firsts = first_places(tab)
    for k in range(slots):
        h = hid[firsts[0, k]]
        slope[k] = cdf(h) + h * jnp.exp(-0.5 * h * h) * (1.0 / math.sqrt(2.0 * math.pi))


def back_kernel(dims, tab, places, own, *refs):
    slots, n_row, n_col, n_tok = dims
    peers, refs = refs[: n_row - 1], refs[n_row - 1 :]
    slope, w1, taken_t = refs[:3]
    refs = refs[3:]
    outs, refs = refs[:n_col], refs[n_col:]
    grads, (acc, value, grad) = refs[:n_tok], refs[n_tok:]
    found = [places[8 * i : 8 * i + 8] for i in range(len(peers))]
    at = [[place[0, W2_HID * slots + k] for k in range(slots)] for place in found]
    firsts = first_places(tab)
    firsts = [firsts[0, k] for k in range(slots)]
    add_peers(acc, own, at, peers, slots)
    for k in range(slots):
        g = (acc[firsts[k]] * slope[k]).astype(bf16)
        grad[k] = dot(taken_t[k], g, (1, 0))
        cut(grad.at[k], grads, k, "tok")
        value[k] = dot(g, w1[k], (1, 1))
        cut(value.at[k], outs, k, "col")
    for ref in grads:
        rows = slots * grad.shape[1] // n_tok
        if ref.shape[0] > rows:
            ref[rows:, :] = jnp.zeros((ref.shape[0] - rows, LANES), bf16)


def join_kernel(dims, grad2, half, *refs):
    slots, n_row, n_col, n_tok = dims
    side = max(1, n_tok // 2)
    part = grad2.shape[1] // n_tok
    shares, joined = refs[:side], refs[-side:]
    for d in range(side):
        to = target("tok", d)
        begin = pl.multiple_of(to * part, part)
        size = shares[d].shape[0]
        joined[d][:size, :] = shares[d][...]
        for k in range(slots):
            total = grad2[k, pl.ds(begin, part), :]
            if n_tok > 1:
                there = pl.multiple_of(k * side * part + lax.rem(to, side) * part, part)
                total = total + half[pl.ds(there, part), :].astype(f32)
            joined[d][size + k * part : size + (k + 1) * part, :] = total.astype(bf16)


def add_shares(parts, result, first):
    part = result.shape[1]
    for k in range(result.shape[0]):
        here = slice((first + k) * part, (first + k + 1) * part)
        result[k] = sum(ref[here, :].astype(f32) for ref in parts)


def place_shares(shares, tables, acc):
    slots = len(tables[0])
    share = acc.shape[1]
    acc[...] = jnp.zeros(acc.shape, f32)
    for ref, table in zip(shares, tables):
        for k in range(slots):
            acc[table[k]] = acc[table[k]] + ref[k * share : (k + 1) * share, :].astype(f32)


def store_rows(acc, result, output, sem):
    blk = acc.shape[-1]
    for b in range(acc.shape[0]):
        result[:, b * blk : (b + 1) * blk] = acc[b].astype(bf16)
    copy = pltpu.make_async_copy(result, output, sem)
    copy.start()
    return copy


def tables_of(parts, rows, which, slots):
    return [[table[0, which * slots + k] for k in range(slots)] for table in [numbers(ref, rows) for ref in parts]]


def output_kernel(dims, *refs):
    slots, n_row, n_col, n_tok = dims
    parts, (output, last, result, acc, sem) = refs[:n_col], refs[n_col:]
    rows = slots * acc.shape[1]
    last[...] = jnp.zeros(last.shape, jnp.int32)
    place_shares(parts, tables_of(parts, rows, W2_OUT, slots), acc)
    store_rows(acc, result, output, sem).wait()


def input_kernel(dims, after, sum1, sum2, *refs):
    del after
    slots, n_row, n_col, n_tok = dims
    outs, backs, refs = refs[:n_col], refs[n_col : 2 * n_col], refs[2 * n_col :]
    grad_in, gw1, gw2, result, acc, sems = refs
    stores = [pltpu.make_async_copy(sum1, gw1, sems.at[0]), pltpu.make_async_copy(sum2, gw2, sems.at[1])]
    for c in stores:
        c.start()
    rows = slots * acc.shape[1]
    place_shares(backs, tables_of(outs, rows, W1_ROW, slots), acc)
    stores.append(store_rows(acc, result, grad_in, sems.at[2]))
    for c in stores:
        c.wait()


def grad_kernel(*refs):
    parts, gw1, gw2 = refs[:-2], refs[-2], refs[-1]
    slots, part, _ = gw1.shape
    add_shares(parts, gw1, 0)
    add_shares([ref for ref in parts if ref.shape[0] == 2 * slots * part], gw2, slots)


def near_last(n):
    return [0] + list(range(2, n)) + [1][: n - 1]


def shards(tokens, w1_blocks, w1_rows, w1_cols, w2_blocks, w2_hidden, w2_outs, grad_out):
    slots, blk = w1_blocks.shape[2], w1_blocks.shape[-1]
    rows = tokens.shape[0]
    n_row, n_col, n_tok = (lax.axis_size(a) for a in ("row", "col", "tok"))
    dims = (slots, n_row, n_col, n_tok)
    row_blocks = tokens.shape[1] // blk
    col_blocks = FF // n_col // blk
    share, part = rows // n_col, blk // n_tok
    w1 = w1_blocks.reshape(slots, blk, blk)
    w2 = w2_blocks.reshape(slots, blk, blk)
    tables = [t.reshape(slots) for t in (w1_rows, w1_cols, w2_hidden, w2_outs)]

    S = jax.ShapeDtypeStruct
    message = S((slots * rows + 16, blk), bf16)
    wide, narrow = S((slots, rows, blk), f32), S((slots, rows, blk), bf16)

    p_send = call(
        token_kernel,
        "take_tokens",
        TAKE_LIMIT,
        out_shape=message,
        in_specs=[HBM] * 6,
        out_specs=HBM,
        scratch_shapes=[
            pltpu.VMEM(tokens.shape, bf16),
            pltpu.VMEM((slots, blk, blk), bf16),
            pltpu.VMEM((slots * rows + 16, blk), bf16),
        ]
        + [pltpu.SMEM((slots,), jnp.int32)] * 4
        + [pltpu.SemaphoreType.DMA((7 + slots,))],
    )(*tables, tokens, w1)
    p_peers = [send(p_send, "row", d) for d in range(1, n_row)]

    b_send, taken_t, cot, hid, back, tab, row = call(
        cotangent_kernel,
        "take_cotangent",
        out_shape=(
            S((slots * rows, blk), bf16),
            S((slots, blk, rows), bf16),
            narrow,
            S((2 * slots, rows, blk), f32),
            S((slots + 1, rows, blk), f32),
            S((8 + 2 * slots, LANES), jnp.int32),
            S((16, LANES), bf16),
        ),
        in_specs=[SMEM] * 4 + [HBM, HBM] + [VMEM] * 2,
        out_specs=(VMEM,) * 7,
        scratch_shapes=[
            pltpu.SMEM((col_blocks,), jnp.int32),
            pltpu.VMEM((slots, rows, blk), bf16),
            pltpu.SemaphoreType.DMA((2, slots)),
        ],
    )(*tables, tokens, grad_out, w1, w2)
    b_peers = [send(b_send, "row", d) for d in range(1, n_row)]

    single = S((slots * part, blk), bf16)
    side = max(1, n_tok // 2)
    spare = [16, 16]
    grads = tuple(single if d < side else S((slots * part + spare[d % 2], blk), bf16) for d in range(n_tok))
    half = S((slots * side * part, blk), bf16)
    peer_rows = 8 * max(1, n_row - 1)
    active, hid, places, grad2, half = call(
        functools.partial(hidden_kernel, dims),
        "hidden",
        out_shape=(
            narrow,
            S((2 * slots, rows, blk), f32),
            S((peer_rows, LANES), jnp.int32),
            S((slots, blk, blk), f32),
            half,
        ),
        in_specs=[VMEM] * (n_row + 2),
        out_specs=(VMEM,) * 5,
    )(tab, hid, *p_peers, cot)
    if n_tok > 1:
        half = lax.ppermute(half, "tok", [(i, (i + side) % n_tok) for i in range(n_tok)])
    out_share, back_share = S((slots * share + 16, blk), bf16), S((slots * share, blk), bf16)
    slope, *o_sent = call(
        functools.partial(slope_kernel, dims),
        "slope",
        out_shape=(wide,) + (out_share,) * n_col,
        in_specs=[VMEM] * 5,
        out_specs=(VMEM,) * (1 + n_col),
        scratch_shapes=[pltpu.VMEM((slots, rows, blk), f32)],
    )(tab, row, active, hid, w2)
    o_parts = [send(o_sent[d], "col", d) for d in [0] + near_last(n_col)[-2:0:-1] + [1][: n_col - 1]]

    sent = call(
        functools.partial(back_kernel, dims),
        "back",
        out_shape=(back_share,) * n_col + grads,
        in_specs=[VMEM] * (n_row + 5),
        out_specs=(VMEM,) * (n_col + n_tok),
        scratch_shapes=[
            pltpu.VMEM((slots, rows, blk), f32),
            pltpu.VMEM((slots, rows, blk), f32),
            pltpu.VMEM((slots, blk, blk), f32),
        ],
    )(tab, places, back, *b_peers, slope, w1, taken_t)
    i_sent, g_sent = list(sent[:n_col]), list(sent[n_col:])
    early = o_parts[1:]
    g_sent[:side] = call(
        functools.partial(join_kernel, dims),
        "join_shares",
        out_shape=(S((2 * slots * part, blk), bf16),) * side,
        in_specs=[VMEM] * (2 + side) + [ANY] * len(early),
        out_specs=(VMEM,) * side,
    )(grad2, half, *g_sent[:side], *early)
    i_parts = [send(i_sent[d], "col", d) for d in near_last(n_col)]
    tok_parts = [send(g_sent[d], "tok", d) for d in range(n_tok)]

    result = S((share, row_blocks * blk), bf16)
    summed = S((slots, part, blk), f32)
    acc = pltpu.VMEM((row_blocks, share, blk), f32)
    summed = S((slots, part, blk), f32)
    sums = call(
        grad_kernel,
        "add_grads",
        out_shape=(summed, summed),
        in_specs=[VMEM] * n_tok,
        out_specs=(VMEM,) * 2,
    )(*tok_parts[:1], *tok_parts[2:], *tok_parts[1:2])
    output, last = call(
        functools.partial(output_kernel, dims),
        "add_outputs",
        out_shape=(result, S((8, LANES), jnp.int32)),
        in_specs=[VMEM] * n_col,
        out_specs=(HBM, VMEM),
        scratch_shapes=[pltpu.VMEM(result.shape, bf16), acc, pltpu.SemaphoreType.DMA],
    )(*o_parts)
    grad_in, gw1, gw2 = call(
        functools.partial(input_kernel, dims),
        "add_inputs",
        out_shape=(result, summed, summed),
        in_specs=[ANY] + [VMEM] * len([*sums, *o_parts, *i_parts]),
        out_specs=(HBM,) * 3,
        scratch_shapes=[pltpu.VMEM(result.shape, bf16), acc, pltpu.SemaphoreType.DMA((3,))],
    )(last, *sums, o_parts[0], *o_parts[-2:0:-1], *o_parts[1:][-1:], *i_parts)
    return (output, grad_in, gw1.reshape(1, 1, slots, part, blk), gw2.reshape(1, 1, slots, part, blk))


def solution(mesh):
    placed = (
        P("tok", "row"),
        P("row", "col", None, None, None),
        P("row", "col", None),
        P("row", "col", None),
        P("row", "col", None, None, None),
        P("row", "col", None),
        P("row", "col", None),
        P("tok", "row"),
    )
    return jax.shard_map(
        shards,
        mesh=mesh,
        in_specs=placed,
        out_specs=(
            P(("tok", "col"), "row"),
            P(("tok", "col"), "row"),
            P("row", "col", None, "tok", None),
            P("row", "col", None, "tok", None),
        ),
        check_vma=False,
    )
```
